32 devices in a mesh: batch: 8 (over y, x, core), head: 4 (over z).
Axes of the slice: x: 2, y: 2, z: 4, core: 2. Of those that a mesh axis runs over, the one named last changes fastest.
Arguments:
- tokens: bfloat16 [24576, 768], P(('batch', 'head')), may hold values from -6 to 6
- query_weight: bfloat16 [768, 768], P(None, 'head'), may hold values from -0.21875 to 0.21875
- key_weight: bfloat16 [768, 768], P(None, 'head'), may hold values from -0.21875 to 0.21875
- value_weight: bfloat16 [768, 768], P(None, 'head'), may hold values from -0.21875 to 0.21875
- query_bias: float32 [768], P('head'), may hold values from -3 to 3
- value_bias: float32 [768], P('head'), may hold values from -3 to 3
- mixer_weight: bfloat16 [768, 768], replicated, may hold values from -1.25 to 1.25
- mixer_bias: float32 [768], replicated, may hold values from -2 to 2
- first_gain: float32 [768], replicated, may hold values from 0.5 to 1.5
- first_shift: float32 [768], replicated, may hold values from -2 to 2
- expand_weight: bfloat16 [768, 3072], replicated, may hold values from -0.21875 to 0.21875
- expand_bias: float32 [3072], replicated, may hold values from -3 to 3
- reduce_weight: bfloat16 [3072, 768], replicated, may hold values from -0.109375 to 0.109375
- reduce_bias: float32 [768], replicated, may hold values from -2 to 2
- second_gain: float32 [768], replicated, may hold values from 0.5 to 1.5
- second_shift: float32 [768], replicated, may hold values from -2 to 2
- cotangent: bfloat16 [24576, 768], P(('batch', 'head')), may hold values from -6 to 6
- group_kinds: int32 [8], P('batch'), may hold values from 0 to 1
- pair_orders: int32 [24, 12, 2], P('batch', 'head'), may hold values from 0 to 1, each once within a row
- triple_orders: int32 [16, 12, 3], P('batch', 'head'), may hold values from 0 to 2, each once within a row
Outputs:
- layer_output: bfloat16 [24576, 768], P(('batch', 'head'))
- tokens_grad: bfloat16 [24576, 768], P(('batch', 'head'))
- query_weight_grad: float32 [768, 768], P(None, 'head')
- key_weight_grad: float32 [768, 768], P(None, 'head')
- value_weight_grad: float32 [768, 768], P(None, 'head')
- query_bias_grad: float32 [768], P('head')
- value_bias_grad: float32 [768], P('head')
- mixer_weight_grad: float32 [768, 768], P('head')
- mixer_bias_grad: float32 [768], replicated
- first_gain_grad: float32 [768], replicated
- first_shift_grad: float32 [768], replicated
- expand_weight_grad: float32 [768, 3072], P(None, 'head')
- expand_bias_grad: float32 [3072], replicated
- reduce_weight_grad: float32 [3072, 768], P('head')
- reduce_bias_grad: float32 [768], replicated
- second_gain_grad: float32 [768], replicated
- second_shift_grad: float32 [768], replicated
The draws below stay inside these ranges and needn't reach their ends.
Inputs may be any that keep to these rules, and one draw needn't show every extreme that they name: `group_kinds`: 0: the group's six blocks are three sequences of two blocks; 1: two sequences of three blocks. Each pair_orders[s, h, :] is a permutation. Each triple_orders[s, h, :] is a permutation.
All inputs are finite; a program needn't handle non-finite values.
Results may differ from the reference program's by a relative error of at most 0.018.
Values may be sent and summed in bfloat16 or wider, within the bound.
A program may use at most 192 MiB of HBM per device.

```python
import math
import jax
import jax.numpy as jnp
from jax import lax

D = 768
HEADS = 12
HEAD_SIZE = 64
FF = 3072
BLOCK = 512
GROUPS = 1
TOK_DEV = 3072
TOKENS = 24576
KIND_ROWS = 8
PAIR_SEQS = 24
TRIPLE_SEQS = 16
N_BATCH = 8


def plant(result, rng, smallest, largest):
    spot = [jax.random.randint(jax.random.fold_in(rng, axis), (), 0, length) for axis, length in enumerate(result.shape)]
    widest = result.shape.index(max(result.shape))
    beside = spot[:widest] + [(spot[widest] + 1) % result.shape[widest]] + spot[widest + 1:]
    return result.at[tuple(spot)].set(smallest).at[tuple(beside)].set(largest)


def block_scale(rng, shape, cuts, least, top_value):
    loudness = 1.0
    for axis_at, parts in cuts:
        heights = jax.random.uniform(jax.random.fold_in(jax.random.fold_in(rng, 6), axis_at), (parts,), jnp.float32, least / len(cuts), top_value / len(cuts))
        loudness = loudness * jnp.repeat(jnp.exp(heights), shape[axis_at] // parts).reshape((-1,) + (1,) * (len(shape) - 1 - axis_at))
    return loudness


def gaussian(key, dims, width, limit, split=(), kind=jnp.bfloat16):
    array = jax.random.normal(key, dims, jnp.float32) * width
    if len(split) > 0:
        array = block_scale(key, dims, split, -0.22, 0.18) * array
    return jnp.clip(array, min=-limit, max=limit).astype(kind)


def setup_inputs(seed: int = 0) -> dict:
    splits = jax.random.split(jax.random.key(seed), 21)
    return {
        "tokens": gaussian(splits[0], (TOKENS, D), 1.0, 6.0, ((0, 32),)),
        "query_weight": gaussian(splits[1], (D, D), D ** -0.5, 0.21875, ((1, 4),)),
        "key_weight": gaussian(splits[2], (D, D), D ** -0.5, 0.21875, ((1, 4),)),
        "value_weight": gaussian(splits[3], (D, D), D ** -0.5, 0.21875, ((1, 4),)),
        "query_bias": gaussian(splits[4], (D,), 0.5, 3.0, ((0, 4),), jnp.float32),
        "value_bias": gaussian(splits[5], (D,), 0.5, 3.0, ((0, 4),), jnp.float32),
        "mixer_weight": gaussian(splits[6], (D, D), (D // 32) ** -0.5, 1.25),
        "mixer_bias": gaussian(splits[7], (D,), 0.3, 2.0, (), jnp.float32),
        "first_gain": jnp.clip(1.0 + 0.1 * jax.random.normal(splits[8], (D,), jnp.float32), 0.5, 1.5),
        "first_shift": gaussian(splits[9], (D,), 0.3, 2.0, (), jnp.float32),
        "expand_weight": gaussian(splits[10], (D, FF), D ** -0.5, 0.21875),
        "expand_bias": gaussian(splits[11], (FF,), 0.5, 3.0, (), jnp.float32),
        "reduce_weight": gaussian(splits[12], (FF, D), FF ** -0.5, 0.109375),
        "reduce_bias": gaussian(splits[13], (D,), 0.3, 2.0, (), jnp.float32),
        "second_gain": jnp.clip(1.0 + 0.1 * jax.random.normal(splits[14], (D,), jnp.float32), 0.5, 1.5),
        "second_shift": gaussian(splits[15], (D,), 0.3, 2.0, (), jnp.float32),
        "cotangent": gaussian(splits[16], (TOKENS, D), 1.0, 6.0, ((0, 32),)),
        "group_kinds": plant(jax.random.randint(splits[17], (KIND_ROWS,), 0, 2), jax.random.fold_in(splits[17], 1), 0, 1).astype(jnp.int32),
        "pair_orders": jax.vmap(lambda own: jax.random.permutation(own, 2))(jax.random.split(splits[18], PAIR_SEQS * HEADS)).reshape((PAIR_SEQS, HEADS, 2)).astype(jnp.int32),
        "triple_orders": jax.vmap(lambda own: jax.random.permutation(own, 3))(jax.random.split(splits[19], TRIPLE_SEQS * HEADS)).reshape((TRIPLE_SEQS, HEADS, 3)).astype(jnp.int32),
    }


EPSILON = 1e-05
HIGH = lax.Precision.HIGHEST

@jax.custom_vjp
def low(v):
    return lax.optimization_barrier(v.astype(jnp.bfloat16)).astype(jnp.float32)

@jax.custom_vjp
def low_back(v):
    return v

def low_keep(v):
    return (low(v), None)

def low_pass(kept, grad):
    return (grad,)

def back_keep(v):
    return (v, None)

def back_low(kept, grad):
    return (low(grad),)
low.defvjp(low_keep, low_pass)
low_back.defvjp(back_keep, back_low)

def dense(matrix_a, matrix_b):
    return jnp.dot(matrix_a, matrix_b, precision=HIGH)

def layer_norm(values, gain_vec, shift_vec):
    center = values - lax.optimization_barrier(jnp.mean(values, axis=-1, keepdims=True))
    spread = lax.optimization_barrier(jnp.mean(center * center, axis=-1, keepdims=True))
    return center * lax.rsqrt(spread + EPSILON) * gain_vec + shift_vec

def key_blocks(group_kinds, pair_orders, triple_orders):
    block_count = group_kinds.shape[0] * 6
    block_ids = jnp.arange(block_count, dtype=jnp.int32)
    group_ids = block_ids // 6
    position = block_ids % 6
    first_block = group_ids * 6
    pair_pick = pair_orders[group_ids * 3 + position // 2, :, position % 2].astype(jnp.int32)
    triple_pick = triple_orders[group_ids * 2 + position // 3, :, position % 3].astype(jnp.int32)
    pair_key = (first_block + 2 * (position // 2))[:, None] + pair_pick
    triple_key = (first_block + 3 * (position // 3))[:, None] + triple_pick
    use_pairs = (group_kinds[group_ids] == 0)[:, None]
    return jnp.where(use_pairs, pair_key, triple_key).astype(jnp.int32)

def attend(queries, keys, values, chosen):
    block_shape = (chosen.shape[0], BLOCK, HEADS, HEAD_SIZE)
    score_scale = 1.0 / math.sqrt(HEAD_SIZE)
    head_ids = jnp.arange(HEADS, dtype=jnp.int32)[None, :]
    query_quad = queries.reshape(block_shape)
    key_sel = keys.reshape(block_shape)[chosen, :, head_ids, :]
    value_sel = values.reshape(block_shape)[chosen, :, head_ids, :]

    def one_block(operands):
        query_blk, key_blk, value_blk = operands
        scores = jnp.einsum('qhe,hke->hqk', query_blk, key_blk, precision=HIGH)
        scores = low_back(scores * score_scale)
        row_max = lax.optimization_barrier(jnp.max(scores, axis=-1, keepdims=True))
        raised = jnp.exp(scores - row_max)
        probs = raised / lax.optimization_barrier(jnp.sum(raised, axis=-1, keepdims=True))
        return jnp.einsum('hqk,hke->qhe', low(probs), value_blk, precision=HIGH)
    attended = lax.map(jax.checkpoint(one_block), (query_quad, key_sel, value_sel))
    return attended.reshape(queries.shape)

def forward(token_rows, weight_set, chosen):
    query_weight, key_weight, value_weight, query_bias, value_bias, mixer_weight, mixer_bias, first_gain, first_shift, expand_weight, expand_bias, reduce_weight, reduce_bias, second_gain, second_shift = weight_set
    queries = low(low_back(dense(token_rows, query_weight) + query_bias))
    keys = low(low_back(dense(token_rows, key_weight)))
    values = low(low_back(dense(token_rows, value_weight) + value_bias))
    attended = low(low_back(attend(queries, keys, values, chosen)))
    mixed = low_back(dense(attended, mixer_weight) + mixer_bias) + token_rows
    normed = layer_norm(mixed, first_gain, first_shift)
    hidden = low_back(dense(low(normed), expand_weight) + expand_bias)
    active = low(jax.nn.gelu(hidden, approximate=False))
    branch = low_back(dense(active, reduce_weight) + reduce_bias)
    return layer_norm(branch + normed, second_gain, second_shift)

def widen(operand):
    return operand.astype(jnp.float32)

def reference(tokens, query_weight, key_weight, value_weight, query_bias, value_bias, mixer_weight, mixer_bias, first_gain, first_shift, expand_weight, expand_bias, reduce_weight, reduce_bias, second_gain, second_shift, cotangent, group_kinds, pair_orders, triple_orders):
    weight_set = jax.tree.map(widen, (query_weight, key_weight, value_weight, query_bias, value_bias, mixer_weight, mixer_bias, first_gain, first_shift, expand_weight, expand_bias, reduce_weight, reduce_bias, second_gain, second_shift))
    shard_tokens = tokens.astype(jnp.float32).reshape(N_BATCH, TOK_DEV, D)
    shard_cots = cotangent.astype(jnp.float32).reshape(N_BATCH, TOK_DEV, D)
    shard_kinds = group_kinds.reshape(N_BATCH, GROUPS)
    shard_pairs = pair_orders.reshape(N_BATCH, 3 * GROUPS, HEADS, 2)
    shard_triples = triple_orders.reshape(N_BATCH, 2 * GROUPS, HEADS, 3)

    def shard_step(totals, inputs):
        token_rows, cot_rows, kind_row, pair_rows, triple_rows = inputs
        chosen = key_blocks(kind_row, pair_rows, triple_rows)

        def shard_forward(rows_in, weights_in):
            return forward(rows_in, weights_in, chosen)
        output_rows, pullback = jax.vjp(shard_forward, token_rows, weight_set)
        token_grad, weight_grads = pullback(cot_rows)
        totals = jax.tree.map(jnp.add, totals, weight_grads)
        return (totals, (output_rows.astype(jnp.bfloat16), token_grad.astype(jnp.bfloat16)))
    start_totals = jax.tree.map(jnp.zeros_like, weight_set)
    totals, stacked = lax.scan(shard_step, start_totals, (shard_tokens, shard_cots, shard_kinds, shard_pairs, shard_triples))
    layer_output = stacked[0].reshape(TOKENS, D)
    tokens_grad = stacked[1].reshape(TOKENS, D)
    return (layer_output, tokens_grad, totals[0], totals[1], totals[2], totals[3], totals[4], totals[5], totals[6], totals[7], totals[8], totals[9], totals[10], totals[11], totals[12], totals[13], totals[14])
```

```python
import functools
import math

import jax
import jax.numpy as jnp
from jax import lax
from jax.experimental import pallas as pl
from jax.experimental.pallas import tpu as pltpu
from jax.sharding import PartitionSpec as P

MESH = pl.DeviceIdType.MESH
BF = jnp.bfloat16
F32 = jnp.float32
VMEM_LIMIT = 60 * 2**20

D = 768
HEAD_SIZE = 64
BLOCK = 512
ROWS = 768
TILE = 256
WINDOW = 2048
SLOT = 192
FF = 3072
EPSILON = 1e-05
SCALE = 1.0 / math.sqrt(HEAD_SIZE)
EXP2_SCALE = SCALE * math.log2(math.e)
CHUNKS = 6


def dot_nn(a, b):
    return lax.dot_general(a, b, (((1,), (0,)), ((), ())), preferred_element_type=F32)


def dot_nt(a, b):
    return lax.dot_general(a, b, (((1,), (1,)), ((), ())), preferred_element_type=F32)


def dot_tn(a, b):
    return lax.dot_general(a, b, (((0,), (0,)), ((), ())), preferred_element_type=F32)


def remote(src, dst, send, recv, b, h):
    return pltpu.make_async_remote_copy(
        src_ref=src, dst_ref=dst, send_sem=send, recv_sem=recv, device_id=(b, h), device_id_type=MESH
    )


def flip(b, step):
    return b + step - 2 * step * ((b // step) % 2)


def own_offset(h):
    return pl.multiple_of(768 * h - 1024 * (h // 2), 256)


def start_kernel(
    tok, wq, wk, wv, qb, vb, pairs, triples,
    xw, wt, qbs, vbs, pairs_all, triples_all,
    tok_v, w_v, loc, send, recv,
):
    b = lax.axis_index("batch")
    h = lax.axis_index("head")
    core = b % 2
    pc, px, py = flip(b, 1), flip(b, 2), flip(b, 4)
    hp = flip(h, 1)
    hm = 3 - h
    middle = jnp.logical_or(h == 1, h == 2)
    others = [(h + d) % 4 for d in (1, 2, 3)]
    barrier = pltpu.get_barrier_semaphore()
    for target in [(pc, h), (px, h), (py, h)] + [(b, o) for o in others]:
        pl.semaphore_signal(barrier, inc=1, device_id=target, device_id_type=MESH)

    own = own_offset(h)
    small = ((qb, qbs), (vb, vbs), (pairs, pairs_all), (triples, triples_all))
    weights = (wq, wk, wv)
    fetch = [(tok, tok_v)] + [(src, w_v.at[m]) for m, src in enumerate(weights)]
    fetch = [pltpu.make_async_copy(src, dst, loc.at[i]) for i, (src, dst) in enumerate(fetch)]
    kept = [(tok_v, xw.at[pl.ds(own, ROWS)])]
    kept += [(w_v.at[m], wt.at[h, m]) for m in range(3)]
    kept += [(src, dst.at[h]) for src, dst in small]
    kept = [pltpu.make_async_copy(src, dst, loc.at[4 + i]) for i, (src, dst) in enumerate(kept)]
    fill = pltpu.make_async_copy(
        tok_v.at[pl.ds(0, BLOCK)],
        xw.at[pl.ds(pl.multiple_of(1536 - 512 * h, 256), BLOCK)],
        loc.at[12],
    )
    for c in fetch + kept[4:]:
        c.start()
    pl.semaphore_wait(barrier, 6)

    def piece(who):
        return pl.ds(pl.multiple_of(((who // 2) % 4) * 48, 16), 48)

    lanes = pl.ds(pl.multiple_of(core * 384, 128), 384)
    sem = iter(range(128))

    def make(src, dst, who, where):
        i = next(sem)
        c = remote(src, dst, send.at[i], recv.at[i], who, where)
        return c

    mine = piece(b)
    near = (1, 3, 2)
    over_z = {}
    for d in near:
        for m, src in enumerate(weights):
            c = make(src.at[mine, lanes], wt.at[h, m, mine, lanes], b, others[d - 1])
            c.start()
            over_z[d, m] = c
    tables = []
    for src, dst in small:
        for d in near:
            c = make(src, dst.at[h], b, others[d - 1])
            c.start()
            tables.append(c)
    pair = make(tok, xw.at[pl.ds(own, ROWS)], b, hp)
    cross = make(
        tok.at[pl.ds(pl.multiple_of(256 * (h % 2), 256), BLOCK)],
        xw.at[pl.ds(pl.multiple_of(1536 * ((h + 1) % 2), 256), BLOCK)],
        b,
        hm,
    )

    for i, c in enumerate(fetch):
        c.wait()
        kept[i].start()

    @pl.when(jnp.logical_not(middle))
    def _():
        fill.start()

    def forward(d, m, rows, who):
        slot = (h + 4 - d) % 4
        ref = wt.at[slot, m, rows, lanes]
        c = make(ref, ref, who, h)
        c.start()
        return c

    units = [(d, m) for d in near for m in range(3)]
    first = {}
    for i, (d, m) in enumerate(units):
        over_z[d, m].wait()
        first[d, m] = forward(d, m, mine, px if i % 2 == 0 else py)
        if i == 5:
            pair.start()

            @pl.when(middle)
            def _():
                cross.start()

    second = {}
    for i, (d, m) in enumerate(units):
        first[d, m].wait()
        came, go = (px, py) if i % 2 == 0 else (py, px)
        second[d, m] = [forward(d, m, mine, go), forward(d, m, piece(came), go)]
    third = {}
    for d, m in units:
        for c in second[d, m]:
            c.wait()
        third[d, m] = forward(d, m, slice(None), pc)
    for c in third.values():
        c.wait()
    for c in tables:
        c.wait()
    pair.wait()
    for c in kept:
        c.wait()

    @pl.when(middle)
    def _():
        cross.wait()

    @pl.when(jnp.logical_not(middle))
    def _():
        fill.wait()


def start_exchange(*args):
    hb = pl.BlockSpec(memory_space=pl.ANY)
    qb, pairs, triples = args[4], args[6], args[7]
    return pl.pallas_call(
        start_kernel,
        out_shape=(
            jax.ShapeDtypeStruct((WINDOW, D), BF),
            jax.ShapeDtypeStruct((4, 3, SLOT, D), BF),
            jax.ShapeDtypeStruct((4,) + qb.shape, F32),
            jax.ShapeDtypeStruct((4,) + qb.shape, F32),
            jax.ShapeDtypeStruct((4,) + pairs.shape, jnp.int32),
            jax.ShapeDtypeStruct((4,) + triples.shape, jnp.int32),
        ),
        in_specs=[hb] * 8,
        out_specs=(hb,) * 6,
        scratch_shapes=[
            pltpu.VMEM((ROWS, D), BF),
            pltpu.VMEM((3, SLOT, D), BF),
            pltpu.SemaphoreType.DMA((13,)),
            pltpu.SemaphoreType.DMA((60,)),
            pltpu.SemaphoreType.DMA((60,)),
        ],
        compiler_params=pltpu.CompilerParams(
            collective_id=0, has_side_effects=True, vmem_limit_bytes=VMEM_LIMIT
        ),
        name="start_exchange",
    )(*args)


def key_index(kinds, pairs, triples, h, tile, head):
    block = (3 * h + tile) // 2
    slot, local = head // 3, head % 3
    pair_pick = 2 * (block // 2) + pairs[slot, block // 2, block % 2, local]
    triple_pick = 3 * (block // 3) + triples[slot, local, block // 3, block % 3]
    chosen = jnp.where(kinds[0] == 0, pair_pick, triple_pick)
    return pl.multiple_of((chosen - 2 * (h // 2)) * BLOCK, BLOCK)


def left_lanes(rows):
    return lax.broadcasted_iota(jnp.int32, (rows, 128), 1) < 64


def attend_kernel(
    kinds, pairs, triples, qbs, vbs, xw, wt,
    p_out, att_out, inv_out, q_out, ks_out, vs_out, mask_out,
    x_v, w_v, q_v, k_v, v_v, sems,
):
    g, t = pl.program_id(0), pl.program_id(1)
    h = lax.axis_index("head")

    @pl.when(jnp.logical_and(g == 0, t == 0))
    def _():
        loads = [pltpu.make_async_copy(wt, w_v, sems.at[0])]
        for c in range(4):
            part = pl.ds(512 * c, 512)
            loads.append(pltpu.make_async_copy(xw.at[part], x_v.at[part], sems.at[1 + c]))
        for c in loads:
            c.start()
        q_bias = jnp.concatenate([qbs[s] for s in range(4)], axis=1)
        v_bias = jnp.concatenate([vbs[s] for s in range(4)], axis=1)
        for c in loads:
            c.wait()
        w_q = w_v[:, 0].reshape(D, D)
        w_k = w_v[:, 1].reshape(D, D)
        w_v2 = w_v[:, 2].reshape(D, D)

        @pl.loop(0, 4)
        def _(c):
            at = pl.ds(pl.multiple_of(c * 512, 512), 512)
            x = x_v[at, :]
            k = dot_nt(x, w_k).astype(BF)
            v = (dot_nt(x, w_v2) + v_bias).astype(BF)
            for s in range(3):
                k_v[s, at, :] = k[:, 256 * s : 256 * s + 256]
                v_v[s, at, :] = v[:, 256 * s : 256 * s + 256]

        own = own_offset(h)

        @pl.loop(0, 3)
        def _(c):
            x = x_v[pl.ds(pl.multiple_of(own + c * TILE, TILE), TILE), :]
            q = (dot_nt(x, w_q) + q_bias).astype(BF)
            for s in range(3):
                q_v[s, pl.ds(pl.multiple_of(c * TILE, TILE), TILE), :] = q[:, 256 * s : 256 * s + 256]

    left = left_lanes(TILE)
    left_keys = left_lanes(BLOCK)
    lane_head = lax.broadcasted_iota(jnp.int32, (8, 256), 1) // 64
    key_block = lax.broadcasted_iota(jnp.int32, (8, 256), 0)
    mask_rows = jnp.zeros((8, 256), F32)
    for pair in range(2):
        at = slice(128 * pair, 128 * pair + 128)
        q = q_v[g, pl.ds(pl.multiple_of(t * TILE, TILE), TILE), at]
        q_out[:, at] = q
        found, picked = [], []
        for side in range(2):
            mask = left if side == 0 else jnp.logical_not(left)
            mask_keys = left_keys if side == 0 else jnp.logical_not(left_keys)
            row = key_index(kinds, pairs, triples, h, t, 4 * g + 2 * pair + side)
            keys = k_v[g, pl.ds(row, BLOCK), at]
            values = v_v[g, pl.ds(row, BLOCK), at]
            picked.append((keys, values))
            here = jnp.logical_and(lane_head == 2 * pair + side, key_block == row // BLOCK)
            mask_rows = jnp.where(here, 1.0, mask_rows)
            scores = dot_nt(jnp.where(mask, q, jnp.zeros_like(q)), keys)
            top = jnp.max(scores, axis=-1, keepdims=True)
            raised = jnp.exp2((scores - top) * EXP2_SCALE).astype(BF)
            p_out[0, 2 * pair + side] = raised
            found.append(dot_nn(raised, jnp.where(mask_keys, values, jnp.ones_like(values))))
        result = jnp.where(left, found[0], found[1])
        total = jnp.where(left, found[1], found[0])
        inverse = 1.0 / pltpu.roll(total, 64, 1)
        att_out[:, at] = (result * inverse).astype(BF)
        inv_out[:, at] = inverse
        ks_out[0, :, at] = jnp.where(left_keys, picked[0][0], picked[1][0])
        vs_out[0, :, at] = jnp.where(left_keys, picked[0][1], picked[1][1])
    mask_out[0] = mask_rows


def attend(kinds, pairs, triples, qbs, vbs, xw, wt):
    hb = pl.BlockSpec(memory_space=pl.ANY)
    sm = pl.BlockSpec(memory_space=pltpu.SMEM)
    vm = pl.BlockSpec(memory_space=pltpu.VMEM)
    tile = pl.BlockSpec((TILE, 256), lambda g, t: (t, g))
    picked = pl.BlockSpec((1, BLOCK, 256), lambda g, t: (3 * g + t, 0, 0))
    return pl.pallas_call(
        attend_kernel,
        grid=(3, 3),
        out_shape=(
            jax.ShapeDtypeStruct((9, 4, TILE, BLOCK), BF),
            jax.ShapeDtypeStruct((ROWS, D), BF),
            jax.ShapeDtypeStruct((ROWS, D), F32),
            jax.ShapeDtypeStruct((ROWS, D), BF),
            jax.ShapeDtypeStruct((9, BLOCK, 256), BF),
            jax.ShapeDtypeStruct((9, BLOCK, 256), BF),
            jax.ShapeDtypeStruct((3, 8, D), F32),
        ),
        in_specs=[sm, sm, sm, vm, vm, hb, hb],
        out_specs=(
            pl.BlockSpec((1, 4, TILE, BLOCK), lambda g, t: (3 * g + t, 0, 0, 0)),
            tile,
            tile,
            tile,
            picked,
            picked,
            pl.BlockSpec((1, 8, 256), lambda g, t: (t, 0, g)),
        ),
        scratch_shapes=[
            pltpu.VMEM((WINDOW, D), BF),
            pltpu.VMEM((4, 3, SLOT, D), BF),
            pltpu.VMEM((3, ROWS, 256), BF),
            pltpu.VMEM((3, WINDOW, 256), BF),
            pltpu.VMEM((3, WINDOW, 256), BF),
            pltpu.SemaphoreType.DMA((8,)),
        ],
        compiler_params=pltpu.CompilerParams(
            dimension_semantics=("arbitrary", "arbitrary"), vmem_limit_bytes=VMEM_LIMIT
        ),
        name="attend",
    )(kinds, pairs, triples, qbs, vbs, xw, wt)


def normal_parts(v):
    bell = jnp.exp2(v * v * (-0.5 * math.log2(math.e)))
    t = 1.0 / (1.0 + (0.3275911 / math.sqrt(2.0)) * jnp.abs(v))
    poly = 0.5 * 1.061405429
    poly = poly * t + 0.5 * -1.453152027
    poly = poly * t + 0.5 * 1.421413741
    poly = poly * t + 0.5 * -0.284496736
    poly = poly * t + 0.5 * 0.254829592
    tail = poly * t * bell
    phi_sum = jnp.where(v >= 0, 1.0 - tail, tail)
    return phi_sum, bell * (1.0 / math.sqrt(2.0 * math.pi))


def norm_parts(values):
    center = values - jnp.mean(values, axis=-1, keepdims=True)
    inverse = lax.rsqrt(jnp.mean(center * center, axis=-1, keepdims=True) + EPSILON)
    return center * inverse, inverse


def norm_back(inner, scaled, inverse):
    inner_mean = jnp.mean(inner, axis=-1, keepdims=True)
    cross_mean = jnp.mean(inner * scaled, axis=-1, keepdims=True)
    return inverse * (inner - inner_mean - scaled * cross_mean)


def column_sum(values):
    return jnp.sum(values, axis=0, keepdims=True)


def dense_kernel(
    att_h, tok_h, cot_h, mw_h, ew_h, rw_h, inv_h, mb, g1, s1, rb, g2, s2, eb,
    out_o, mixed_o, delta_o, low, rdel, mdel, act_h, hdel_h, sums_o,
    att, tok, cot, mw, ew, rw, inv, act, slope, hdel, sems,
):
    loads = [
        pltpu.make_async_copy(src, dst, sems.at[i])
        for i, (src, dst) in enumerate(
            ((att_h, att), (mw_h, mw), (tok_h, tok), (ew_h, ew), (rw_h, rw), (cot_h, cot), (inv_h, inv))
        )
    ]
    for c in loads:
        c.start()
    sums_o[...] = jnp.zeros_like(sums_o)
    for c in loads:
        c.wait()

    @pl.loop(0, 3)
    def _(t):
        at = pl.ds(pl.multiple_of(t * TILE, TILE), TILE)
        mixed = dot_nn(att[at, :], mw[...]) + mb[...] + tok[at, :].astype(F32)
        scaled_one, inverse_one = norm_parts(mixed)
        normed = scaled_one * g1[...] + s1[...]
        normed_low = normed.astype(BF)
        low[at, :] = normed_low
        branch = rb[...] + normed
        for j in range(4):
            cols = slice(768 * j, 768 * j + 768)
            hidden = dot_nn(normed_low, ew[:, cols]) + eb[:, cols]
            phi_sum, bell = normal_parts(hidden)
            active = (hidden * phi_sum).astype(BF)
            act[j, at, :] = active
            slope[:, cols] = (phi_sum + hidden * bell).astype(BF)
            branch += dot_nn(active, rw[cols, :])
        scaled_two, inverse_two = norm_parts(branch)
        out_o[at, :] = (scaled_two * g2[...] + s2[...]).astype(BF)
        upstream = cot[at, :].astype(F32)
        sums_o[4:5, :] += column_sum(upstream * scaled_two)
        sums_o[5:6, :] += column_sum(upstream)
        branch_delta = norm_back(upstream * g2[...], scaled_two, inverse_two)
        reduce_delta = branch_delta.astype(BF)
        rdel[at, :] = reduce_delta
        sums_o[3:4, :] += column_sum(reduce_delta.astype(F32))
        normed_delta = branch_delta
        for j in range(4):
            cols = slice(768 * j, 768 * j + 768)
            back = dot_nt(reduce_delta, rw[cols, :]) * slope[:, cols].astype(F32)
            back_low = back.astype(BF)
            hdel[j, at, :] = back_low
            sums_o[6 + j : 7 + j, :] += column_sum(back_low.astype(F32))
            normed_delta += dot_nt(back_low, ew[:, cols])
        sums_o[1:2, :] += column_sum(normed_delta * scaled_one)
        sums_o[2:3, :] += column_sum(normed_delta)
        mixed_delta = norm_back(normed_delta * g1[...], scaled_one, inverse_one)
        mixed_o[at, :] = mixed_delta
        mixer_delta = mixed_delta.astype(BF)
        mdel[at, :] = mixer_delta
        sums_o[0:1, :] += column_sum(mixer_delta.astype(F32))
        delta_o[at, :] = (dot_nt(mixer_delta, mw[...]) * inv[at, :]).astype(BF)
        pltpu.make_async_copy(act.at[:, at], act_h.at[:, at], sems.at[7 + t]).start()
        pltpu.make_async_copy(hdel.at[:, at], hdel_h.at[:, at], sems.at[10 + t]).start()

    for t in range(3):
        at = pl.ds(t * TILE, TILE)
        pltpu.make_async_copy(act.at[:, at], act_h.at[:, at], sems.at[7 + t]).wait()
        pltpu.make_async_copy(hdel.at[:, at], hdel_h.at[:, at], sems.at[10 + t]).wait()


def dense(*args):
    hb = pl.BlockSpec(memory_space=pl.ANY)
    vm = pl.BlockSpec(memory_space=pltpu.VMEM)
    rows = jax.ShapeDtypeStruct((ROWS, D), BF)
    wide = jax.ShapeDtypeStruct((4, ROWS, D), BF)
    return pl.pallas_call(
        dense_kernel,
        out_shape=(
            rows,
            jax.ShapeDtypeStruct((ROWS, D), F32),
            rows,
            rows,
            rows,
            rows,
            wide,
            wide,
            jax.ShapeDtypeStruct((16, D), F32),
        ),
        in_specs=[hb] * 7 + [vm] * 7,
        out_specs=(vm,) * 6 + (hb, hb, vm),
        scratch_shapes=[
            pltpu.VMEM((ROWS, D), BF),
            pltpu.VMEM((ROWS, D), BF),
            pltpu.VMEM((ROWS, D), BF),
            pltpu.VMEM((D, D), BF),
            pltpu.VMEM((D, FF), BF),
            pltpu.VMEM((FF, D), BF),
            pltpu.VMEM((ROWS, D), F32),
            pltpu.VMEM((4, ROWS, D), BF),
            pltpu.VMEM((TILE, FF), BF),
            pltpu.VMEM((4, ROWS, D), BF),
            pltpu.SemaphoreType.DMA((13,)),
        ],
        compiler_params=pltpu.CompilerParams(vmem_limit_bytes=VMEM_LIMIT),
        name="dense",
    )(*args)


def finish_kernel(
    nb, act_h, hdel_h, low_h, rdel_h, att_h, mdel_h, p_h, ks_h, vs_h, q_h, delta_h, xw_h, wt_h, mixed_h, masks, sums_in,
    res_h, tg_o, sums_o, from_more,
    stage, from_core, from_a, from_b, from_z, res, dx_pair, dx_mid, vec, vec_in,
    wide_a, wide_b, four, dv_low, own, p_v, ks_v, vs_v, q_v, d_v, a_v, dx_v, mid_v, own_v, loc, flow, send, recv,
):
    b = lax.axis_index("batch")
    h = lax.axis_index("head")
    core, xb, yb = b % 2, (b // 2) % 2, (b // 4) % 2
    pc, px, py = flip(b, 1), flip(b, 2), flip(b, 4)
    hp, hm, hq = flip(h, 1), 3 - h, flip(h, 2)
    middle = jnp.logical_or(h == 1, h == 2)
    others = [(h + d) % 4 for d in (1, 2, 3)]
    more = []
    step = 8
    while step < nb:
        more.append(flip(b, step))
        step *= 2
    barrier = pltpu.get_barrier_semaphore()
    targets = [(pc, h), (px, h), (py, h)] + [(m, h) for m in more] + [(b, o) for o in others]
    for target in targets:
        pl.semaphore_signal(barrier, inc=1, device_id=target, device_id_type=MESH)

    def local(i, src, dst):
        return pltpu.make_async_copy(src, dst, loc.at[i])

    loads = [
        local(0, act_h, wide_a),
        local(1, rdel_h, four.at[1]),
        local(2, low_h, four.at[0]),
        local(3, hdel_h, wide_b),
        local(4, att_h, four.at[2]),
        local(5, mdel_h, four.at[3]),
        local(6, mixed_h, own),
    ]
    for c in loads[:2]:
        c.start()

    def make(i, src, dst, who, where):
        return remote(src, dst, send.at[i], recv.at[i], who, where)

    bits = ((xb, px, yb, py), (yb, py, xb, px))
    columns = (pl.ds(0, 384), pl.ds(384, 384))

    def rows_of(start, count):
        return pl.ds(pl.multiple_of(start, 16), count)

    def place_start(part, level):
        start = core * 192
        if level < 2:
            start = start + bits[part][0] * 96
        if level < 1:
            start = start + bits[part][2] * 48
        return start

    def place(part, level):
        return rows_of(place_start(part, level), (48, 96, 192)[level])

    def core_copy(k):
        return make(k, stage.at[k % 4, :, rows_of((1 - core) * 192, 192)], from_core.at[k], pc, h)

    def a_copy(k, part):
        a_bit, who = bits[part][:2]
        src = stage.at[k % 4, :, rows_of(core * 192 + (1 - a_bit) * 96, 96), columns[part]]
        return make(6 + 2 * k + part, src, from_a.at[k, :, :, columns[part]], who, h)

    def b_copy(k, part):
        a_bit, _, b_bit, who = bits[part]
        src = stage.at[k % 4, :, rows_of(core * 192 + a_bit * 96 + (1 - b_bit) * 48, 48), columns[part]]
        return make(18 + 2 * k + part, src, from_b.at[k, :, :, columns[part]], who, h)

    def z_copy(k, part, d):
        o = others[d - 1]
        src = stage.at[k % 4, o, place(part, 0), columns[part]]
        return make(30 + 6 * k + 3 * part + d - 1, src, from_z.at[k, d - 1, :, columns[part]], b, o)

    def gather_copy(k, part, level):
        ref = res.at[k, place(part, level), columns[part]]
        return make(66 + 12 * level + 2 * k + part, ref, ref, bits[part][3 if level == 0 else 1], h)

    def last_copy(k):
        ref = res.at[k, rows_of(core * 192, 192)]
        return make(90 + k, ref, ref, pc, h)

    def more_copy(k, part, i):
        src = stage.at[k % 4, :, place(part, 0), columns[part]]
        dst = from_more.at[k, i, :, :, columns[part]]
        return make(106 + len(more) * (2 * k + part + 1) + i, src, dst, more[i], h)

    def out_copy(k):
        return local(8 + k, res.at[k], res_h.at[k])

    def add(k, part, level, other):
        start, count = place_start(part, level), (48, 96, 192)[level]
        cols = slice(0, D) if level == 2 else slice(384 * part, 384 * part + 384)

        @pl.loop(0, count // 48 * 4)
        def _(i):
            z, block = i % 4, i // 4
            mine = rows_of(start + 48 * block, 48)
            theirs = rows_of(48 * block, 48)
            total = stage[k % 4, z, mine, cols].astype(F32) + other[z, theirs, cols].astype(F32)
            stage[k % 4, z, mine, cols] = total.astype(BF)

    def stage_core(k):
        core_copy(k).wait()
        add(k, 0, 2, from_core.at[k])
        for part in range(2):
            a_copy(k, part).start()

    def stage_a(k):
        for part in range(2):
            a_copy(k, part).wait()
            add(k, part, 1, from_a.at[k])
            b_copy(k, part).start()

    def stage_b(k):
        for part in range(2):
            b_copy(k, part).wait()
            add(k, part, 0, from_b.at[k])
            for i in range(len(more)):
                more_copy(k, part, i).start()
                more_copy(k, part, i).wait()
                get = local(8 + k, from_more.at[k, i], from_b.at[k])
                get.start()
                get.wait()
                add(k, part, 0, from_b.at[k])
            for d in (2, 1, 3):
                z_copy(k, part, d).start()

    def stage_z(k):
        for part in range(2):
            cols = slice(384 * part, 384 * part + 384)
            total = stage[k % 4, h, place(part, 0), cols].astype(F32)
            for d in (1, 2, 3):
                z_copy(k, part, d).wait()
                total += from_z[k, d - 1, :, cols].astype(F32)
            res[k, place(part, 0), cols] = total.astype(BF)
            gather_copy(k, part, 0).start()

    def stage_y(k):
        for part in range(2):
            gather_copy(k, part, 0).wait()
            gather_copy(k, part, 1).start()

    def stage_x(k):
        for part in range(2):
            gather_copy(k, part, 1).wait()
        last_copy(k).start()

    def stage_out(k):
        last_copy(k).wait()
        out_copy(k).start()

    vec_steps = [(pc, h), (px, h), (py, h)] + [(m, h) for m in more] + [(b, hp), (b, hq)]

    def vec_copy(i):
        return make(101 + i, vec, vec_in.at[i], *vec_steps[i])

    def stage_vec(i):
        vec_copy(i).wait()
        vec[...] += vec_in[i]
        if i + 1 < len(vec_steps):
            vec_copy(i + 1).start()

    stages = {
        "c": stage_core, "a": stage_a, "b": stage_b, "z": stage_z, "y": stage_y, "x": stage_x, "o": stage_out,
        "v": stage_vec,
    }

    def run(*items):
        for kind, k in items:
            stages[kind](k)

    def reduce_chunk(k, half):
        for z in range(4):
            grad = dot_tn(wide_a[z, :, 384 * half : 384 * half + 384], four[1])
            stage[k, z] = grad.astype(BF)

    def expand_chunk(k, half):
        for z in range(4):
            grad = dot_tn(four[0, :, 384 * half : 384 * half + 384], wide_b[z])
            stage[k, z] = grad.astype(BF)

    def weight_grad(k, start, product):
        for half in range(2):
            grad = product(slice(384 * half, 384 * half + 384)).astype(BF)
            for z in range(2):
                stage[k, 2 * half + z, start : start + SLOT, :] = grad[SLOT * z : SLOT * z + SLOT, :]

    def to_keys(source, target):
        @pl.loop(0, 32)
        def _(i):
            rows = pl.ds(pl.multiple_of(i * 16, 16), 16)
            parts = [source[t, rows, :].astype(F32) for t in range(3)]
            for kb in range(4):
                total = parts[0] * masks[0, kb : kb + 1, :]
                for t in (1, 2):
                    total += parts[t] * masks[t, kb : kb + 1, :]
                target[kb, rows, :] = total.astype(BF)

    def fetch(i, slot):
        g, t = i // 3, i % 3
        tile = (pl.ds(pl.multiple_of(t * TILE, TILE), TILE), pl.ds(pl.multiple_of(g * 256, 256), 256))
        pairs = (
            (p_h.at[i], p_v), (ks_h.at[i], ks_v), (vs_h.at[i], vs_v),
            (q_h.at[tile], q_v), (delta_h.at[tile], d_v), (att_h.at[tile], a_v),
        )
        return [pltpu.make_async_copy(src, dst.at[slot], flow.at[n, slot]) for n, (src, dst) in enumerate(pairs)]

    loads[0].wait()
    loads[1].wait()
    for c in loads[2:] + fetch(0, 0):
        c.start()
    reduce_chunk(0, 0)
    pl.semaphore_wait(barrier, len(targets))
    core_copy(0).start()
    reduce_chunk(1, 1)
    core_copy(1).start()
    run(("c", 0))
    loads[2].wait()
    loads[3].wait()
    expand_chunk(2, 0)
    core_copy(2).start()
    run(("c", 1))
    expand_chunk(3, 1)
    core_copy(3).start()

    left = left_lanes(TILE)
    plan = {
        0: (("c", 2),),
        1: (("a", 0),),
        3: (("a", 1),),
        4: (("c", 3),),
        5: (("a", 2),),
        6: (("b", 0),),
        7: (("b", 1),),
        8: (("a", 3),),
    }

    @pl.loop(0, 9)
    def _(i):
        slot = i % 2
        g, t = i // 3, i % 3
        lanes = pl.multiple_of(g * 256, 256)

        @pl.when(i < 8)
        def _():
            for c in fetch(i + 1, 1 - slot):
                c.start()

        for c in fetch(i, slot):
            c.wait()
        for pair in range(2):
            at = slice(128 * pair, 128 * pair + 128)
            q = q_v[slot, :, at]
            delta = d_v[slot, :, at]
            keys = ks_v[slot, :, at]
            values = vs_v[slot, :, at]
            prod = delta.astype(F32) * a_v[slot, :, at].astype(F32)
            dq, dk, dv = [], [], []
            for side in range(2):
                mask = left if side == 0 else jnp.logical_not(left)
                inner = jnp.sum(jnp.where(mask, prod, 0.0), axis=-1, keepdims=True)
                delta_side = jnp.where(mask, delta, jnp.zeros_like(delta))
                probs = p_v[slot, 2 * pair + side]
                dp = dot_nt(delta_side, values)
                ds = (probs.astype(F32) * (dp - inner)).astype(BF)
                dv.append(dot_tn(probs, delta_side))
                dk.append(dot_tn(ds, jnp.where(mask, q, jnp.zeros_like(q))))
                dq.append(dot_nn(ds, keys))
            where = pl.ds(pl.multiple_of(lanes + 128 * pair, 128), 128)
            wide_a[t, 0:BLOCK, where] = ((dk[0] + dk[1]) * SCALE).astype(BF)
            wide_b[t, 0:BLOCK, where] = (dv[0] + dv[1]).astype(BF)
            wide_a[3, pl.ds(pl.multiple_of(t * TILE, TILE), TILE), where] = (
                jnp.where(left, dq[0], dq[1]) * SCALE
            ).astype(BF)
        for n, items in plan.items():

            @pl.when(i == n)
            def _():
                run(*items)

    run(("z", 0))
    loads[4].wait()
    loads[5].wait()
    weight_grad(0, 0, lambda at: dot_tn(four[2, :, at], four[3]))
    to_keys(wide_b, dv_low)
    get_x = [local(16 + kb, xw_h.at[pl.ds(BLOCK * kb, BLOCK)], wide_b.at[kb, pl.ds(0, BLOCK)]) for kb in range(4)]
    for c in get_x:
        c.start()
    run(("b", 2))
    own_at = own_offset(h)
    own_x = [
        local(32 + c, xw_h.at[pl.ds(pl.multiple_of(own_at + TILE * c, TILE), TILE)], own_v.at[pl.ds(TILE * c, TILE)])
        for c in range(3)
    ]
    for c in own_x:
        c.start()
    to_keys(wide_a, four)
    get_w = [
        local(20 + 4 * m + s, wt_h.at[s, m], wide_a.at[m, pl.ds(SLOT * s, SLOT)]) for m in range(3) for s in range(4)
    ]
    for c in get_w:
        c.start()
    for c in get_x:
        c.wait()

    def x_rows():
        return wide_b[:, 0:BLOCK, :].reshape(WINDOW, D)

    weight_grad(0, SLOT, lambda at: dot_tn(dv_low[:, :, at].reshape(WINDOW, 384), x_rows()))
    core_copy(4).start()
    run(("z", 1), ("b", 3))
    vec[...] = sums_in[...]
    vec[10:11, :] = column_sum(wide_a[3].astype(F32))
    vec[11:12, :] = (
        column_sum(dv_low[0].astype(F32))
        + column_sum(dv_low[1].astype(F32))
        + column_sum(dv_low[2].astype(F32))
        + column_sum(dv_low[3].astype(F32))
    )
    vec_copy(0).start()
    run(("c", 4), ("y", 0))
    for c in get_w:
        c.wait()
    loads[6].wait()
    pair_at = own_offset(hp)
    mid_at = pl.multiple_of(1536 * (h % 2), 256)

    def row_part(start):
        kb, rows = start // BLOCK, pl.ds(pl.multiple_of(start % BLOCK, TILE), TILE)
        return dot_nn(four[kb, rows, :], wide_a[1]) + dot_nn(dv_low[kb, rows, :], wide_a[2])

    def pair_copy(c):
        part = pl.ds(TILE * c, TILE)
        return make(96 + c, dx_v.at[part], dx_pair.at[part], b, hp)

    def mid_copy(c):
        part = pl.ds(TILE * c, TILE)
        return make(99 + c, mid_v.at[part], dx_mid.at[part], b, hm)

    def pair_part(c):
        dx_v[TILE * c : TILE * c + TILE, :] = row_part(pair_at + TILE * c).astype(BF)

    def mid_part(c):
        @pl.when(middle)
        def _():
            mid_v[TILE * c : TILE * c + TILE, :] = row_part(mid_at + TILE * c).astype(BF)

    def mid_start(c):
        @pl.when(middle)
        def _():
            mid_copy(c).start()

    def own_part(c):
        rows = slice(TILE * c, TILE * c + TILE)
        own[rows, :] += row_part(own_at + TILE * c) + dot_nn(wide_a[3, rows, :], wide_a[0])

    pair_part(0)
    pair_copy(0).start()
    pair_part(1)
    pair_copy(1).start()
    run(("y", 1), ("v", 0), ("z", 2))
    mid_part(0)
    mid_start(0)
    weight_grad(1, 0, lambda at: dot_tn(four[:, 0:BLOCK, at].reshape(WINDOW, 384), x_rows()))
    run(("x", 0), ("v", 1))
    for c in own_x:
        c.wait()
    weight_grad(1, SLOT, lambda at: dot_tn(wide_a[3, :, at], own_v[...]))
    core_copy(5).start()
    run(("a", 4), ("z", 3), ("y", 2))
    pair_part(2)
    run(("c", 5), ("x", 1), ("v", 2))
    mid_part(1)
    own_part(0)
    run(("b", 4), ("y", 3), ("x", 2))
    own_part(1)
    run(("v", 3),)
    own_part(2)
    run(("o", 0), ("o", 1), ("a", 5), ("x", 3), ("v", 4), ("b", 5))
    pair_copy(2).start()
    mid_start(1)
    run(("o", 2), ("z", 4), ("o", 3), ("y", 4), ("x", 4), ("z", 5), ("o", 4), ("y", 5))
    for i in range(5, len(vec_steps)):
        run(("v", i))
    sums_o[...] = vec[...]
    run(("x", 5),)
    for c in range(3):
        pair_copy(c).wait()
        rows = slice(TILE * c, TILE * c + TILE)
        own[rows, :] += dx_pair[rows, :].astype(F32)

    @pl.when(middle)
    def _():
        for c in range(2):
            mid_copy(c).wait()
            rows = pl.ds(pl.multiple_of(256 * (h % 2) + TILE * c, TILE), TILE)
            own[rows, :] += dx_mid[TILE * c : TILE * c + TILE, :].astype(F32)

    tg_o[...] = own[...].astype(BF)
    run(("o", 5),)
    for k in range(CHUNKS):
        out_copy(k).wait()


def finish(nb, *args):
    hb = pl.BlockSpec(memory_space=pl.ANY)
    vm = pl.BlockSpec(memory_space=pltpu.VMEM)
    extra = max(0, nb.bit_length() - 4)
    count = 106 + extra * (2 * CHUNKS + 1)
    return pl.pallas_call(
        functools.partial(finish_kernel, nb),
        out_shape=(
            jax.ShapeDtypeStruct((CHUNKS, 384, D), BF),
            jax.ShapeDtypeStruct((ROWS, D), BF),
            jax.ShapeDtypeStruct((16, D), F32),
            jax.ShapeDtypeStruct((CHUNKS, extra, 4, 48, D) if extra else (1, 1, 1, 16, 128), BF),
        ),
        in_specs=[hb] * 14 + [vm] * 2,
        out_specs=(hb, vm, vm, hb),
        scratch_shapes=[
            pltpu.VMEM((4, 4, 384, D), BF),
            pltpu.VMEM((CHUNKS, 4, 192, D), BF),
            pltpu.VMEM((CHUNKS, 4, 96, D), BF),
            pltpu.VMEM((CHUNKS, 4, 48, D), BF),
            pltpu.VMEM((CHUNKS, 3, 48, D), BF),
            pltpu.VMEM((CHUNKS, 384, D), BF),
            pltpu.VMEM((ROWS, D), BF),
            pltpu.VMEM((BLOCK, D), BF),
            pltpu.VMEM((16, D), F32),
            pltpu.VMEM((5 + extra, 16, D), F32),
            pltpu.VMEM((4, ROWS, D), BF),
            pltpu.VMEM((4, ROWS, D), BF),
            pltpu.VMEM((4, ROWS, D), BF),
            pltpu.VMEM((4, BLOCK, D), BF),
            pltpu.VMEM((ROWS, D), F32),
            pltpu.VMEM((2, 4, TILE, BLOCK), BF),
            pltpu.VMEM((2, BLOCK, 256), BF),
            pltpu.VMEM((2, BLOCK, 256), BF),
            pltpu.VMEM((2, TILE, 256), BF),
            pltpu.VMEM((2, TILE, 256), BF),
            pltpu.VMEM((2, TILE, 256), BF),
            pltpu.VMEM((ROWS, D), BF),
            pltpu.VMEM((BLOCK, D), BF),
            pltpu.VMEM((ROWS, D), BF),
            pltpu.SemaphoreType.DMA((35,)),
            pltpu.SemaphoreType.DMA((6, 2)),
            pltpu.SemaphoreType.DMA((count,)),
            pltpu.SemaphoreType.DMA((count,)),
        ],
        compiler_params=pltpu.CompilerParams(
            collective_id=1, has_side_effects=True, vmem_limit_bytes=63 * 2**20
        ),
        name="finish",
    )(*args)


def layer(
    nb, tokens, query_weight, key_weight, value_weight, query_bias, value_bias, mixer_weight, mixer_bias,
    first_gain, first_shift, expand_weight, expand_bias, reduce_weight, reduce_bias, second_gain,
    second_shift, cotangent, group_kinds, pair_orders, triple_orders,
):
    h = lax.axis_index("head")
    xw, wt, qbs, vbs, pairs, triples = start_exchange(
        tokens,
        query_weight.T,
        key_weight.T,
        value_weight.T,
        query_bias.reshape(1, -1),
        value_bias.reshape(1, -1),
        pair_orders.transpose(0, 2, 1),
        triple_orders.transpose(1, 0, 2),
    )
    probs, att, inv, q, keys, values, masks = attend(group_kinds, pairs, triples, qbs, vbs, xw, wt)
    vecs = [
        v.reshape(1, -1)
        for v in (mixer_bias, first_gain, first_shift, reduce_bias, second_gain, second_shift, expand_bias)
    ]
    layer_output, mixed_delta, delta, low, rdel, mdel, act, hdel, sums = dense(
        att, tokens, cotangent, mixer_weight, expand_weight, reduce_weight, inv, *vecs
    )
    res, tokens_grad, sums, _ = finish(
        nb, act, hdel, low, rdel, att, mdel, probs, keys, values, q, delta, xw, wt, mixed_delta, masks, sums
    )
    expand_grad = res[2:4].reshape(D, D).astype(F32)
    reduce_grad = res[0:2].reshape(D, D).astype(F32)
    mixer_grad = res[4, 0:SLOT].astype(F32)
    value_grad = res[4, SLOT:].astype(F32).T
    key_grad = res[5, 0:SLOT].astype(F32).T
    query_grad = res[5, SLOT:].astype(F32).T
    biases = lax.dynamic_slice(sums, (10, SLOT * h), (2, SLOT))
    return (
        layer_output,
        tokens_grad,
        query_grad,
        key_grad,
        value_grad,
        biases[0],
        biases[1],
        mixer_grad,
        sums[0],
        sums[1],
        sums[2],
        expand_grad,
        sums[6:10].reshape(FF),
        reduce_grad,
        sums[3],
        sums[4],
        sums[5],
    )


def solution(mesh):
    rows = P(("batch", "head"), None)
    return jax.shard_map(
        functools.partial(layer, mesh.shape["batch"]),
        mesh=mesh,
        in_specs=(
            rows,
            P(None, "head"),
            P(None, "head"),
            P(None, "head"),
            P("head"),
            P("head"),
            P(),
            P(),
            P(),
            P(),
            P(),
            P(),
            P(),
            P(),
            P(),
            P(),
            rows,
            P("batch"),
            P("batch", "head", None),
            P("batch", "head", None),
        ),
        out_specs=(
            rows,
            rows,
            P(None, "head"),
            P(None, "head"),
            P(None, "head"),
            P("head"),
            P("head"),
            P("head", None),
            P(),
            P(),
            P(),
            P(None, "head"),
            P(),
            P("head", None),
            P(),
            P(),
            P(),
        ),
        check_vma=False,
    )
```

```python
import functools
import math

import jax
import jax.numpy as jnp
from jax import lax
from jax.experimental import pallas as pl
from jax.experimental.pallas import tpu as pltpu
from jax.sharding import PartitionSpec as P

MESH = pl.DeviceIdType.MESH
BF = jnp.bfloat16
F32 = jnp.float32
VMEM_LIMIT = 60 * 2**20

D = 768
HEAD_SIZE = 64
BLOCK = 512
ROWS = 768
TILE = 256
WINDOW = 2048
SLOT = 192
FF = 3072
EPSILON = 1e-05
SCALE = 1.0 / math.sqrt(HEAD_SIZE)
EXP2_SCALE = SCALE * math.log2(math.e)
CHUNKS = 6
PIECES = ((0, 0, 384), (1, 0, 384), (2, 0, 384), (3, 0, 384), (4, 0, 384), (5, 0, 256), (5, 256, 128))


def dot_nn(a, b):
    return lax.dot_general(a, b, (((1,), (0,)), ((), ())), preferred_element_type=F32)


def dot_nt(a, b):
    return lax.dot_general(a, b, (((1,), (1,)), ((), ())), preferred_element_type=F32)


def dot_tn(a, b):
    return lax.dot_general(a, b, (((0,), (0,)), ((), ())), preferred_element_type=F32)


def remote(src, dst, send, recv, b, h):
    return pltpu.make_async_remote_copy(
        src_ref=src, dst_ref=dst, send_sem=send, recv_sem=recv, device_id=(b, h), device_id_type=MESH
    )


def flip(b, step):
    return b + step - 2 * step * ((b // step) % 2)


def own_offset(h):
    return pl.multiple_of(768 * h - 1024 * (h // 2), 256)


def start_kernel(
    tok, wq, wk, wv, qb, vb, pairs, triples,
    xw, wt, qbs, vbs, pairs_all, triples_all,
    tok_v, w_v, loc, send, recv,
):
    b = lax.axis_index("batch")
    h = lax.axis_index("head")
    core = b % 2
    pc, px, py = flip(b, 1), flip(b, 2), flip(b, 4)
    hp = flip(h, 1)
    hm = 3 - h
    middle = jnp.logical_or(h == 1, h == 2)
    others = [(h + d) % 4 for d in (1, 2, 3)]
    barrier = pltpu.get_barrier_semaphore()
    for target in [(pc, h), (px, h), (py, h)] + [(b, o) for o in others]:
        pl.semaphore_signal(barrier, inc=1, device_id=target, device_id_type=MESH)

    own = own_offset(h)
    small = ((qb, qbs), (vb, vbs), (pairs, pairs_all), (triples, triples_all))
    weights = (wq, wk, wv)
    fetch = [(tok, tok_v)] + [(src, w_v.at[m]) for m, src in enumerate(weights)]
    fetch = [pltpu.make_async_copy(src, dst, loc.at[i]) for i, (src, dst) in enumerate(fetch)]
    kept = [(tok_v, xw.at[pl.ds(own, ROWS)])]
    kept += [(w_v.at[m], wt.at[h, m]) for m in range(3)]
    kept += [(src, dst.at[h]) for src, dst in small]
    kept = [pltpu.make_async_copy(src, dst, loc.at[4 + i]) for i, (src, dst) in enumerate(kept)]
    fill = pltpu.make_async_copy(
        tok_v.at[pl.ds(0, BLOCK)],
        xw.at[pl.ds(pl.multiple_of(1536 - 512 * h, 256), BLOCK)],
        loc.at[12],
    )
    for c in fetch + kept[4:]:
        c.start()
    pl.semaphore_wait(barrier, 6)

    def piece(who):
        return pl.ds(pl.multiple_of(((who // 2) % 4) * 48, 16), 48)

    lanes = pl.ds(pl.multiple_of(core * 384, 128), 384)
    sem = iter(range(128))

    def make(src, dst, who, where):
        i = next(sem)
        c = remote(src, dst, send.at[i], recv.at[i], who, where)
        return c

    mine = piece(b)
    near = (1, 3, 2)
    over_z = {}
    for d in near:
        for m, src in enumerate(weights):
            c = make(src.at[mine, lanes], wt.at[h, m, mine, lanes], b, others[d - 1])
            c.start()
            over_z[d, m] = c
    tables = []
    for src, dst in small:
        for d in near:
            c = make(src, dst.at[h], b, others[d - 1])
            c.start()
            tables.append(c)
    pair = make(tok, xw.at[pl.ds(own, ROWS)], b, hp)
    cross = make(
        tok.at[pl.ds(pl.multiple_of(256 * (h % 2), 256), BLOCK)],
        xw.at[pl.ds(pl.multiple_of(1536 * ((h + 1) % 2), 256), BLOCK)],
        b,
        hm,
    )

    for i, c in enumerate(fetch):
        c.wait()
        kept[i].start()

    @pl.when(jnp.logical_not(middle))
    def _():
        fill.start()

    def forward(d, m, rows, who):
        slot = (h + 4 - d) % 4
        ref = wt.at[slot, m, rows, lanes]
        c = make(ref, ref, who, h)
        c.start()
        return c

    units = [(d, m) for d in near for m in range(3)]
    first = {}
    for i, (d, m) in enumerate(units):
        over_z[d, m].wait()
        first[d, m] = forward(d, m, mine, px if i % 2 == 0 else py)
        if i == 5:
            pair.start()

            @pl.when(middle)
            def _():
                cross.start()

    second = {}
    for i, (d, m) in enumerate(units):
        first[d, m].wait()
        came, go = (px, py) if i % 2 == 0 else (py, px)
        second[d, m] = [forward(d, m, mine, go), forward(d, m, piece(came), go)]
    third = {}
    for d, m in units:
        for c in second[d, m]:
            c.wait()
        third[d, m] = forward(d, m, slice(None), pc)
    for c in third.values():
        c.wait()
    for c in tables:
        c.wait()
    pair.wait()
    for c in kept:
        c.wait()

    @pl.when(middle)
    def _():
        cross.wait()

    @pl.when(jnp.logical_not(middle))
    def _():
        fill.wait()


def start_exchange(*args):
    hb = pl.BlockSpec(memory_space=pl.ANY)
    qb, pairs, triples = args[4], args[6], args[7]
    return pl.pallas_call(
        start_kernel,
        out_shape=(
            jax.ShapeDtypeStruct((WINDOW, D), BF),
            jax.ShapeDtypeStruct((4, 3, SLOT, D), BF),
            jax.ShapeDtypeStruct((4,) + qb.shape, F32),
            jax.ShapeDtypeStruct((4,) + qb.shape, F32),
            jax.ShapeDtypeStruct((4,) + pairs.shape, jnp.int32),
            jax.ShapeDtypeStruct((4,) + triples.shape, jnp.int32),
        ),
        in_specs=[hb] * 8,
        out_specs=(hb,) * 6,
        scratch_shapes=[
            pltpu.VMEM((ROWS, D), BF),
            pltpu.VMEM((3, SLOT, D), BF),
            pltpu.SemaphoreType.DMA((13,)),
            pltpu.SemaphoreType.DMA((60,)),
            pltpu.SemaphoreType.DMA((60,)),
        ],
        compiler_params=pltpu.CompilerParams(
            collective_id=0, has_side_effects=True, vmem_limit_bytes=VMEM_LIMIT
        ),
        name="start_exchange",
    )(*args)


def key_index(kinds, pairs, triples, h, tile, head):
    block = (3 * h + tile) // 2
    slot, local = head // 3, head % 3
    pair_pick = 2 * (block // 2) + pairs[slot, block // 2, block % 2, local]
    triple_pick = 3 * (block // 3) + triples[slot, local, block // 3, block % 3]
    chosen = jnp.where(kinds[0] == 0, pair_pick, triple_pick)
    return pl.multiple_of((chosen - 2 * (h // 2)) * BLOCK, BLOCK)


def left_lanes(rows):
    return lax.broadcasted_iota(jnp.int32, (rows, 128), 1) < 64


def attend_kernel(
    kinds, pairs, triples, qbs, vbs, xw, wt,
    p_out, att_out, inv_out, q_out, ks_out, vs_out, mask_out,
    x_v, w_v, q_v, k_v, v_v, sems,
):
    g, t = pl.program_id(0), pl.program_id(1)
    h = lax.axis_index("head")

    @pl.when(jnp.logical_and(g == 0, t == 0))
    def _():
        loads = [pltpu.make_async_copy(wt, w_v, sems.at[0])]
        for c in range(4):
            part = pl.ds(512 * c, 512)
            loads.append(pltpu.make_async_copy(xw.at[part], x_v.at[part], sems.at[1 + c]))
        for c in loads:
            c.start()
        q_bias = jnp.concatenate([qbs[s] for s in range(4)], axis=1)
        v_bias = jnp.concatenate([vbs[s] for s in range(4)], axis=1)
        for c in loads:
            c.wait()
        w_q = w_v[:, 0].reshape(D, D)
        w_k = w_v[:, 1].reshape(D, D)
        w_v2 = w_v[:, 2].reshape(D, D)

        @pl.loop(0, 4)
        def _(c):
            at = pl.ds(pl.multiple_of(c * 512, 512), 512)
            x = x_v[at, :]
            k = dot_nt(x, w_k).astype(BF)
            v = (dot_nt(x, w_v2) + v_bias).astype(BF)
            for s in range(3):
                k_v[s, at, :] = k[:, 256 * s : 256 * s + 256]
                v_v[s, at, :] = v[:, 256 * s : 256 * s + 256]

        own = own_offset(h)

        @pl.loop(0, 3)
        def _(c):
            x = x_v[pl.ds(pl.multiple_of(own + c * TILE, TILE), TILE), :]
            q = (dot_nt(x, w_q) + q_bias).astype(BF)
            for s in range(3):
                q_v[s, pl.ds(pl.multiple_of(c * TILE, TILE), TILE), :] = q[:, 256 * s : 256 * s + 256]

    left = left_lanes(TILE)
    left_keys = left_lanes(BLOCK)
    lane_head = lax.broadcasted_iota(jnp.int32, (8, 256), 1) // 64
    key_block = lax.broadcasted_iota(jnp.int32, (8, 256), 0)
    mask_rows = jnp.zeros((8, 256), F32)
    for pair in range(2):
        at = slice(128 * pair, 128 * pair + 128)
        q = q_v[g, pl.ds(pl.multiple_of(t * TILE, TILE), TILE), at]
        q_out[:, at] = q
        found, picked = [], []
        for side in range(2):
            mask = left if side == 0 else jnp.logical_not(left)
            mask_keys = left_keys if side == 0 else jnp.logical_not(left_keys)
            row = key_index(kinds, pairs, triples, h, t, 4 * g + 2 * pair + side)
            keys = k_v[g, pl.ds(row, BLOCK), at]
            values = v_v[g, pl.ds(row, BLOCK), at]
            picked.append((keys, values))
            here = jnp.logical_and(lane_head == 2 * pair + side, key_block == row // BLOCK)
            mask_rows = jnp.where(here, 1.0, mask_rows)
            scores = dot_nt(jnp.where(mask, q, jnp.zeros_like(q)), keys)
            top = jnp.max(scores, axis=-1, keepdims=True)
            raised = jnp.exp2((scores - top) * EXP2_SCALE).astype(BF)
            p_out[0, 2 * pair + side] = raised
            found.append(dot_nn(raised, jnp.where(mask_keys, values, jnp.ones_like(values))))
        result = jnp.where(left, found[0], found[1])
        total = jnp.where(left, found[1], found[0])
        inverse = 1.0 / pltpu.roll(total, 64, 1)
        att_out[:, at] = (result * inverse).astype(BF)
        inv_out[:, at] = inverse
        ks_out[0, :, at] = jnp.where(left_keys, picked[0][0], picked[1][0])
        vs_out[0, :, at] = jnp.where(left_keys, picked[0][1], picked[1][1])
    mask_out[0] = mask_rows


def attend(kinds, pairs, triples, qbs, vbs, xw, wt):
    hb = pl.BlockSpec(memory_space=pl.ANY)
    sm = pl.BlockSpec(memory_space=pltpu.SMEM)
    vm = pl.BlockSpec(memory_space=pltpu.VMEM)
    tile = pl.BlockSpec((TILE, 256), lambda g, t: (t, g))
    picked = pl.BlockSpec((1, BLOCK, 256), lambda g, t: (3 * g + t, 0, 0))
    return pl.pallas_call(
        attend_kernel,
        grid=(3, 3),
        out_shape=(
            jax.ShapeDtypeStruct((9, 4, TILE, BLOCK), BF),
            jax.ShapeDtypeStruct((ROWS, D), BF),
            jax.ShapeDtypeStruct((ROWS, D), F32),
            jax.ShapeDtypeStruct((ROWS, D), BF),
            jax.ShapeDtypeStruct((9, BLOCK, 256), BF),
            jax.ShapeDtypeStruct((9, BLOCK, 256), BF),
            jax.ShapeDtypeStruct((3, 8, D), F32),
        ),
        in_specs=[sm, sm, sm, vm, vm, hb, hb],
        out_specs=(
            pl.BlockSpec((1, 4, TILE, BLOCK), lambda g, t: (3 * g + t, 0, 0, 0)),
            tile,
            tile,
            tile,
            picked,
            picked,
            pl.BlockSpec((1, 8, 256), lambda g, t: (t, 0, g)),
        ),
        scratch_shapes=[
            pltpu.VMEM((WINDOW, D), BF),
            pltpu.VMEM((4, 3, SLOT, D), BF),
            pltpu.VMEM((3, ROWS, 256), BF),
            pltpu.VMEM((3, WINDOW, 256), BF),
            pltpu.VMEM((3, WINDOW, 256), BF),
            pltpu.SemaphoreType.DMA((8,)),
        ],
        compiler_params=pltpu.CompilerParams(
            dimension_semantics=("arbitrary", "arbitrary"), vmem_limit_bytes=VMEM_LIMIT
        ),
        name="attend",
    )(kinds, pairs, triples, qbs, vbs, xw, wt)


def normal_parts(v):
    bell = jnp.exp2(v * v * (-0.5 * math.log2(math.e)))
    t = 1.0 / (1.0 + (0.3275911 / math.sqrt(2.0)) * jnp.abs(v))
    poly = 0.5 * 1.061405429
    poly = poly * t + 0.5 * -1.453152027
    poly = poly * t + 0.5 * 1.421413741
    poly = poly * t + 0.5 * -0.284496736
    poly = poly * t + 0.5 * 0.254829592
    tail = poly * t * bell
    phi_sum = jnp.where(v >= 0, 1.0 - tail, tail)
    return phi_sum, bell * (1.0 / math.sqrt(2.0 * math.pi))


def norm_parts(values):
    center = values - jnp.mean(values, axis=-1, keepdims=True)
    inverse = lax.rsqrt(jnp.mean(center * center, axis=-1, keepdims=True) + EPSILON)
    return center * inverse, inverse


def norm_back(inner, scaled, inverse):
    inner_mean = jnp.mean(inner, axis=-1, keepdims=True)
    cross_mean = jnp.mean(inner * scaled, axis=-1, keepdims=True)
    return inverse * (inner - inner_mean - scaled * cross_mean)


def column_sum(values):
    return jnp.sum(values, axis=0, keepdims=True)


def dense_kernel(
    att_h, tok_h, cot_h, mw_h, ew_h, rw_h, inv_h, mb, g1, s1, rb, g2, s2, eb,
    out_o, mixed_o, delta_o, low, rdel, mdel, act_h, hdel_h, sums_o,
    att, tok, cot, mw, ew, rw, inv, act, slope, hdel, sems,
):
    loads = [
        pltpu.make_async_copy(src, dst, sems.at[i])
        for i, (src, dst) in enumerate(
            ((att_h, att), (mw_h, mw), (tok_h, tok), (ew_h, ew), (rw_h, rw), (cot_h, cot), (inv_h, inv))
        )
    ]
    for c in loads:
        c.start()
    sums_o[...] = jnp.zeros_like(sums_o)

    def row(ref):
        return ref[...].reshape(1, -1)

    for c in loads:
        c.wait()

    @pl.loop(0, 3)
    def _(t):
        at = pl.ds(pl.multiple_of(t * TILE, TILE), TILE)
        mixed = dot_nn(att[at, :], mw[...]) + row(mb) + tok[at, :].astype(F32)
        scaled_one, inverse_one = norm_parts(mixed)
        normed = scaled_one * row(g1) + row(s1)
        normed_low = normed.astype(BF)
        low[at, :] = normed_low
        branch = row(rb) + normed
        for j in range(4):
            cols = slice(768 * j, 768 * j + 768)
            hidden = dot_nn(normed_low, ew[:, cols]) + row(eb)[:, cols]
            phi_sum, bell = normal_parts(hidden)
            active = (hidden * phi_sum).astype(BF)
            act[j, at, :] = active
            slope[:, cols] = (phi_sum + hidden * bell).astype(BF)
            branch += dot_nn(active, rw[cols, :])
        scaled_two, inverse_two = norm_parts(branch)
        out_o[at, :] = (scaled_two * row(g2) + row(s2)).astype(BF)
        upstream = cot[at, :].astype(F32)
        sums_o[4:5, :] += column_sum(upstream * scaled_two)
        sums_o[5:6, :] += column_sum(upstream)
        branch_delta = norm_back(upstream * row(g2), scaled_two, inverse_two)
        reduce_delta = branch_delta.astype(BF)
        rdel[at, :] = reduce_delta
        sums_o[3:4, :] += column_sum(reduce_delta.astype(F32))
        normed_delta = branch_delta
        for j in range(4):
            cols = slice(768 * j, 768 * j + 768)
            back = dot_nt(reduce_delta, rw[cols, :]) * slope[:, cols].astype(F32)
            back_low = back.astype(BF)
            hdel[j, at, :] = back_low
            sums_o[6 + j : 7 + j, :] += column_sum(back_low.astype(F32))
            normed_delta += dot_nt(back_low, ew[:, cols])
        sums_o[1:2, :] += column_sum(normed_delta * scaled_one)
        sums_o[2:3, :] += column_sum(normed_delta)
        mixed_delta = norm_back(normed_delta * row(g1), scaled_one, inverse_one)
        mixed_o[at, :] = mixed_delta
        mixer_delta = mixed_delta.astype(BF)
        mdel[at, :] = mixer_delta
        sums_o[0:1, :] += column_sum(mixer_delta.astype(F32))
        delta_o[at, :] = (dot_nt(mixer_delta, mw[...]) * inv[at, :]).astype(BF)
        pltpu.make_async_copy(act.at[:, at], act_h.at[:, at], sems.at[7 + t]).start()
        pltpu.make_async_copy(hdel.at[:, at], hdel_h.at[:, at], sems.at[10 + t]).start()

    for t in range(3):
        at = pl.ds(t * TILE, TILE)
        pltpu.make_async_copy(act.at[:, at], act_h.at[:, at], sems.at[7 + t]).wait()
        pltpu.make_async_copy(hdel.at[:, at], hdel_h.at[:, at], sems.at[10 + t]).wait()


def dense(*args):
    hb = pl.BlockSpec(memory_space=pl.ANY)
    vm = pl.BlockSpec(memory_space=pltpu.VMEM)
    rows = jax.ShapeDtypeStruct((ROWS, D), BF)
    wide = jax.ShapeDtypeStruct((4, ROWS, D), BF)
    return pl.pallas_call(
        dense_kernel,
        out_shape=(
            rows,
            jax.ShapeDtypeStruct((ROWS, D), F32),
            rows,
            rows,
            rows,
            rows,
            wide,
            wide,
            jax.ShapeDtypeStruct((16, D), F32),
        ),
        in_specs=[hb] * 7 + [vm] * 7,
        out_specs=(vm,) * 6 + (hb, hb, vm),
        scratch_shapes=[
            pltpu.VMEM((ROWS, D), BF),
            pltpu.VMEM((ROWS, D), BF),
            pltpu.VMEM((ROWS, D), BF),
            pltpu.VMEM((D, D), BF),
            pltpu.VMEM((D, FF), BF),
            pltpu.VMEM((FF, D), BF),
            pltpu.VMEM((ROWS, D), F32),
            pltpu.VMEM((4, ROWS, D), BF),
            pltpu.VMEM((TILE, FF), BF),
            pltpu.VMEM((4, ROWS, D), BF),
            pltpu.SemaphoreType.DMA((13,)),
        ],
        compiler_params=pltpu.CompilerParams(vmem_limit_bytes=VMEM_LIMIT),
        name="dense",
    )(*args)


def finish_kernel(
    nb, act_h, hdel_h, low_h, rdel_h, att_h, mdel_h, p_h, ks_h, vs_h, q_h, delta_h, xw_h, wt_h, mixed_h, masks, sums_in,
    res_h, tg_o, sums_o, from_more,
    stage, from_core, from_a, from_b, from_z, res, dx_pair, dx_mid, vec, vec_in,
    wide_a, wide_b, four, dv_low, own, p_v, ks_v, vs_v, q_v, d_v, a_v, dx_v, mid_v, own_v, loc, flow, send, recv,
):
    b = lax.axis_index("batch")
    h = lax.axis_index("head")
    core, xb, yb = b % 2, (b // 2) % 2, (b // 4) % 2
    pc, px, py = flip(b, 1), flip(b, 2), flip(b, 4)
    hp, hm, hq = flip(h, 1), 3 - h, flip(h, 2)
    middle = jnp.logical_or(h == 1, h == 2)
    others = [(h + d) % 4 for d in (1, 2, 3)]
    more = []
    step = 8
    while step < nb:
        more.append(flip(b, step))
        step *= 2
    barrier = pltpu.get_barrier_semaphore()
    targets = [(pc, h), (px, h), (py, h)] + [(m, h) for m in more] + [(b, o) for o in others]
    for target in targets:
        pl.semaphore_signal(barrier, inc=1, device_id=target, device_id_type=MESH)

    def local(i, src, dst):
        return pltpu.make_async_copy(src, dst, loc.at[i])

    loads = [
        local(0, act_h, wide_a),
        local(1, rdel_h, four.at[1]),
        local(2, low_h, four.at[0]),
        local(3, hdel_h, wide_b),
        local(4, att_h, four.at[2]),
        local(5, mdel_h, four.at[3]),
        local(6, mixed_h, own),
    ]
    for c in loads[:2]:
        c.start()

    def make(i, src, dst, who, where):
        return remote(src, dst, send.at[i], recv.at[i], who, where)

    bits = ((xb, px, yb, py), (yb, py, xb, px))
    columns = (pl.ds(0, 384), pl.ds(384, 384))

    def rows_of(start, count):
        return pl.ds(pl.multiple_of(start, 16), count)

    def size(n, level):
        return (PIECES[n][2] // 8, PIECES[n][2] // 4, PIECES[n][2] // 2)[level]

    def place_start(n, part, level):
        start = PIECES[n][1] + core * size(n, 2)
        if level < 2:
            start = start + bits[part][0] * size(n, 1)
        if level < 1:
            start = start + bits[part][2] * size(n, 0)
        return start

    def place(n, part, level):
        return rows_of(place_start(n, part, level), size(n, level))

    def landing(n, level):
        return slice(PIECES[n][1] * size(n, level) // PIECES[n][2], (PIECES[n][1] + PIECES[n][2]) * size(n, level) // PIECES[n][2])

    def land(ref, n, level, cols):
        rows = landing(n, level)
        return ref.at[PIECES[n][0], :, pl.ds(rows.start, rows.stop - rows.start), cols]

    def core_copy(n):
        k, first, _ = PIECES[n]
        src = stage.at[k % 4, :, rows_of(first + (1 - core) * size(n, 2), size(n, 2))]
        return make(n, src, land(from_core, n, 2, slice(None)), pc, h)

    def a_copy(n, part):
        k, first, _ = PIECES[n]
        a_bit, who = bits[part][:2]
        rows = rows_of(first + core * size(n, 2) + (1 - a_bit) * size(n, 1), size(n, 1))
        return make(7 + 2 * n + part, stage.at[k % 4, :, rows, columns[part]], land(from_a, n, 1, columns[part]), who, h)

    def b_copy(n, part):
        k = PIECES[n][0]
        _, _, b_bit, who = bits[part]
        rows = rows_of(place_start(n, part, 1) + (1 - b_bit) * size(n, 0), size(n, 0))
        return make(21 + 2 * n + part, stage.at[k % 4, :, rows, columns[part]], land(from_b, n, 0, columns[part]), who, h)

    def z_copy(n, part, d):
        o = others[d - 1]
        k = PIECES[n][0]
        rows = landing(n, 0)
        dst = from_z.at[k, d - 1, pl.ds(rows.start, rows.stop - rows.start), columns[part]]
        return make(35 + 6 * n + 3 * part + d - 1, stage.at[k % 4, o, place(n, part, 0), columns[part]], dst, b, o)

    def gather_copy(n, part, level):
        ref = res.at[PIECES[n][0], place(n, part, level), columns[part]]
        return make(77 + 14 * level + 2 * n + part, ref, ref, bits[part][3 if level == 0 else 1], h)

    def last_copy(n):
        ref = res.at[PIECES[n][0], place(n, 0, 2)]
        return make(105 + n, ref, ref, pc, h)

    def more_copy(n, part, i):
        src = stage.at[PIECES[n][0] % 4, :, place(n, part, 0), columns[part]]
        dst = from_more.at[n, i, :, pl.ds(0, size(n, 0)), columns[part]]
        return make(122 + len(more) * (2 * n + part + 1) + i, src, dst, more[i], h)

    def out_copy(k):
        return local(8 + k, res.at[k], res_h.at[k])

    def add(n, part, level, other):
        k, block = PIECES[n][0] % 4, size(n, 0)
        start, first = place_start(n, part, level), landing(n, level).start
        cols = slice(0, D) if level == 2 else slice(384 * part, 384 * part + 384)

        @pl.loop(0, size(n, level) // block * 4)
        def _(i):
            z, at = i % 4, i // 4 * block
            mine = rows_of(start + at, block)
            stage[k, z, mine, cols] = stage[k, z, mine, cols] + other[PIECES[n][0], z, rows_of(first + at, block), cols]

    def stage_core(n):
        core_copy(n).wait()
        add(n, 0, 2, from_core)
        for part in range(2):
            a_copy(n, part).start()

    def stage_a(n):
        for part in range(2):
            a_copy(n, part).wait()
            add(n, part, 1, from_a)
            b_copy(n, part).start()

    def stage_b(n):
        for part in range(2):
            b_copy(n, part).wait()
            add(n, part, 0, from_b)
            for i in range(len(more)):
                more_copy(n, part, i).start()
                more_copy(n, part, i).wait()
                get = local(7, from_more.at[n, i, :, pl.ds(0, size(n, 0))], land(from_b, n, 0, slice(None)))
                get.start()
                get.wait()
                add(n, part, 0, from_b)
            for d in (2, 1, 3):
                z_copy(n, part, d).start()

    def stage_z(n):
        k, rows = PIECES[n][0], landing(n, 0)
        for part in range(2):
            cols = slice(384 * part, 384 * part + 384)
            total = stage[k % 4, h, place(n, part, 0), cols].astype(F32)
            for d in (1, 2, 3):
                z_copy(n, part, d).wait()
                total += from_z[k, d - 1, rows, cols].astype(F32)
            res[k, place(n, part, 0), cols] = total.astype(BF)
            gather_copy(n, part, 0).start()

    def stage_y(n):
        for part in range(2):
            gather_copy(n, part, 0).wait()
            gather_copy(n, part, 1).start()

    def stage_x(n):
        for part in range(2):
            gather_copy(n, part, 1).wait()
        last_copy(n).start()

    def stage_out(n):
        last_copy(n).wait()
        if n != len(PIECES) - 2:
            out_copy(PIECES[n][0]).start()

    vec_steps = [(pc, h), (px, h), (py, h)] + [(m, h) for m in more] + [(b, hp), (b, hq)]

    def vec_copy(i):
        return make(117 + i, vec, vec_in.at[i], *vec_steps[i])

    def stage_vec(i):
        vec_copy(i).wait()
        vec[...] += vec_in[i]
        if i + 1 < len(vec_steps):
            vec_copy(i + 1).start()

    stages = {
        "c": stage_core, "a": stage_a, "b": stage_b, "z": stage_z, "y": stage_y, "x": stage_x, "o": stage_out,
        "v": stage_vec,
    }

    def run(*items):
        for kind, k in items:
            stages[kind](k)

    def reduce_chunk(k, half):
        for z in range(4):
            grad = dot_tn(wide_a[z, :, 384 * half : 384 * half + 384], four[1])
            stage[k, z] = grad.astype(BF)

    def expand_chunk(k, half):
        for z in range(4):
            grad = dot_tn(four[0, :, 384 * half : 384 * half + 384], wide_b[z])
            stage[k, z] = grad.astype(BF)

    def weight_grad(k, start, product):
        for half in range(2):
            grad = product(slice(384 * half, 384 * half + 384)).astype(BF)
            for z in range(2):
                stage[k, 2 * half + z, start : start + SLOT, :] = grad[SLOT * z : SLOT * z + SLOT, :]

    def to_keys(source, target):
        @pl.loop(0, 32)
        def _(i):
            rows = pl.ds(pl.multiple_of(i * 16, 16), 16)
            parts = [source[t, rows, :].astype(F32) for t in range(3)]
            for kb in range(4):
                total = parts[0] * masks[0, kb : kb + 1, :]
                for t in (1, 2):
                    total += parts[t] * masks[t, kb : kb + 1, :]
                target[kb, rows, :] = total.astype(BF)

    def fetch(i, slot):
        g, t = i // 3, i % 3
        tile = (pl.ds(pl.multiple_of(t * TILE, TILE), TILE), pl.ds(pl.multiple_of(g * 256, 256), 256))
        pairs = (
            (p_h.at[i], p_v), (ks_h.at[i], ks_v), (vs_h.at[i], vs_v),
            (q_h.at[tile], q_v), (delta_h.at[tile], d_v), (att_h.at[tile], a_v),
        )
        return [pltpu.make_async_copy(src, dst.at[slot], flow.at[n, slot]) for n, (src, dst) in enumerate(pairs)]

    loads[0].wait()
    loads[1].wait()
    for c in loads[2:] + fetch(0, 0):
        c.start()
    reduce_chunk(0, 0)
    pl.semaphore_wait(barrier, len(targets))
    core_copy(0).start()
    reduce_chunk(1, 1)
    core_copy(1).start()
    run(("c", 0))
    loads[2].wait()
    loads[3].wait()
    expand_chunk(2, 0)
    core_copy(2).start()
    run(("c", 1))
    expand_chunk(3, 1)
    core_copy(3).start()

    left = left_lanes(TILE)
    plan = {
        0: (("c", 2),),
        1: (("a", 0),),
        3: (("a", 1),),
        4: (("c", 3),),
        5: (("a", 2),),
        6: (("b", 0),),
        7: (("b", 1),),
        8: (("a", 3),),
    }

    @pl.loop(0, 9)
    def _(i):
        slot = i % 2
        g, t = i // 3, i % 3
        lanes = pl.multiple_of(g * 256, 256)

        @pl.when(i < 8)
        def _():
            for c in fetch(i + 1, 1 - slot):
                c.start()

        for c in fetch(i, slot):
            c.wait()
        for pair in range(2):
            at = slice(128 * pair, 128 * pair + 128)
            q = q_v[slot, :, at]
            delta = d_v[slot, :, at]
            keys = ks_v[slot, :, at]
            values = vs_v[slot, :, at]
            prod = delta.astype(F32) * a_v[slot, :, at].astype(F32)
            dq, dk, dv = [], [], []
            for side in range(2):
                mask = left if side == 0 else jnp.logical_not(left)
                inner = jnp.sum(jnp.where(mask, prod, 0.0), axis=-1, keepdims=True)
                delta_side = jnp.where(mask, delta, jnp.zeros_like(delta))
                probs = p_v[slot, 2 * pair + side]
                dp = dot_nt(delta_side, values)
                ds = (probs.astype(F32) * (dp - inner)).astype(BF)
                dv.append(dot_tn(probs, delta_side))
                dk.append(dot_tn(ds, jnp.where(mask, q, jnp.zeros_like(q))))
                dq.append(dot_nn(ds, keys))
            where = pl.ds(pl.multiple_of(lanes + 128 * pair, 128), 128)
            wide_a[t, 0:BLOCK, where] = ((dk[0] + dk[1]) * SCALE).astype(BF)
            wide_b[t, 0:BLOCK, where] = (dv[0] + dv[1]).astype(BF)
            wide_a[3, pl.ds(pl.multiple_of(t * TILE, TILE), TILE), where] = (
                jnp.where(left, dq[0], dq[1]) * SCALE
            ).astype(BF)
        for n, items in plan.items():

            @pl.when(i == n)
            def _():
                run(*items)

    run(("z", 0))
    loads[4].wait()
    loads[5].wait()
    weight_grad(0, 0, lambda at: dot_tn(four[2, :, at], four[3]))
    to_keys(wide_b, dv_low)
    get_x = [local(16 + kb, xw_h.at[pl.ds(BLOCK * kb, BLOCK)], wide_b.at[kb, pl.ds(0, BLOCK)]) for kb in range(4)]
    for c in get_x:
        c.start()
    run(("b", 2))
    own_at = own_offset(h)
    own_x = [
        local(32 + c, xw_h.at[pl.ds(pl.multiple_of(own_at + TILE * c, TILE), TILE)], own_v.at[pl.ds(TILE * c, TILE)])
        for c in range(3)
    ]
    for c in own_x:
        c.start()
    to_keys(wide_a, four)
    get_w = [
        local(20 + 4 * m + s, wt_h.at[s, m], wide_a.at[m, pl.ds(SLOT * s, SLOT)]) for m in range(3) for s in range(4)
    ]
    for c in get_w:
        c.start()
    for c in get_x:
        c.wait()

    def x_rows():
        return wide_b[:, 0:BLOCK, :].reshape(WINDOW, D)

    weight_grad(0, SLOT, lambda at: dot_tn(dv_low[:, :, at].reshape(WINDOW, 384), x_rows()))
    core_copy(4).start()
    run(("z", 1), ("b", 3))
    vec[...] = sums_in[...]
    vec[10:11, :] = column_sum(wide_a[3].astype(F32))
    vec[11:12, :] = (
        column_sum(dv_low[0].astype(F32))
        + column_sum(dv_low[1].astype(F32))
        + column_sum(dv_low[2].astype(F32))
        + column_sum(dv_low[3].astype(F32))
    )
    vec_copy(0).start()
    run(("c", 4), ("y", 0))
    for c in get_w:
        c.wait()
    loads[6].wait()
    pair_at = own_offset(hp)
    mid_at = pl.multiple_of(1536 * (h % 2), 256)

    def row_part(start):
        kb, rows = start // BLOCK, pl.ds(pl.multiple_of(start % BLOCK, TILE), TILE)
        return dot_nn(four[kb, rows, :], wide_a[1]) + dot_nn(dv_low[kb, rows, :], wide_a[2])

    def pair_copy(c):
        part = pl.ds(TILE * c, TILE)
        return make(112 + c, dx_v.at[part], dx_pair.at[part], b, hp)

    def mid_copy(c):
        part = pl.ds(TILE * c, TILE)
        return make(115 + c, mid_v.at[part], dx_mid.at[part], b, hm)

    def pair_part(c):
        dx_v[TILE * c : TILE * c + TILE, :] = row_part(pair_at + TILE * c).astype(BF)

    def mid_part(c):
        @pl.when(middle)
        def _():
            mid_v[TILE * c : TILE * c + TILE, :] = row_part(mid_at + TILE * c).astype(BF)

    def mid_start(c):
        @pl.when(middle)
        def _():
            mid_copy(c).start()

    def own_part(c):
        rows = slice(TILE * c, TILE * c + TILE)
        own[rows, :] += row_part(own_at + TILE * c) + dot_nn(wide_a[3, rows, :], wide_a[0])

    pair_part(0)
    pair_copy(0).start()
    pair_part(1)
    pair_copy(1).start()
    run(("y", 1), ("v", 0), ("z", 2))
    mid_part(0)
    mid_start(0)
    weight_grad(1, 0, lambda at: dot_tn(four[:, 0:BLOCK, at].reshape(WINDOW, 384), x_rows()))
    run(("x", 0), ("v", 1))
    for c in own_x:
        c.wait()
    weight_grad(1, SLOT, lambda at: dot_tn(wide_a[3, :, at], own_v[...]))
    core_copy(5).start()
    core_copy(6).start()
    run(("a", 4), ("z", 3), ("y", 2))
    pair_part(2)
    run(("c", 5), ("c", 6), ("x", 1), ("v", 2))
    mid_part(1)
    own_part(0)
    run(("b", 4), ("y", 3), ("x", 2))
    own_part(1)
    run(("v", 3),)
    own_part(2)
    run(("o", 0), ("o", 1), ("a", 5), ("x", 3), ("v", 4), ("a", 6), ("z", 4), ("b", 5), ("b", 6))
    pair_copy(2).start()
    mid_start(1)
    run(
        ("o", 2), ("y", 4), ("o", 3), ("z", 5), ("x", 4), ("y", 5), ("z", 6), ("o", 4), ("x", 5), ("y", 6), ("o", 5),
        ("x", 6),
    )
    for i in range(5, len(vec_steps)):
        run(("v", i))
    sums_o[...] = vec[...]
    for c in range(3):
        pair_copy(c).wait()
        rows = slice(TILE * c, TILE * c + TILE)
        own[rows, :] += dx_pair[rows, :].astype(F32)

    @pl.when(middle)
    def _():
        for c in range(2):
            mid_copy(c).wait()
            rows = pl.ds(pl.multiple_of(256 * (h % 2) + TILE * c, TILE), TILE)
            own[rows, :] += dx_mid[TILE * c : TILE * c + TILE, :].astype(F32)

    tg_o[...] = own[...].astype(BF)
    run(("o", 6),)
    for k in range(CHUNKS):
        out_copy(k).wait()


def finish(nb, *args):
    hb = pl.BlockSpec(memory_space=pl.ANY)
    vm = pl.BlockSpec(memory_space=pltpu.VMEM)
    extra = max(0, nb.bit_length() - 4)
    count = 122 + extra * (2 * len(PIECES) + 1)
    return pl.pallas_call(
        functools.partial(finish_kernel, nb),
        out_shape=(
            jax.ShapeDtypeStruct((CHUNKS, 384, D), BF),
            jax.ShapeDtypeStruct((ROWS, D), BF),
            jax.ShapeDtypeStruct((16, D), F32),
            jax.ShapeDtypeStruct((len(PIECES), extra, 4, 48, D) if extra else (1, 1, 1, 16, 128), BF),
        ),
        in_specs=[hb] * 14 + [vm] * 2,
        out_specs=(hb, vm, vm, hb),
        scratch_shapes=[
            pltpu.VMEM((4, 4, 384, D), BF),
            pltpu.VMEM((CHUNKS, 4, 192, D), BF),
            pltpu.VMEM((CHUNKS, 4, 96, D), BF),
            pltpu.VMEM((CHUNKS, 4, 48, D), BF),
            pltpu.VMEM((CHUNKS, 3, 48, D), BF),
            pltpu.VMEM((CHUNKS, 384, D), BF),
            pltpu.VMEM((ROWS, D), BF),
            pltpu.VMEM((BLOCK, D), BF),
            pltpu.VMEM((16, D), F32),
            pltpu.VMEM((5 + extra, 16, D), F32),
            pltpu.VMEM((4, ROWS, D), BF),
            pltpu.VMEM((4, ROWS, D), BF),
            pltpu.VMEM((4, ROWS, D), BF),
            pltpu.VMEM((4, BLOCK, D), BF),
            pltpu.VMEM((ROWS, D), F32),
            pltpu.VMEM((2, 4, TILE, BLOCK), BF),
            pltpu.VMEM((2, BLOCK, 256), BF),
            pltpu.VMEM((2, BLOCK, 256), BF),
            pltpu.VMEM((2, TILE, 256), BF),
            pltpu.VMEM((2, TILE, 256), BF),
            pltpu.VMEM((2, TILE, 256), BF),
            pltpu.VMEM((ROWS, D), BF),
            pltpu.VMEM((BLOCK, D), BF),
            pltpu.VMEM((ROWS, D), BF),
            pltpu.SemaphoreType.DMA((35,)),
            pltpu.SemaphoreType.DMA((6, 2)),
            pltpu.SemaphoreType.DMA((count,)),
            pltpu.SemaphoreType.DMA((count,)),
        ],
        compiler_params=pltpu.CompilerParams(
            collective_id=1, has_side_effects=True, vmem_limit_bytes=63 * 2**20
        ),
        name="finish",
    )(*args)


def unpack_kernel(res, sums, reduce_o, expand_o, mixer_o, value_o, key_o, query_o, qbias_o, vbias_o, hidden_o, *vec_o):
    i = pl.program_id(0)
    h = lax.axis_index("head")

    @pl.when(i == 0)
    def _():
        for n, ref in enumerate(vec_o):
            ref[...] = sums[n : n + 1, :].reshape(D)
        for j in range(4):
            hidden_o[D * j : D * j + D] = sums[6 + j : 7 + j, :].reshape(D)
        for n, ref in ((10, qbias_o), (11, vbias_o)):
            mine = sums[n : n + 1, 0:SLOT]
            for z in range(1, 4):
                mine = jnp.where(h == z, sums[n : n + 1, SLOT * z : SLOT * z + SLOT], mine)
            ref[...] = mine.reshape(SLOT)

    @pl.when(i < 2)
    def _():
        reduce_o[...] = res[0].astype(F32)

    @pl.when(jnp.logical_and(i >= 2, i < 4))
    def _():
        expand_o[...] = res[0].astype(F32)

    @pl.when(i == 4)
    def _():
        mixer_o[...] = res[0, 0:SLOT, :].astype(F32)
        value_o[...] = res[0, SLOT:, :].astype(F32)

    @pl.when(i == 5)
    def _():
        key_o[...] = res[0, 0:SLOT, :].astype(F32)
        query_o[...] = res[0, SLOT:, :].astype(F32)


def unpack(res, sums):
    vm = pl.BlockSpec(memory_space=pltpu.VMEM)
    square = jax.ShapeDtypeStruct((D, D), F32)
    strip = jax.ShapeDtypeStruct((SLOT, D), F32)
    short = jax.ShapeDtypeStruct((SLOT,), F32)
    row = jax.ShapeDtypeStruct((D,), F32)
    return pl.pallas_call(
        unpack_kernel,
        grid=(CHUNKS,),
        out_shape=(square, square, strip, strip, strip, strip, short, short, jax.ShapeDtypeStruct((FF,), F32)) + (row,) * 6,
        in_specs=[pl.BlockSpec((1, 384, D), lambda i: (i, 0, 0)), vm],
        out_specs=(
            pl.BlockSpec((384, D), lambda i: (jnp.minimum(i, 1), 0)),
            pl.BlockSpec((384, D), lambda i: (jnp.clip(i - 2, 0, 1), 0)),
        )
        + (vm,) * 13,
        compiler_params=pltpu.CompilerParams(dimension_semantics=("arbitrary",), vmem_limit_bytes=VMEM_LIMIT),
        name="unpack",
    )(res, sums)


def layer(
    nb, tokens, query_weight, key_weight, value_weight, query_bias, value_bias, mixer_weight, mixer_bias,
    first_gain, first_shift, expand_weight, expand_bias, reduce_weight, reduce_bias, second_gain,
    second_shift, cotangent, group_kinds, pair_orders, triple_orders,
):
    xw, wt, qbs, vbs, pairs, triples = start_exchange(
        tokens,
        query_weight.T,
        key_weight.T,
        value_weight.T,
        query_bias.reshape(1, -1),
        value_bias.reshape(1, -1),
        pair_orders.transpose(0, 2, 1),
        triple_orders.transpose(1, 0, 2),
    )
    probs, att, inv, q, keys, values, masks = attend(group_kinds, pairs, triples, qbs, vbs, xw, wt)
    vecs = (mixer_bias, first_gain, first_shift, reduce_bias, second_gain, second_shift, expand_bias)
    layer_output, mixed_delta, delta, low, rdel, mdel, act, hdel, sums = dense(
        att, tokens, cotangent, mixer_weight, expand_weight, reduce_weight, inv, *vecs
    )
    res, tokens_grad, sums, _ = finish(
        nb, act, hdel, low, rdel, att, mdel, probs, keys, values, q, delta, xw, wt, mixed_delta, masks, sums
    )
    out = unpack(res, sums)
    reduce_grad, expand_grad, mixer_grad, value_grad, key_grad, query_grad, query_sum, value_sum, hidden_sum = out[:9]
    mixer_sum, gain_one, shift_one, reduce_sum, gain_two, shift_two = out[9:]
    return (
        layer_output,
        tokens_grad,
        query_grad.T,
        key_grad.T,
        value_grad.T,
        query_sum,
        value_sum,
        mixer_grad,
        mixer_sum,
        gain_one,
        shift_one,
        expand_grad,
        hidden_sum,
        reduce_grad,
        reduce_sum,
        gain_two,
        shift_two,
    )


def solution(mesh):
    rows = P(("batch", "head"), None)
    return jax.shard_map(
        functools.partial(layer, mesh.shape["batch"]),
        mesh=mesh,
        in_specs=(
            rows,
            P(None, "head"),
            P(None, "head"),
            P(None, "head"),
            P("head"),
            P("head"),
            P(),
            P(),
            P(),
            P(),
            P(),
            P(),
            P(),
            P(),
            P(),
            P(),
            rows,
            P("batch"),
            P("batch", "head", None),
            P("batch", "head", None),
        ),
        out_specs=(
            rows,
            rows,
            P(None, "head"),
            P(None, "head"),
            P(None, "head"),
            P("head"),
            P("head"),
            P("head", None),
            P(),
            P(),
            P(),
            P(None, "head"),
            P(),
            P("head", None),
            P(),
            P(),
            P(),
        ),
        check_vma=False,
    )
```

```python
import functools
import math

import jax
import jax.numpy as jnp
from jax import lax
from jax.experimental import pallas as pl
from jax.experimental.pallas import tpu as pltpu
from jax.sharding import PartitionSpec as P

MESH = pl.DeviceIdType.MESH
BF = jnp.bfloat16
F32 = jnp.float32
VMEM_LIMIT = 60 * 2**20

D = 768
HEAD_SIZE = 64
BLOCK = 512
ROWS = 768
TILE = 256
WINDOW = 2048
SLOT = 192
FF = 3072
EPSILON = 1e-05
SCALE = 1.0 / math.sqrt(HEAD_SIZE)
EXP2_SCALE = SCALE * math.log2(math.e)
CHUNKS = 6
PIECES = ((0, 0, 384), (1, 0, 384), (2, 0, 384), (3, 0, 384), (4, 0, 384), (5, 0, 256), (5, 256, 128))


def dot_nn(a, b):
    return lax.dot_general(a, b, (((1,), (0,)), ((), ())), preferred_element_type=F32)


def dot_nt(a, b):
    return lax.dot_general(a, b, (((1,), (1,)), ((), ())), preferred_element_type=F32)


def dot_tn(a, b):
    return lax.dot_general(a, b, (((0,), (0,)), ((), ())), preferred_element_type=F32)


def remote(src, dst, send, recv, b, h):
    return pltpu.make_async_remote_copy(
        src_ref=src, dst_ref=dst, send_sem=send, recv_sem=recv, device_id=(b, h), device_id_type=MESH
    )


def flip(b, step):
    return b + step - 2 * step * ((b // step) % 2)


def own_offset(h):
    return pl.multiple_of(768 * h - 1024 * (h // 2), 256)


def key_index(kinds, pairs, triples, h, tile, head):
    block = (3 * h + tile) // 2
    slot, local = head // 3, head % 3
    pair_pick = 2 * (block // 2) + pairs[slot, block // 2, block % 2, local]
    triple_pick = 3 * (block // 3) + triples[slot, local, block // 3, block % 3]
    chosen = jnp.where(kinds[0] == 0, pair_pick, triple_pick)
    return chosen - 2 * (h // 2)


def left_lanes(rows):
    return lax.broadcasted_iota(jnp.int32, (rows, 128), 1) < 64


def normal_parts(v):
    bell = jnp.exp2(v * v * (-0.5 * math.log2(math.e)))
    t = 1.0 / (1.0 + (0.3275911 / math.sqrt(2.0)) * jnp.abs(v))
    poly = 0.5 * 1.061405429
    poly = poly * t + 0.5 * -1.453152027
    poly = poly * t + 0.5 * 1.421413741
    poly = poly * t + 0.5 * -0.284496736
    poly = poly * t + 0.5 * 0.254829592
    tail = poly * t * bell
    phi_sum = jnp.where(v >= 0, 1.0 - tail, tail)
    return phi_sum, bell * (1.0 / math.sqrt(2.0 * math.pi))


def norm_parts(values):
    center = values - jnp.mean(values, axis=-1, keepdims=True)
    inverse = lax.rsqrt(jnp.mean(center * center, axis=-1, keepdims=True) + EPSILON)
    return center * inverse, inverse


def norm_back(inner, scaled, inverse):
    inner_mean = jnp.mean(inner, axis=-1, keepdims=True)
    cross_mean = jnp.mean(inner * scaled, axis=-1, keepdims=True)
    return inverse * (inner - inner_mean - scaled * cross_mean)


def column_sum(values):
    return jnp.sum(values, axis=0, keepdims=True)


def begin_kernel(
    tok, wq, wk, wv, qb, vb, pairs, triples, kinds, cot_h, mw_h, ew_h, rw_h, mb, g1, s1, rb, g2, s2, eb,
    xw_h, wt_h, qbs, vbs, pairs_all, triples_all, p_h, ks_h, vs_h, q_h, att_h, low_h, rdel_h, mdel_h, delta_h, out_h,
    mixed_h, act_h, hdel_h, masks_o, sums_o,
    x_v, w_v, qb_v, vb_v, pairs_s, triples_s, kv, q_v, p_v, ks_v, vs_v, att, inv, cot, mw, ew, rw, act, slope,
    low, rdel, mdel, delta_v, out_v, mixed_v, loc, flow, send, recv,
):
    b = lax.axis_index("batch")
    h = lax.axis_index("head")
    core = b % 2
    pc, px, py = flip(b, 1), flip(b, 2), flip(b, 4)
    hp = flip(h, 1)
    hm = 3 - h
    middle = jnp.logical_or(h == 1, h == 2)
    others = [(h + d) % 4 for d in (1, 2, 3)]
    barrier = pltpu.get_barrier_semaphore()
    for target in [(pc, h), (px, h), (py, h)] + [(b, o) for o in others]:
        pl.semaphore_signal(barrier, inc=1, device_id=target, device_id_type=MESH)

    def local(i, src, dst):
        return pltpu.make_async_copy(src, dst, loc.at[i])

    own = own_offset(h)
    rest = pl.multiple_of(1536 * (1 - h // 2), 256)
    small = ((qb, qbs), (vb, vbs), (pairs, pairs_all), (triples, triples_all))
    weights = (wq, wk, wv)
    kept = [local(0, tok, x_v.at[pl.ds(own, ROWS)])]
    kept += [local(1 + m, src, w_v.at[h, m]) for m, src in enumerate(weights)]
    kept += [local(4 + m, src, dst.at[h]) for m, (src, dst) in enumerate(small)]
    for c in kept:
        c.start()
    fill = local(8, tok.at[pl.ds(0, BLOCK)], x_v.at[pl.ds(rest, BLOCK)])

    @pl.when(jnp.logical_not(middle))
    def _():
        fill.start()

    pl.semaphore_wait(barrier, 6)

    def piece(who):
        return pl.ds(pl.multiple_of(((who // 2) % 4) * 48, 16), 48)

    lanes = pl.ds(pl.multiple_of(core * 384, 128), 384)
    sem = iter(range(128))

    def make(src, dst, who, where):
        i = next(sem)
        return remote(src, dst, send.at[i], recv.at[i], who, where)

    mine = piece(b)
    near = (1, 3, 2)
    over_z = {}
    for d in near:
        for m, src in enumerate(weights):
            c = make(src.at[mine, lanes], w_v.at[h, m, mine, lanes], b, others[d - 1])
            c.start()
            over_z[d, m] = c
    tables = []
    for src, dst in small:
        for d in near:
            c = make(src, dst.at[h], b, others[d - 1])
            c.start()
            tables.append(c)
    pair = make(tok, x_v.at[pl.ds(own, ROWS)], b, hp)
    cross = make(
        tok.at[pl.ds(pl.multiple_of(256 * (h % 2), 256), BLOCK)],
        x_v.at[pl.ds(pl.multiple_of(1536 * ((h + 1) % 2), 256), BLOCK)],
        b,
        hm,
    )
    loads = [
        local(9 + i, src, dst)
        for i, (src, dst) in enumerate(((mw_h, mw), (ew_h, ew), (rw_h, rw), (cot_h, cot)))
    ]
    for c in loads:
        c.start()
    sums_o[...] = jnp.zeros_like(sums_o)

    def forward(d, m, rows, who):
        slot = (h + 4 - d) % 4
        ref = w_v.at[slot, m, rows, lanes]
        c = make(ref, ref, who, h)
        c.start()
        return c

    units = [(d, m) for d in near for m in range(3)]
    first = {}
    for i, (d, m) in enumerate(units):
        over_z[d, m].wait()
        first[d, m] = forward(d, m, mine, px if i % 2 == 0 else py)
        if i == 5:
            pair.start()

            @pl.when(middle)
            def _():
                cross.start()

    second = {}
    for i, (d, m) in enumerate(units):
        first[d, m].wait()
        came, go = (px, py) if i % 2 == 0 else (py, px)
        second[d, m] = [forward(d, m, mine, go), forward(d, m, piece(came), go)]
    third = {}
    for d, m in units:
        for c in second[d, m]:
            c.wait()
        third[d, m] = forward(d, m, slice(None), pc)
    for c in tables:
        c.wait()
    for c in kept:
        c.wait()
    tables = [
        local(13 + i, src, dst)
        for i, (src, dst) in enumerate(((qbs, qb_v), (vbs, vb_v), (pairs_all, pairs_s), (triples_all, triples_s)))
    ]
    for c in tables:
        c.start()
    for c in third.values():
        c.wait()
    for c in tables:
        c.wait()

    save_w = local(17, w_v, wt_h)
    save_w.start()
    q_bias = jnp.concatenate([qb_v[s] for s in range(4)], axis=1)
    v_bias = jnp.concatenate([vb_v[s] for s in range(4)], axis=1)

    def keys_values(start, count):
        for c in range(count // TILE):
            rows = pl.ds(pl.multiple_of(start + c * TILE, TILE), TILE)
            x = x_v[rows, :]
            kv[rows, :] = dot_nt(x, w_v[:, 1].reshape(D, D)).astype(BF)
            more = pl.ds(pl.multiple_of(WINDOW + start + c * TILE, TILE), TILE)
            kv[more, :] = (dot_nt(x, w_v[:, 2].reshape(D, D)) + v_bias).astype(BF)

    for c in range(3):
        x = x_v[pl.ds(pl.multiple_of(own + c * TILE, TILE), TILE), :]
        q = (dot_nt(x, w_v[:, 0].reshape(D, D)) + q_bias).astype(BF)
        for s in range(3):
            q_v[s, TILE * c : TILE * c + TILE, :] = q[:, 256 * s : 256 * s + 256]
    save_q = local(18, q_v, q_h)
    save_q.start()
    keys_values(own, ROWS)
    pair.wait()
    keys_values(own_offset(hp), ROWS)

    @pl.when(middle)
    def _():
        cross.wait()

    @pl.when(jnp.logical_not(middle))
    def _():
        fill.wait()

    keys_values(rest, BLOCK)
    save_x = local(19, x_v, xw_h)
    save_x.start()

    left = left_lanes(TILE)
    left_keys = left_lanes(BLOCK)
    lane_head = lax.broadcasted_iota(jnp.int32, (8, 256), 1) // 64
    key_block = lax.broadcasted_iota(jnp.int32, (8, 256), 0)

    def stream(i, slot):
        parts = ((p_v, p_h), (ks_v, ks_h), (vs_v, vs_h))
        return [pltpu.make_async_copy(src.at[slot], dst.at[i], flow.at[n, slot]) for n, (src, dst) in enumerate(parts)]

    @pl.loop(0, 9)
    def _(i):
        slot = i % 2
        g, t = i // 3, i % 3
        rows = pl.ds(pl.multiple_of(t * TILE, TILE), TILE)

        @pl.when(i >= 2)
        def _():
            for c in stream(i - 2, slot):
                c.wait()

        mask_rows = jnp.zeros((8, 256), F32)
        for two in range(2):
            at = slice(128 * two, 128 * two + 128)
            wide = pl.ds(pl.multiple_of(g * 256 + 128 * two, 128), 128)
            q = q_v[g, rows, at]
            for side in range(2):
                chosen = key_index(kinds, pairs_s, triples_s, h, t, 4 * g + 2 * two + side)
                here = jnp.logical_and(lane_head == 2 * two + side, key_block == chosen)
                mask_rows = jnp.where(here, 1.0, mask_rows)

            def pick(first):
                total = None
                for kb in range(4):
                    part = kv[first + BLOCK * kb : first + BLOCK * kb + BLOCK, wide] * mask_rows[kb : kb + 1, at].astype(BF)
                    total = part if total is None else total + part
                return total

            keys, values = pick(0), pick(WINDOW)
            ks_v[slot, :, at] = keys
            vs_v[slot, :, at] = values
            found = []
            for side in range(2):
                mask = left if side == 0 else jnp.logical_not(left)
                mask_keys = left_keys if side == 0 else jnp.logical_not(left_keys)
                scores = dot_nt(jnp.where(mask, q, jnp.zeros_like(q)), keys)
                top = jnp.max(scores, axis=-1, keepdims=True)
                raised = jnp.exp2((scores - top) * EXP2_SCALE).astype(BF)
                p_v[slot, 2 * two + side] = raised
                found.append(dot_nn(raised, jnp.where(mask_keys, values, jnp.ones_like(values))))
            result = jnp.where(left, found[0], found[1])
            total = jnp.where(left, found[1], found[0])
            inverse = 1.0 / pltpu.roll(total, 64, 1)
            att[rows, wide] = (result * inverse).astype(BF)
            inv[rows, wide] = inverse
        masks_o[t, :, pl.ds(pl.multiple_of(g * 256, 256), 256)] = mask_rows
        for c in stream(i, slot):
            c.start()

    for i in (7, 8):
        for c in stream(i, i % 2):
            c.wait()
    save_att = local(20, att, att_h)
    save_att.start()
    for c in loads:
        c.wait()

    def row(ref):
        return ref[...].reshape(1, -1)

    def hdel(j, t):
        return pl.ds(pl.multiple_of(768 * j + t * TILE, TILE), TILE)

    def tile_saves(t):
        at = pl.ds(pl.multiple_of(t * TILE, TILE), TILE)
        parts = [(low, low_h), (rdel, rdel_h), (mdel, mdel_h), (delta_v, delta_h), (out_v, out_h), (mixed_v, mixed_h)]
        parts = [(src.at[at], dst.at[at]) for src, dst in parts]
        parts.append((act.at[:, at], act_h.at[:, at]))
        parts += [(kv.at[hdel(j, t)], hdel_h.at[j, at]) for j in range(4)]
        return [local(21 + n, src, dst) for n, (src, dst) in enumerate(parts)]

    @pl.loop(0, 3)
    def _(t):
        at = pl.ds(pl.multiple_of(t * TILE, TILE), TILE)
        x = x_v[pl.ds(pl.multiple_of(own + t * TILE, TILE), TILE), :]
        mixed = dot_nn(att[at, :], mw[...]) + row(mb) + x.astype(F32)
        scaled_one, inverse_one = norm_parts(mixed)
        normed = scaled_one * row(g1) + row(s1)
        normed_low = normed.astype(BF)
        low[at, :] = normed_low
        branch = row(rb) + normed
        for j in range(4):
            cols = slice(768 * j, 768 * j + 768)
            hidden = dot_nn(normed_low, ew[:, cols]) + row(eb)[:, cols]
            phi_sum, bell = normal_parts(hidden)
            active = (hidden * phi_sum).astype(BF)
            act[j, at, :] = active
            slope[:, cols] = (phi_sum + hidden * bell).astype(BF)
            branch += dot_nn(active, rw[cols, :])
        scaled_two, inverse_two = norm_parts(branch)
        out_v[at, :] = (scaled_two * row(g2) + row(s2)).astype(BF)
        upstream = cot[at, :].astype(F32)
        sums_o[4:5, :] += column_sum(upstream * scaled_two)
        sums_o[5:6, :] += column_sum(upstream)
        branch_delta = norm_back(upstream * row(g2), scaled_two, inverse_two)
        reduce_delta = branch_delta.astype(BF)
        rdel[at, :] = reduce_delta
        sums_o[3:4, :] += column_sum(reduce_delta.astype(F32))
        normed_delta = branch_delta
        for j in range(4):
            cols = slice(768 * j, 768 * j + 768)
            back = dot_nt(reduce_delta, rw[cols, :]) * slope[:, cols].astype(F32)
            back_low = back.astype(BF)
            kv[hdel(j, t), :] = back_low
            sums_o[6 + j : 7 + j, :] += column_sum(back_low.astype(F32))
            normed_delta += dot_nt(back_low, ew[:, cols])
        sums_o[1:2, :] += column_sum(normed_delta * scaled_one)
        sums_o[2:3, :] += column_sum(normed_delta)
        mixed_delta = norm_back(normed_delta * row(g1), scaled_one, inverse_one)
        mixed_v[at, :] = mixed_delta
        mixer_delta = mixed_delta.astype(BF)
        mdel[at, :] = mixer_delta
        sums_o[0:1, :] += column_sum(mixer_delta.astype(F32))
        delta_v[at, :] = (dot_nt(mixer_delta, mw[...]) * inv[at, :]).astype(BF)

        @pl.when(t > 0)
        def _():
            for c in tile_saves(t - 1):
                c.wait()

        for c in tile_saves(t):
            c.start()

    for c in tile_saves(2):
        c.wait()
    for c in (save_w, save_q, save_x, save_att):
        c.wait()


def begin(*args):
    hb = pl.BlockSpec(memory_space=pl.ANY)
    vm = pl.BlockSpec(memory_space=pltpu.VMEM)
    sm = pl.BlockSpec(memory_space=pltpu.SMEM)
    qb, pairs, triples = args[4], args[6], args[7]
    rows = jax.ShapeDtypeStruct((ROWS, D), BF)
    rows_wide = jax.ShapeDtypeStruct((ROWS, D), F32)
    wide = jax.ShapeDtypeStruct((4, ROWS, D), BF)
    picked = jax.ShapeDtypeStruct((9, BLOCK, 256), BF)
    return pl.pallas_call(
        begin_kernel,
        out_shape=(
            jax.ShapeDtypeStruct((WINDOW, D), BF),
            jax.ShapeDtypeStruct((4, 3, SLOT, D), BF),
            jax.ShapeDtypeStruct((4,) + qb.shape, F32),
            jax.ShapeDtypeStruct((4,) + qb.shape, F32),
            jax.ShapeDtypeStruct((4,) + pairs.shape, jnp.int32),
            jax.ShapeDtypeStruct((4,) + triples.shape, jnp.int32),
            jax.ShapeDtypeStruct((9, 4, TILE, BLOCK), BF),
            picked,
            picked,
            jax.ShapeDtypeStruct((3, ROWS, 256), BF),
            rows,
            rows,
            rows,
            rows,
            rows,
            rows,
            rows_wide,
            wide,
            wide,
            jax.ShapeDtypeStruct((3, 8, D), F32),
            jax.ShapeDtypeStruct((16, D), F32),
        ),
        in_specs=[hb] * 8 + [sm] + [hb] * 4 + [vm] * 7,
        out_specs=(hb,) * 19 + (vm, vm),
        scratch_shapes=[
            pltpu.VMEM((WINDOW, D), BF),
            pltpu.VMEM((4, 3, SLOT, D), BF),
            pltpu.VMEM((4,) + qb.shape, F32),
            pltpu.VMEM((4,) + qb.shape, F32),
            pltpu.SMEM((4,) + pairs.shape, jnp.int32),
            pltpu.SMEM((4,) + triples.shape, jnp.int32),
            pltpu.VMEM((2 * WINDOW, D), BF),
            pltpu.VMEM((3, ROWS, 256), BF),
            pltpu.VMEM((2, 4, TILE, BLOCK), BF),
            pltpu.VMEM((2, BLOCK, 256), BF),
            pltpu.VMEM((2, BLOCK, 256), BF),
            pltpu.VMEM((ROWS, D), BF),
            pltpu.VMEM((ROWS, D), F32),
            pltpu.VMEM((ROWS, D), BF),
            pltpu.VMEM((D, D), BF),
            pltpu.VMEM((D, FF), BF),
            pltpu.VMEM((FF, D), BF),
            pltpu.VMEM((4, ROWS, D), BF),
            pltpu.VMEM((TILE, FF), BF),
            pltpu.VMEM((ROWS, D), BF),
            pltpu.VMEM((ROWS, D), BF),
            pltpu.VMEM((ROWS, D), BF),
            pltpu.VMEM((ROWS, D), BF),
            pltpu.VMEM((ROWS, D), BF),
            pltpu.VMEM((ROWS, D), F32),
            pltpu.SemaphoreType.DMA((32,)),
            pltpu.SemaphoreType.DMA((3, 2)),
            pltpu.SemaphoreType.DMA((60,)),
            pltpu.SemaphoreType.DMA((60,)),
        ],
        compiler_params=pltpu.CompilerParams(
            collective_id=0, has_side_effects=True, vmem_limit_bytes=63 * 2**20
        ),
        name="begin",
    )(*args)


def finish_kernel(
    nb, act_h, hdel_h, low_h, rdel_h, att_h, mdel_h, p_h, ks_h, vs_h, q_h, delta_h, xw_h, wt_h, mixed_h, masks, sums_in,
    res_h, tg_o, sums_o, from_more,
    stage, from_core, from_a, from_b, from_z, res, dx_pair, dx_mid, vec, vec_in,
    wide_a, wide_b, four, dv_low, own, p_v, ks_v, vs_v, q_v, d_v, a_v, dx_v, mid_v, own_v, loc, flow, send, recv,
):
    b = lax.axis_index("batch")
    h = lax.axis_index("head")
    core, xb, yb = b % 2, (b // 2) % 2, (b // 4) % 2
    pc, px, py = flip(b, 1), flip(b, 2), flip(b, 4)
    hp, hm, hq = flip(h, 1), 3 - h, flip(h, 2)
    middle = jnp.logical_or(h == 1, h == 2)
    others = [(h + d) % 4 for d in (1, 2, 3)]
    more = []
    step = 8
    while step < nb:
        more.append(flip(b, step))
        step *= 2
    barrier = pltpu.get_barrier_semaphore()
    targets = [(pc, h), (px, h), (py, h)] + [(m, h) for m in more] + [(b, o) for o in others]
    for target in targets:
        pl.semaphore_signal(barrier, inc=1, device_id=target, device_id_type=MESH)

    def local(i, src, dst):
        return pltpu.make_async_copy(src, dst, loc.at[i])

    loads = [
        local(0, act_h, wide_a),
        local(1, rdel_h, four.at[1]),
        local(2, low_h, four.at[0]),
        local(3, hdel_h, wide_b),
        local(4, att_h, four.at[2]),
        local(5, mdel_h, four.at[3]),
        local(6, mixed_h, own),
    ]
    for c in loads[:2]:
        c.start()

    def make(i, src, dst, who, where):
        return remote(src, dst, send.at[i], recv.at[i], who, where)

    bits = ((xb, px, yb, py), (yb, py, xb, px))
    columns = (pl.ds(0, 384), pl.ds(384, 384))

    def rows_of(start, count):
        return pl.ds(pl.multiple_of(start, 16), count)

    def size(n, level):
        return (PIECES[n][2] // 8, PIECES[n][2] // 4, PIECES[n][2] // 2)[level]

    def place_start(n, part, level):
        start = PIECES[n][1] + core * size(n, 2)
        if level < 2:
            start = start + bits[part][0] * size(n, 1)
        if level < 1:
            start = start + bits[part][2] * size(n, 0)
        return start

    def place(n, part, level):
        return rows_of(place_start(n, part, level), size(n, level))

    def landing(n, level):
        return slice(PIECES[n][1] * size(n, level) // PIECES[n][2], (PIECES[n][1] + PIECES[n][2]) * size(n, level) // PIECES[n][2])

    def land(ref, n, level, cols):
        rows = landing(n, level)
        return ref.at[PIECES[n][0], :, pl.ds(rows.start, rows.stop - rows.start), cols]

    def core_copy(n):
        k, first, _ = PIECES[n]
        src = stage.at[k % 4, :, rows_of(first + (1 - core) * size(n, 2), size(n, 2))]
        return make(n, src, land(from_core, n, 2, slice(None)), pc, h)

    def a_copy(n, part):
        k, first, _ = PIECES[n]
        a_bit, who = bits[part][:2]
        rows = rows_of(first + core * size(n, 2) + (1 - a_bit) * size(n, 1), size(n, 1))
        return make(7 + 2 * n + part, stage.at[k % 4, :, rows, columns[part]], land(from_a, n, 1, columns[part]), who, h)

    def b_copy(n, part):
        k = PIECES[n][0]
        _, _, b_bit, who = bits[part]
        rows = rows_of(place_start(n, part, 1) + (1 - b_bit) * size(n, 0), size(n, 0))
        return make(21 + 2 * n + part, stage.at[k % 4, :, rows, columns[part]], land(from_b, n, 0, columns[part]), who, h)

    def z_copy(n, part, d):
        o = others[d - 1]
        k = PIECES[n][0]
        rows = landing(n, 0)
        dst = from_z.at[k, d - 1, pl.ds(rows.start, rows.stop - rows.start), columns[part]]
        return make(35 + 6 * n + 3 * part + d - 1, stage.at[k % 4, o, place(n, part, 0), columns[part]], dst, b, o)

    def gather_copy(n, part, level):
        ref = res.at[PIECES[n][0], place(n, part, level), columns[part]]
        return make(77 + 14 * level + 2 * n + part, ref, ref, bits[part][3 if level == 0 else 1], h)

    def last_copy(n):
        ref = res.at[PIECES[n][0], place(n, 0, 2)]
        return make(105 + n, ref, ref, pc, h)

    def more_copy(n, part, i):
        src = stage.at[PIECES[n][0] % 4, :, place(n, part, 0), columns[part]]
        dst = from_more.at[n, i, :, pl.ds(0, size(n, 0)), columns[part]]
        return make(122 + len(more) * (2 * n + part + 1) + i, src, dst, more[i], h)

    def out_copy(k):
        return local(8 + k, res.at[k], res_h.at[k])

    def add(n, part, level, other):
        k, block = PIECES[n][0] % 4, size(n, 0)
        start, first = place_start(n, part, level), landing(n, level).start
        cols = slice(0, D) if level == 2 else slice(384 * part, 384 * part + 384)

        @pl.loop(0, size(n, level) // block * 4)
        def _(i):
            z, at = i % 4, i // 4 * block
            mine = rows_of(start + at, block)
            stage[k, z, mine, cols] = stage[k, z, mine, cols] + other[PIECES[n][0], z, rows_of(first + at, block), cols]

    def stage_core(n):
        core_copy(n).wait()
        add(n, 0, 2, from_core)
        for part in range(2):
            a_copy(n, part).start()

    def stage_a(n):
        for part in range(2):
            a_copy(n, part).wait()
            add(n, part, 1, from_a)
            b_copy(n, part).start()

    def stage_b(n):
        for part in range(2):
            b_copy(n, part).wait()
            add(n, part, 0, from_b)
            for i in range(len(more)):
                more_copy(n, part, i).start()
                more_copy(n, part, i).wait()
                get = local(7, from_more.at[n, i, :, pl.ds(0, size(n, 0))], land(from_b, n, 0, slice(None)))
                get.start()
                get.wait()
                add(n, part, 0, from_b)
            for d in (2, 1, 3):
                z_copy(n, part, d).start()

    def stage_z(n):
        k, rows = PIECES[n][0], landing(n, 0)
        for part in range(2):
            cols = slice(384 * part, 384 * part + 384)
            total = stage[k % 4, h, place(n, part, 0), cols].astype(F32)
            for d in (1, 2, 3):
                z_copy(n, part, d).wait()
                total += from_z[k, d - 1, rows, cols].astype(F32)
            res[k, place(n, part, 0), cols] = total.astype(BF)
            gather_copy(n, part, 0).start()

    def stage_y(n):
        for part in range(2):
            gather_copy(n, part, 0).wait()
            gather_copy(n, part, 1).start()

    def stage_x(n):
        for part in range(2):
            gather_copy(n, part, 1).wait()
        last_copy(n).start()

    def stage_out(n):
        last_copy(n).wait()
        if n != len(PIECES) - 2:
            out_copy(PIECES[n][0]).start()

    vec_steps = [(pc, h), (px, h), (py, h)] + [(m, h) for m in more] + [(b, hp), (b, hq)]

    def vec_copy(i):
        return make(117 + i, vec, vec_in.at[i], *vec_steps[i])

    def stage_vec(i):
        vec_copy(i).wait()
        vec[...] += vec_in[i]
        if i + 1 < len(vec_steps):
            vec_copy(i + 1).start()

    stages = {
        "c": stage_core, "a": stage_a, "b": stage_b, "z": stage_z, "y": stage_y, "x": stage_x, "o": stage_out,
        "v": stage_vec,
    }

    def run(*items):
        for kind, k in items:
            stages[kind](k)

    def reduce_chunk(k, half):
        for z in range(4):
            grad = dot_tn(wide_a[z, :, 384 * half : 384 * half + 384], four[1])
            stage[k, z] = grad.astype(BF)

    def expand_chunk(k, half):
        for z in range(4):
            grad = dot_tn(four[0, :, 384 * half : 384 * half + 384], wide_b[z])
            stage[k, z] = grad.astype(BF)

    def weight_grad(k, start, product):
        for half in range(2):
            grad = product(slice(384 * half, 384 * half + 384)).astype(BF)
            for z in range(2):
                stage[k, 2 * half + z, start : start + SLOT, :] = grad[SLOT * z : SLOT * z + SLOT, :]

    def to_keys(source, target):
        @pl.loop(0, 32)
        def _(i):
            rows = pl.ds(pl.multiple_of(i * 16, 16), 16)
            parts = [source[t, rows, :].astype(F32) for t in range(3)]
            for kb in range(4):
                total = parts[0] * masks[0, kb : kb + 1, :]
                for t in (1, 2):
                    total += parts[t] * masks[t, kb : kb + 1, :]
                target[kb, rows, :] = total.astype(BF)

    def fetch(i, slot):
        g, t = i // 3, i % 3
        tile = (pl.ds(pl.multiple_of(t * TILE, TILE), TILE), pl.ds(pl.multiple_of(g * 256, 256), 256))
        pairs = (
            (p_h.at[i], p_v), (ks_h.at[i], ks_v), (vs_h.at[i], vs_v),
            (q_h.at[g, tile[0]], q_v), (delta_h.at[tile], d_v), (att_h.at[tile], a_v),
        )
        return [pltpu.make_async_copy(src, dst.at[slot], flow.at[n, slot]) for n, (src, dst) in enumerate(pairs)]

    loads[0].wait()
    loads[1].wait()
    for c in loads[2:] + fetch(0, 0):
        c.start()
    reduce_chunk(0, 0)
    pl.semaphore_wait(barrier, len(targets))
    core_copy(0).start()
    reduce_chunk(1, 1)
    core_copy(1).start()
    run(("c", 0))
    loads[2].wait()
    loads[3].wait()
    expand_chunk(2, 0)
    core_copy(2).start()
    run(("c", 1))
    expand_chunk(3, 1)
    core_copy(3).start()

    left = left_lanes(TILE)
    plan = {
        0: (("c", 2),),
        1: (("a", 0),),
        3: (("a", 1),),
        4: (("c", 3),),
        5: (("a", 2),),
        6: (("b", 0),),
        7: (("b", 1),),
        8: (("a", 3),),
    }

    @pl.loop(0, 9)
    def _(i):
        slot = i % 2
        g, t = i // 3, i % 3
        lanes = pl.multiple_of(g * 256, 256)

        @pl.when(i < 8)
        def _():
            for c in fetch(i + 1, 1 - slot):
                c.start()

        for c in fetch(i, slot):
            c.wait()
        for pair in range(2):
            at = slice(128 * pair, 128 * pair + 128)
            q = q_v[slot, :, at]
            delta = d_v[slot, :, at]
            keys = ks_v[slot, :, at]
            values = vs_v[slot, :, at]
            prod = delta.astype(F32) * a_v[slot, :, at].astype(F32)
            dq, dk, dv = [], [], []
            for side in range(2):
                mask = left if side == 0 else jnp.logical_not(left)
                inner = jnp.sum(jnp.where(mask, prod, 0.0), axis=-1, keepdims=True)
                delta_side = jnp.where(mask, delta, jnp.zeros_like(delta))
                probs = p_v[slot, 2 * pair + side]
                dp = dot_nt(delta_side, values)
                ds = (probs.astype(F32) * (dp - inner)).astype(BF)
                dv.append(dot_tn(probs, delta_side))
                dk.append(dot_tn(ds, jnp.where(mask, q, jnp.zeros_like(q))))
                dq.append(dot_nn(ds, keys))
            where = pl.ds(pl.multiple_of(lanes + 128 * pair, 128), 128)
            wide_a[t, 0:BLOCK, where] = ((dk[0] + dk[1]) * SCALE).astype(BF)
            wide_b[t, 0:BLOCK, where] = (dv[0] + dv[1]).astype(BF)
            wide_a[3, pl.ds(pl.multiple_of(t * TILE, TILE), TILE), where] = (
                jnp.where(left, dq[0], dq[1]) * SCALE
            ).astype(BF)
        for n, items in plan.items():

            @pl.when(i == n)
            def _():
                run(*items)

    run(("z", 0))
    loads[4].wait()
    loads[5].wait()
    weight_grad(0, 0, lambda at: dot_tn(four[2, :, at], four[3]))
    to_keys(wide_b, dv_low)
    get_x = [local(16 + kb, xw_h.at[pl.ds(BLOCK * kb, BLOCK)], wide_b.at[kb, pl.ds(0, BLOCK)]) for kb in range(4)]
    for c in get_x:
        c.start()
    run(("b", 2))
    own_at = own_offset(h)
    own_x = [
        local(32 + c, xw_h.at[pl.ds(pl.multiple_of(own_at + TILE * c, TILE), TILE)], own_v.at[pl.ds(TILE * c, TILE)])
        for c in range(3)
    ]
    for c in own_x:
        c.start()
    to_keys(wide_a, four)
    get_w = [
        local(20 + 4 * m + s, wt_h.at[s, m], wide_a.at[m, pl.ds(SLOT * s, SLOT)]) for m in range(3) for s in range(4)
    ]
    for c in get_w:
        c.start()
    for c in get_x:
        c.wait()

    def x_rows():
        return wide_b[:, 0:BLOCK, :].reshape(WINDOW, D)

    weight_grad(0, SLOT, lambda at: dot_tn(dv_low[:, :, at].reshape(WINDOW, 384), x_rows()))
    core_copy(4).start()
    run(("z", 1), ("b", 3))
    vec[...] = sums_in[...]
    vec[10:11, :] = column_sum(wide_a[3].astype(F32))
    vec[11:12, :] = (
        column_sum(dv_low[0].astype(F32))
        + column_sum(dv_low[1].astype(F32))
        + column_sum(dv_low[2].astype(F32))
        + column_sum(dv_low[3].astype(F32))
    )
    vec_copy(0).start()
    run(("c", 4), ("y", 0))
    for c in get_w:
        c.wait()
    loads[6].wait()
    pair_at = own_offset(hp)
    mid_at = pl.multiple_of(1536 * (h % 2), 256)

    def row_part(start):
        kb, rows = start // BLOCK, pl.ds(pl.multiple_of(start % BLOCK, TILE), TILE)
        return dot_nn(four[kb, rows, :], wide_a[1]) + dot_nn(dv_low[kb, rows, :], wide_a[2])

    def pair_copy(c):
        part = pl.ds(TILE * c, TILE)
        return make(112 + c, dx_v.at[part], dx_pair.at[part], b, hp)

    def mid_copy(c):
        part = pl.ds(TILE * c, TILE)
        return make(115 + c, mid_v.at[part], dx_mid.at[part], b, hm)

    def pair_part(c):
        dx_v[TILE * c : TILE * c + TILE, :] = row_part(pair_at + TILE * c).astype(BF)

    def mid_part(c):
        @pl.when(middle)
        def _():
            mid_v[TILE * c : TILE * c + TILE, :] = row_part(mid_at + TILE * c).astype(BF)

    def mid_start(c):
        @pl.when(middle)
        def _():
            mid_copy(c).start()

    def own_part(c):
        rows = slice(TILE * c, TILE * c + TILE)
        own[rows, :] += row_part(own_at + TILE * c) + dot_nn(wide_a[3, rows, :], wide_a[0])

    pair_part(0)
    pair_copy(0).start()
    pair_part(1)
    pair_copy(1).start()
    run(("y", 1), ("v", 0), ("z", 2))
    mid_part(0)
    mid_start(0)
    weight_grad(1, 0, lambda at: dot_tn(four[:, 0:BLOCK, at].reshape(WINDOW, 384), x_rows()))
    run(("x", 0), ("v", 1))
    for c in own_x:
        c.wait()
    weight_grad(1, SLOT, lambda at: dot_tn(wide_a[3, :, at], own_v[...]))
    core_copy(5).start()
    core_copy(6).start()
    run(("a", 4), ("z", 3), ("y", 2))
    pair_part(2)
    run(("c", 5), ("c", 6), ("x", 1), ("v", 2))
    mid_part(1)
    own_part(0)
    run(("b", 4), ("y", 3), ("x", 2))
    own_part(1)
    run(("v", 3),)
    own_part(2)
    run(("o", 0), ("o", 1), ("a", 5), ("x", 3), ("v", 4), ("a", 6), ("z", 4), ("b", 5), ("b", 6))
    pair_copy(2).start()
    mid_start(1)
    run(
        ("o", 2), ("y", 4), ("o", 3), ("z", 5), ("x", 4), ("y", 5), ("z", 6), ("o", 4), ("x", 5), ("y", 6), ("o", 5),
        ("x", 6),
    )
    for i in range(5, len(vec_steps)):
        run(("v", i))
    sums_o[...] = vec[...]
    for c in range(3):
        pair_copy(c).wait()
        rows = slice(TILE * c, TILE * c + TILE)
        own[rows, :] += dx_pair[rows, :].astype(F32)

    @pl.when(middle)
    def _():
        for c in range(2):
            mid_copy(c).wait()
            rows = pl.ds(pl.multiple_of(256 * (h % 2) + TILE * c, TILE), TILE)
            own[rows, :] += dx_mid[TILE * c : TILE * c + TILE, :].astype(F32)

    tg_o[...] = own[...].astype(BF)
    run(("o", 6),)
    for k in range(CHUNKS):
        out_copy(k).wait()


def finish(nb, *args):
    hb = pl.BlockSpec(memory_space=pl.ANY)
    vm = pl.BlockSpec(memory_space=pltpu.VMEM)
    extra = max(0, nb.bit_length() - 4)
    count = 122 + extra * (2 * len(PIECES) + 1)
    return pl.pallas_call(
        functools.partial(finish_kernel, nb),
        out_shape=(
            jax.ShapeDtypeStruct((CHUNKS, 384, D), BF),
            jax.ShapeDtypeStruct((ROWS, D), BF),
            jax.ShapeDtypeStruct((16, D), F32),
            jax.ShapeDtypeStruct((len(PIECES), extra, 4, 48, D) if extra else (1, 1, 1, 16, 128), BF),
        ),
        in_specs=[hb] * 14 + [vm] * 2,
        out_specs=(hb, vm, vm, hb),
        scratch_shapes=[
            pltpu.VMEM((4, 4, 384, D), BF),
            pltpu.VMEM((CHUNKS, 4, 192, D), BF),
            pltpu.VMEM((CHUNKS, 4, 96, D), BF),
            pltpu.VMEM((CHUNKS, 4, 48, D), BF),
            pltpu.VMEM((CHUNKS, 3, 48, D), BF),
            pltpu.VMEM((CHUNKS, 384, D), BF),
            pltpu.VMEM((ROWS, D), BF),
            pltpu.VMEM((BLOCK, D), BF),
            pltpu.VMEM((16, D), F32),
            pltpu.VMEM((5 + extra, 16, D), F32),
            pltpu.VMEM((4, ROWS, D), BF),
            pltpu.VMEM((4, ROWS, D), BF),
            pltpu.VMEM((4, ROWS, D), BF),
            pltpu.VMEM((4, BLOCK, D), BF),
            pltpu.VMEM((ROWS, D), F32),
            pltpu.VMEM((2, 4, TILE, BLOCK), BF),
            pltpu.VMEM((2, BLOCK, 256), BF),
            pltpu.VMEM((2, BLOCK, 256), BF),
            pltpu.VMEM((2, TILE, 256), BF),
            pltpu.VMEM((2, TILE, 256), BF),
            pltpu.VMEM((2, TILE, 256), BF),
            pltpu.VMEM((ROWS, D), BF),
            pltpu.VMEM((BLOCK, D), BF),
            pltpu.VMEM((ROWS, D), BF),
            pltpu.SemaphoreType.DMA((35,)),
            pltpu.SemaphoreType.DMA((6, 2)),
            pltpu.SemaphoreType.DMA((count,)),
            pltpu.SemaphoreType.DMA((count,)),
        ],
        compiler_params=pltpu.CompilerParams(
            collective_id=1, has_side_effects=True, vmem_limit_bytes=63 * 2**20
        ),
        name="finish",
    )(*args)


def unpack_kernel(
    res, sums, reduce_h, expand_h, mixer_h, value_h, key_h, query_h, qbias_o, vbias_o, hidden_o, *rest
):
    vec_o, (low, full, sems) = rest[:6], rest[6:]
    h = lax.axis_index("head")
    gets = [pltpu.make_async_copy(res.at[k], low.at[k], sems.at[k]) for k in range(CHUNKS)]
    for c in gets:
        c.start()
    for n, ref in enumerate(vec_o):
        ref[...] = sums[n : n + 1, :].reshape(D)
    for j in range(4):
        hidden_o[D * j : D * j + D] = sums[6 + j : 7 + j, :].reshape(D)
    for n, ref in ((10, qbias_o), (11, vbias_o)):
        mine = sums[n : n + 1, 0:SLOT]
        for z in range(1, 4):
            mine = jnp.where(h == z, sums[n : n + 1, SLOT * z : SLOT * z + SLOT], mine)
        ref[...] = mine.reshape(SLOT)
    upper, lower = pl.ds(0, SLOT), pl.ds(SLOT, SLOT)
    targets = (
        (reduce_h.at[pl.ds(0, 384)],),
        (reduce_h.at[pl.ds(384, 384)],),
        (expand_h.at[pl.ds(0, 384)],),
        (expand_h.at[pl.ds(384, 384)],),
        (mixer_h, value_h),
        (key_h, query_h),
    )
    puts = []
    for k in range(CHUNKS):
        gets[k].wait()

        @pl.loop(0, 12)
        def _(i):
            rows = pl.ds(pl.multiple_of(i * 32, 32), 32)
            full[k, rows, :] = low[k, rows, :].astype(F32)

        views = (full.at[k],) if k < 4 else (full.at[k, upper], full.at[k, lower])
        for view, target in zip(views, targets[k]):
            c = pltpu.make_async_copy(view, target, sems.at[CHUNKS + len(puts)])
            c.start()
            puts.append(c)
    for c in puts:
        c.wait()


def unpack(res, sums):
    vm = pl.BlockSpec(memory_space=pltpu.VMEM)
    hb = pl.BlockSpec(memory_space=pl.ANY)
    square = jax.ShapeDtypeStruct((D, D), F32)
    strip = jax.ShapeDtypeStruct((SLOT, D), F32)
    short = jax.ShapeDtypeStruct((SLOT,), F32)
    row = jax.ShapeDtypeStruct((D,), F32)
    return pl.pallas_call(
        unpack_kernel,
        out_shape=(square, square, strip, strip, strip, strip, short, short, jax.ShapeDtypeStruct((FF,), F32)) + (row,) * 6,
        in_specs=[hb, vm],
        out_specs=(hb,) * 6 + (vm,) * 9,
        scratch_shapes=[
            pltpu.VMEM((CHUNKS, 384, D), BF),
            pltpu.VMEM((CHUNKS, 384, D), F32),
            pltpu.SemaphoreType.DMA((14,)),
        ],
        compiler_params=pltpu.CompilerParams(vmem_limit_bytes=VMEM_LIMIT),
        name="unpack",
    )(res, sums)


def layer(
    nb, tokens, query_weight, key_weight, value_weight, query_bias, value_bias, mixer_weight, mixer_bias,
    first_gain, first_shift, expand_weight, expand_bias, reduce_weight, reduce_bias, second_gain,
    second_shift, cotangent, group_kinds, pair_orders, triple_orders,
):
    (
        xw, wt, _, _, _, _, probs, keys, values, q, att, low, rdel, mdel, delta, layer_output, mixed_delta, act, hdel,
        masks, sums,
    ) = begin(
        tokens,
        query_weight.T,
        key_weight.T,
        value_weight.T,
        query_bias.reshape(1, -1),
        value_bias.reshape(1, -1),
        pair_orders.transpose(0, 2, 1),
        triple_orders.transpose(1, 0, 2),
        group_kinds,
        cotangent,
        mixer_weight,
        expand_weight,
        reduce_weight,
        mixer_bias,
        first_gain,
        first_shift,
        reduce_bias,
        second_gain,
        second_shift,
        expand_bias,
    )
    res, tokens_grad, sums, _ = finish(
        nb, act, hdel, low, rdel, att, mdel, probs, keys, values, q, delta, xw, wt, mixed_delta, masks, sums
    )
    out = unpack(res, sums)
    reduce_grad, expand_grad, mixer_grad, value_grad, key_grad, query_grad, query_sum, value_sum, hidden_sum = out[:9]
    mixer_sum, gain_one, shift_one, reduce_sum, gain_two, shift_two = out[9:]
    return (
        layer_output,
        tokens_grad,
        query_grad.T,
        key_grad.T,
        value_grad.T,
        query_sum,
        value_sum,
        mixer_grad,
        mixer_sum,
        gain_one,
        shift_one,
        expand_grad,
        hidden_sum,
        reduce_grad,
        reduce_sum,
        gain_two,
        shift_two,
    )


def solution(mesh):
    rows = P(("batch", "head"), None)
    return jax.shard_map(
        functools.partial(layer, mesh.shape["batch"]),
        mesh=mesh,
        in_specs=(
            rows,
            P(None, "head"),
            P(None, "head"),
            P(None, "head"),
            P("head"),
            P("head"),
            P(),
            P(),
            P(),
            P(),
            P(),
            P(),
            P(),
            P(),
            P(),
            P(),
            rows,
            P("batch"),
            P("batch", "head", None),
            P("batch", "head", None),
        ),
        out_specs=(
            rows,
            rows,
            P(None, "head"),
            P(None, "head"),
            P(None, "head"),
            P("head"),
            P("head"),
            P("head", None),
            P(),
            P(),
            P(),
            P(None, "head"),
            P(),
            P("head", None),
            P(),
            P(),
            P(),
        ),
        check_vma=False,
    )
```

```python
import functools
import math

import jax
import jax.numpy as jnp
from jax import lax
from jax.experimental import pallas as pl
from jax.experimental.pallas import tpu as pltpu
from jax.sharding import PartitionSpec as P

MESH = pl.DeviceIdType.MESH
BF = jnp.bfloat16
F32 = jnp.float32
VMEM_LIMIT = 60 * 2**20

D = 768
HEAD_SIZE = 64
BLOCK = 512
ROWS = 768
TILE = 256
WINDOW = 2048
SLOT = 192
FF = 3072
EPSILON = 1e-05
SCALE = 1.0 / math.sqrt(HEAD_SIZE)
EXP2_SCALE = SCALE * math.log2(math.e)
CHUNKS = 6
PIECES = ((0, 0, 384), (1, 0, 384), (2, 0, 384), (3, 0, 384), (4, 0, 384), (5, 0, 256), (5, 256, 128))


def dot_nn(a, b):
    return lax.dot_general(a, b, (((1,), (0,)), ((), ())), preferred_element_type=F32)


def dot_nt(a, b):
    return lax.dot_general(a, b, (((1,), (1,)), ((), ())), preferred_element_type=F32)


def dot_tn(a, b):
    return lax.dot_general(a, b, (((0,), (0,)), ((), ())), preferred_element_type=F32)


def remote(src, dst, send, recv, b, h):
    return pltpu.make_async_remote_copy(
        src_ref=src, dst_ref=dst, send_sem=send, recv_sem=recv, device_id=(b, h), device_id_type=MESH
    )


def flip(b, step):
    return b + step - 2 * step * ((b // step) % 2)


def own_offset(h):
    return pl.multiple_of(768 * h - 1024 * (h // 2), 256)


def key_index(kinds, pairs, triples, h, tile, head):
    block = (3 * h + tile) // 2
    slot, local = head // 3, head % 3
    pair_pick = 2 * (block // 2) + pairs[slot, block // 2, block % 2, local]
    triple_pick = 3 * (block // 3) + triples[slot, local, block // 3, block % 3]
    chosen = jnp.where(kinds[0] == 0, pair_pick, triple_pick)
    return chosen - 2 * (h // 2)


def left_lanes(rows):
    return lax.broadcasted_iota(jnp.int32, (rows, 128), 1) < 64


def normal_parts(v):
    bell = jnp.exp2(v * v * (-0.5 * math.log2(math.e)))
    t = 1.0 / (1.0 + (0.3275911 / math.sqrt(2.0)) * jnp.abs(v))
    poly = 0.5 * 1.061405429
    poly = poly * t + 0.5 * -1.453152027
    poly = poly * t + 0.5 * 1.421413741
    poly = poly * t + 0.5 * -0.284496736
    poly = poly * t + 0.5 * 0.254829592
    tail = poly * t * bell
    phi_sum = jnp.where(v >= 0, 1.0 - tail, tail)
    return phi_sum, bell * (1.0 / math.sqrt(2.0 * math.pi))


def norm_parts(values):
    center = values - jnp.mean(values, axis=-1, keepdims=True)
    inverse = lax.rsqrt(jnp.mean(center * center, axis=-1, keepdims=True) + EPSILON)
    return center * inverse, inverse


def norm_back(inner, scaled, inverse):
    inner_mean = jnp.mean(inner, axis=-1, keepdims=True)
    cross_mean = jnp.mean(inner * scaled, axis=-1, keepdims=True)
    return inverse * (inner - inner_mean - scaled * cross_mean)


def column_sum(values):
    return jnp.sum(values, axis=0, keepdims=True)


def begin_kernel(
    tok, wq, wk, wv, qb, vb, pairs, triples, kinds, cot_h, mw_h, ew_h, rw_h, mb, g1, s1, rb, g2, s2, eb,
    xw_h, wt_h, qbs, vbs, pairs_all, triples_all, p_h, ks_h, vs_h, q_h, att_h, low_h, rdel_h, scaled_h, out_h,
    inv_h, inverse_h, act_h, slope_h, masks_o, sums_o,
    x_v, w_v, qb_v, vb_v, pairs_s, triples_s, kv, q_v, p_v, ks_v, vs_v, att, inv, cot, mw, ew, rw, act,
    low, rdel, scaled_v, out_v, inverse_v, loc, flow, send, recv,
):
    b = lax.axis_index("batch")
    h = lax.axis_index("head")
    core = b % 2
    pc, px, py = flip(b, 1), flip(b, 2), flip(b, 4)
    hp = flip(h, 1)
    hm = 3 - h
    middle = jnp.logical_or(h == 1, h == 2)
    others = [(h + d) % 4 for d in (1, 2, 3)]
    barrier = pltpu.get_barrier_semaphore()
    for target in [(pc, h), (px, h), (py, h)] + [(b, o) for o in others]:
        pl.semaphore_signal(barrier, inc=1, device_id=target, device_id_type=MESH)

    def local(i, src, dst):
        return pltpu.make_async_copy(src, dst, loc.at[i])

    own = own_offset(h)
    rest = pl.multiple_of(1536 * (1 - h // 2), 256)
    small = ((qb, qbs), (vb, vbs), (pairs, pairs_all), (triples, triples_all))
    weights = (wq, wk, wv)
    kept = [local(0, tok, x_v.at[pl.ds(own, ROWS)])]
    kept += [local(1 + m, src, w_v.at[h, m]) for m, src in enumerate(weights)]
    kept += [local(4 + m, src, dst.at[h]) for m, (src, dst) in enumerate(small)]
    for c in kept:
        c.start()
    fill = local(8, tok.at[pl.ds(0, BLOCK)], x_v.at[pl.ds(rest, BLOCK)])

    @pl.when(jnp.logical_not(middle))
    def _():
        fill.start()

    pl.semaphore_wait(barrier, 6)

    def piece(who):
        return pl.ds(pl.multiple_of(((who // 2) % 4) * 48, 16), 48)

    lanes = pl.ds(pl.multiple_of(core * 384, 128), 384)
    sem = iter(range(128))

    def make(src, dst, who, where):
        i = next(sem)
        return remote(src, dst, send.at[i], recv.at[i], who, where)

    mine = piece(b)
    near = (1, 3, 2)
    over_z = {}
    for d in near:
        for m, src in enumerate(weights):
            c = make(src.at[mine, lanes], w_v.at[h, m, mine, lanes], b, others[d - 1])
            c.start()
            over_z[d, m] = c
    tables = []
    for src, dst in small:
        for d in near:
            c = make(src, dst.at[h], b, others[d - 1])
            c.start()
            tables.append(c)
    pair = make(tok, x_v.at[pl.ds(own, ROWS)], b, hp)
    cross = make(
        tok.at[pl.ds(pl.multiple_of(256 * (h % 2), 256), BLOCK)],
        x_v.at[pl.ds(pl.multiple_of(1536 * ((h + 1) % 2), 256), BLOCK)],
        b,
        hm,
    )
    loads = [
        local(9 + i, src, dst)
        for i, (src, dst) in enumerate(((mw_h, mw), (ew_h, ew), (rw_h, rw), (cot_h, cot)))
    ]
    for c in loads:
        c.start()
    sums_o[...] = jnp.zeros_like(sums_o)

    def forward(d, m, rows, who):
        slot = (h + 4 - d) % 4
        ref = w_v.at[slot, m, rows, lanes]
        c = make(ref, ref, who, h)
        c.start()
        return c

    units = [(d, m) for d in near for m in range(3)]
    first = {}
    for i, (d, m) in enumerate(units):
        over_z[d, m].wait()
        first[d, m] = forward(d, m, mine, px if i % 2 == 0 else py)
        if i == 5:
            pair.start()

            @pl.when(middle)
            def _():
                cross.start()

    second = {}
    for i, (d, m) in enumerate(units):
        first[d, m].wait()
        came, go = (px, py) if i % 2 == 0 else (py, px)
        second[d, m] = [forward(d, m, mine, go), forward(d, m, piece(came), go)]
    third = {}
    for d, m in units:
        for c in second[d, m]:
            c.wait()
        third[d, m] = forward(d, m, slice(None), pc)
    for c in tables:
        c.wait()
    for c in kept:
        c.wait()
    tables = [
        local(13 + i, src, dst)
        for i, (src, dst) in enumerate(((qbs, qb_v), (vbs, vb_v), (pairs_all, pairs_s), (triples_all, triples_s)))
    ]
    for c in tables:
        c.start()
    for c in third.values():
        c.wait()
    for c in tables:
        c.wait()

    save_w = local(17, w_v, wt_h)
    save_w.start()
    q_bias = jnp.concatenate([qb_v[s] for s in range(4)], axis=1)
    v_bias = jnp.concatenate([vb_v[s] for s in range(4)], axis=1)

    def keys_values(start, count):
        for c in range(count // TILE):
            rows = pl.ds(pl.multiple_of(start + c * TILE, TILE), TILE)
            x = x_v[rows, :]
            kv[rows, :] = dot_nt(x, w_v[:, 1].reshape(D, D)).astype(BF)
            more = pl.ds(pl.multiple_of(WINDOW + start + c * TILE, TILE), TILE)
            kv[more, :] = (dot_nt(x, w_v[:, 2].reshape(D, D)) + v_bias).astype(BF)

    for c in range(3):
        x = x_v[pl.ds(pl.multiple_of(own + c * TILE, TILE), TILE), :]
        q = (dot_nt(x, w_v[:, 0].reshape(D, D)) + q_bias).astype(BF)
        for s in range(3):
            q_v[s, TILE * c : TILE * c + TILE, :] = q[:, 256 * s : 256 * s + 256]
    save_q = local(18, q_v, q_h)
    save_q.start()
    keys_values(own, ROWS)
    pair.wait()
    keys_values(own_offset(hp), ROWS)

    @pl.when(middle)
    def _():
        cross.wait()

    @pl.when(jnp.logical_not(middle))
    def _():
        fill.wait()

    keys_values(rest, BLOCK)
    save_x = local(19, x_v, xw_h)
    save_x.start()

    left = left_lanes(TILE)
    left_keys = left_lanes(BLOCK)
    lane_head = lax.broadcasted_iota(jnp.int32, (8, 256), 1) // 64
    key_block = lax.broadcasted_iota(jnp.int32, (8, 256), 0)

    def stream(i, slot):
        parts = ((p_v, p_h), (ks_v, ks_h), (vs_v, vs_h))
        return [pltpu.make_async_copy(src.at[slot], dst.at[i], flow.at[n, slot]) for n, (src, dst) in enumerate(parts)]

    @pl.loop(0, 9)
    def _(i):
        slot = i % 2
        g, t = i // 3, i % 3
        rows = pl.ds(pl.multiple_of(t * TILE, TILE), TILE)

        @pl.when(i >= 2)
        def _():
            for c in stream(i - 2, slot):
                c.wait()

        mask_rows = jnp.zeros((8, 256), F32)
        for two in range(2):
            at = slice(128 * two, 128 * two + 128)
            wide = pl.ds(pl.multiple_of(g * 256 + 128 * two, 128), 128)
            q = q_v[g, rows, at]
            for side in range(2):
                chosen = key_index(kinds, pairs_s, triples_s, h, t, 4 * g + 2 * two + side)
                here = jnp.logical_and(lane_head == 2 * two + side, key_block == chosen)
                mask_rows = jnp.where(here, 1.0, mask_rows)

            def pick(first):
                total = None
                for kb in range(4):
                    part = kv[first + BLOCK * kb : first + BLOCK * kb + BLOCK, wide] * mask_rows[kb : kb + 1, at].astype(BF)
                    total = part if total is None else total + part
                return total

            keys, values = pick(0), pick(WINDOW)
            ks_v[slot, :, at] = keys
            vs_v[slot, :, at] = values
            found = []
            for side in range(2):
                mask = left if side == 0 else jnp.logical_not(left)
                mask_keys = left_keys if side == 0 else jnp.logical_not(left_keys)
                scores = dot_nt(jnp.where(mask, q, jnp.zeros_like(q)), keys)
                top = jnp.max(scores, axis=-1, keepdims=True)
                raised = jnp.exp2((scores - top) * EXP2_SCALE).astype(BF)
                p_v[slot, 2 * two + side] = raised
                found.append(dot_nn(raised, jnp.where(mask_keys, values, jnp.ones_like(values))))
            result = jnp.where(left, found[0], found[1])
            total = jnp.where(left, found[1], found[0])
            inverse = 1.0 / pltpu.roll(total, 64, 1)
            att[rows, wide] = (result * inverse).astype(BF)
            inv[rows, wide] = inverse
        masks_o[t, :, pl.ds(pl.multiple_of(g * 256, 256), 256)] = mask_rows
        for c in stream(i, slot):
            c.start()

    for i in (7, 8):
        for c in stream(i, i % 2):
            c.wait()
    save_att = local(20, att, att_h)
    save_att.start()
    save_inv = local(31, inv, inv_h)
    save_inv.start()
    for c in loads:
        c.wait()

    def row(ref):
        return ref[...].reshape(1, -1)

    def slope(j, t):
        return pl.ds(pl.multiple_of(768 * j + t * TILE, TILE), TILE)

    def tile_saves(t):
        at = pl.ds(pl.multiple_of(t * TILE, TILE), TILE)
        parts = [(low, low_h), (rdel, rdel_h), (scaled_v, scaled_h), (out_v, out_h), (inverse_v, inverse_h)]
        parts = [(src.at[at], dst.at[at]) for src, dst in parts]
        parts.append((act.at[:, at], act_h.at[:, at]))
        parts += [(kv.at[slope(j, t)], slope_h.at[j, at]) for j in range(4)]
        return [local(21 + n, src, dst) for n, (src, dst) in enumerate(parts)]

    @pl.loop(0, 3)
    def _(t):
        at = pl.ds(pl.multiple_of(t * TILE, TILE), TILE)
        x = x_v[pl.ds(pl.multiple_of(own + t * TILE, TILE), TILE), :]
        mixed = dot_nn(att[at, :], mw[...]) + row(mb) + x.astype(F32)
        scaled_one, inverse_one = norm_parts(mixed)
        normed = scaled_one * row(g1) + row(s1)
        normed_low = normed.astype(BF)
        low[at, :] = normed_low
        scaled_v[at, :] = scaled_one.astype(BF)
        inverse_v[at, :] = jnp.broadcast_to(inverse_one, (TILE, 128))
        branch = row(rb) + normed
        for j in range(4):
            cols = slice(768 * j, 768 * j + 768)
            hidden = dot_nn(normed_low, ew[:, cols]) + row(eb)[:, cols]
            phi_sum, bell = normal_parts(hidden)
            active = (hidden * phi_sum).astype(BF)
            act[j, at, :] = active
            kv[slope(j, t), :] = (phi_sum + hidden * bell).astype(BF)
            branch += dot_nn(active, rw[cols, :])
        scaled_two, inverse_two = norm_parts(branch)
        out_v[at, :] = (scaled_two * row(g2) + row(s2)).astype(BF)
        upstream = cot[at, :].astype(F32)
        sums_o[4:5, :] += column_sum(upstream * scaled_two)
        sums_o[5:6, :] += column_sum(upstream)
        branch_delta = norm_back(upstream * row(g2), scaled_two, inverse_two)
        reduce_delta = branch_delta.astype(BF)
        rdel[at, :] = reduce_delta
        sums_o[3:4, :] += column_sum(reduce_delta.astype(F32))

        @pl.when(t > 0)
        def _():
            for c in tile_saves(t - 1):
                c.wait()

        for c in tile_saves(t):
            c.start()

    for c in tile_saves(2):
        c.wait()
    for c in (save_w, save_q, save_x, save_att, save_inv):
        c.wait()


def begin(*args):
    hb = pl.BlockSpec(memory_space=pl.ANY)
    vm = pl.BlockSpec(memory_space=pltpu.VMEM)
    sm = pl.BlockSpec(memory_space=pltpu.SMEM)
    qb, pairs, triples = args[4], args[6], args[7]
    rows = jax.ShapeDtypeStruct((ROWS, D), BF)
    rows_wide = jax.ShapeDtypeStruct((ROWS, D), F32)
    wide = jax.ShapeDtypeStruct((4, ROWS, D), BF)
    picked = jax.ShapeDtypeStruct((9, BLOCK, 256), BF)
    return pl.pallas_call(
        begin_kernel,
        out_shape=(
            jax.ShapeDtypeStruct((WINDOW, D), BF),
            jax.ShapeDtypeStruct((4, 3, SLOT, D), BF),
            jax.ShapeDtypeStruct((4,) + qb.shape, F32),
            jax.ShapeDtypeStruct((4,) + qb.shape, F32),
            jax.ShapeDtypeStruct((4,) + pairs.shape, jnp.int32),
            jax.ShapeDtypeStruct((4,) + triples.shape, jnp.int32),
            jax.ShapeDtypeStruct((9, 4, TILE, BLOCK), BF),
            picked,
            picked,
            jax.ShapeDtypeStruct((3, ROWS, 256), BF),
            rows,
            rows,
            rows,
            rows,
            rows,
            rows_wide,
            jax.ShapeDtypeStruct((ROWS, 128), F32),
            wide,
            wide,
            jax.ShapeDtypeStruct((3, 8, D), F32),
            jax.ShapeDtypeStruct((16, D), F32),
        ),
        in_specs=[hb] * 8 + [sm] + [hb] * 4 + [vm] * 7,
        out_specs=(hb,) * 19 + (vm, vm),
        scratch_shapes=[
            pltpu.VMEM((WINDOW, D), BF),
            pltpu.VMEM((4, 3, SLOT, D), BF),
            pltpu.VMEM((4,) + qb.shape, F32),
            pltpu.VMEM((4,) + qb.shape, F32),
            pltpu.SMEM((4,) + pairs.shape, jnp.int32),
            pltpu.SMEM((4,) + triples.shape, jnp.int32),
            pltpu.VMEM((2 * WINDOW, D), BF),
            pltpu.VMEM((3, ROWS, 256), BF),
            pltpu.VMEM((2, 4, TILE, BLOCK), BF),
            pltpu.VMEM((2, BLOCK, 256), BF),
            pltpu.VMEM((2, BLOCK, 256), BF),
            pltpu.VMEM((ROWS, D), BF),
            pltpu.VMEM((ROWS, D), F32),
            pltpu.VMEM((ROWS, D), BF),
            pltpu.VMEM((D, D), BF),
            pltpu.VMEM((D, FF), BF),
            pltpu.VMEM((FF, D), BF),
            pltpu.VMEM((4, ROWS, D), BF),
            pltpu.VMEM((ROWS, D), BF),
            pltpu.VMEM((ROWS, D), BF),
            pltpu.VMEM((ROWS, D), BF),
            pltpu.VMEM((ROWS, D), BF),
            pltpu.VMEM((ROWS, 128), F32),
            pltpu.SemaphoreType.DMA((32,)),
            pltpu.SemaphoreType.DMA((3, 2)),
            pltpu.SemaphoreType.DMA((60,)),
            pltpu.SemaphoreType.DMA((60,)),
        ],
        compiler_params=pltpu.CompilerParams(
            collective_id=0, has_side_effects=True, vmem_limit_bytes=63 * 2**20
        ),
        name="begin",
    )(*args)


def finish_kernel(
    nb, act_h, slope_h, low_h, rdel_h, att_h, scaled_h, p_h, ks_h, vs_h, q_h, inv_h, xw_h, wt_h, mw_h, ew_h, rw_h,
    inverse_one, g1, masks, sums_in,
    res_h, tg_o, sums_o, from_more,
    stage, from_core, from_a, from_b, from_z, res, dx_pair, dx_mid, vec, vec_in,
    wide_a, wide_b, four, pool, own, p_v, ks_v, vs_v, q_v, i_v, loc, flow, send, recv,
):
    b = lax.axis_index("batch")
    h = lax.axis_index("head")
    core, xb, yb = b % 2, (b // 2) % 2, (b // 4) % 2
    pc, px, py = flip(b, 1), flip(b, 2), flip(b, 4)
    hp, hm, hq = flip(h, 1), 3 - h, flip(h, 2)
    middle = jnp.logical_or(h == 1, h == 2)
    others = [(h + d) % 4 for d in (1, 2, 3)]
    more = []
    step = 8
    while step < nb:
        more.append(flip(b, step))
        step *= 2
    barrier = pltpu.get_barrier_semaphore()
    targets = [(pc, h), (px, h), (py, h)] + [(m, h) for m in more] + [(b, o) for o in others]
    for target in targets:
        pl.semaphore_signal(barrier, inc=1, device_id=target, device_id_type=MESH)

    def local(i, src, dst):
        return pltpu.make_async_copy(src, dst, loc.at[i])

    loads = [
        local(0, act_h, wide_a),
        local(1, rdel_h, four.at[1]),
        local(2, low_h, four.at[0]),
        local(3, slope_h, wide_b),
        local(4, att_h, four.at[2]),
        local(5, scaled_h, four.at[3]),
        local(6, mw_h, pool.at[4]),
    ]
    for c in loads[:2]:
        c.start()

    def get_weights(j):
        cols = pl.ds(768 * j, 768)
        return [
            local(16 + j, rw_h.at[cols], pool.at[j % 2]),
            local(20 + j, ew_h.at[:, cols], pool.at[2 + j % 2]),
        ]

    def make(i, src, dst, who, where):
        return remote(src, dst, send.at[i], recv.at[i], who, where)

    bits = ((xb, px, yb, py), (yb, py, xb, px))
    columns = (pl.ds(0, 384), pl.ds(384, 384))

    def rows_of(start, count):
        return pl.ds(pl.multiple_of(start, 16), count)

    def size(n, level):
        return (PIECES[n][2] // 8, PIECES[n][2] // 4, PIECES[n][2] // 2)[level]

    def place_start(n, part, level):
        start = PIECES[n][1] + core * size(n, 2)
        if level < 2:
            start = start + bits[part][0] * size(n, 1)
        if level < 1:
            start = start + bits[part][2] * size(n, 0)
        return start

    def place(n, part, level):
        return rows_of(place_start(n, part, level), size(n, level))

    def landing(n, level):
        return slice(PIECES[n][1] * size(n, level) // PIECES[n][2], (PIECES[n][1] + PIECES[n][2]) * size(n, level) // PIECES[n][2])

    def land(ref, n, level, cols):
        rows = landing(n, level)
        return ref.at[PIECES[n][0], :, pl.ds(rows.start, rows.stop - rows.start), cols]

    def core_copy(n):
        k, first, _ = PIECES[n]
        src = stage.at[k % 4, :, rows_of(first + (1 - core) * size(n, 2), size(n, 2))]
        return make(n, src, land(from_core, n, 2, slice(None)), pc, h)

    def a_copy(n, part):
        k, first, _ = PIECES[n]
        a_bit, who = bits[part][:2]
        rows = rows_of(first + core * size(n, 2) + (1 - a_bit) * size(n, 1), size(n, 1))
        return make(7 + 2 * n + part, stage.at[k % 4, :, rows, columns[part]], land(from_a, n, 1, columns[part]), who, h)

    def b_copy(n, part):
        k = PIECES[n][0]
        _, _, b_bit, who = bits[part]
        rows = rows_of(place_start(n, part, 1) + (1 - b_bit) * size(n, 0), size(n, 0))
        return make(21 + 2 * n + part, stage.at[k % 4, :, rows, columns[part]], land(from_b, n, 0, columns[part]), who, h)

    def z_copy(n, part, d):
        o = others[d - 1]
        k = PIECES[n][0]
        rows = landing(n, 0)
        dst = from_z.at[k, d - 1, pl.ds(rows.start, rows.stop - rows.start), columns[part]]
        return make(35 + 6 * n + 3 * part + d - 1, stage.at[k % 4, o, place(n, part, 0), columns[part]], dst, b, o)

    def gather_copy(n, part, level):
        ref = res.at[PIECES[n][0], place(n, part, level), columns[part]]
        return make(77 + 14 * level + 2 * n + part, ref, ref, bits[part][3 if level == 0 else 1], h)

    def last_copy(n):
        ref = res.at[PIECES[n][0], place(n, 0, 2)]
        return make(105 + n, ref, ref, pc, h)

    def more_copy(n, part, i):
        src = stage.at[PIECES[n][0] % 4, :, place(n, part, 0), columns[part]]
        dst = from_more.at[n, i, :, pl.ds(0, size(n, 0)), columns[part]]
        return make(122 + len(more) * (2 * n + part + 1) + i, src, dst, more[i], h)

    def out_copy(k):
        return local(8 + k, res.at[k], res_h.at[k])

    def add(n, part, level, other):
        k, block = PIECES[n][0] % 4, size(n, 0)
        start, first = place_start(n, part, level), landing(n, level).start
        cols = slice(0, D) if level == 2 else slice(384 * part, 384 * part + 384)

        @pl.loop(0, size(n, level) // block * 4)
        def _(i):
            z, at = i % 4, i // 4 * block
            mine = rows_of(start + at, block)
            stage[k, z, mine, cols] = stage[k, z, mine, cols] + other[PIECES[n][0], z, rows_of(first + at, block), cols]

    def stage_core(n):
        core_copy(n).wait()
        add(n, 0, 2, from_core)
        for part in range(2):
            a_copy(n, part).start()

    def stage_a(n):
        for part in range(2):
            a_copy(n, part).wait()
            add(n, part, 1, from_a)
            b_copy(n, part).start()

    def stage_b(n):
        for part in range(2):
            b_copy(n, part).wait()
            add(n, part, 0, from_b)
            for i in range(len(more)):
                more_copy(n, part, i).start()
                more_copy(n, part, i).wait()
                get = local(7, from_more.at[n, i, :, pl.ds(0, size(n, 0))], land(from_b, n, 0, slice(None)))
                get.start()
                get.wait()
                add(n, part, 0, from_b)
            for d in (2, 1, 3):
                z_copy(n, part, d).start()

    def stage_z(n):
        k, rows = PIECES[n][0], landing(n, 0)
        for part in range(2):
            cols = slice(384 * part, 384 * part + 384)
            total = stage[k % 4, h, place(n, part, 0), cols].astype(F32)
            for d in (1, 2, 3):
                z_copy(n, part, d).wait()
                total += from_z[k, d - 1, rows, cols].astype(F32)
            res[k, place(n, part, 0), cols] = total.astype(BF)
            gather_copy(n, part, 0).start()

    def stage_y(n):
        for part in range(2):
            gather_copy(n, part, 0).wait()
            gather_copy(n, part, 1).start()

    def stage_x(n):
        for part in range(2):
            gather_copy(n, part, 1).wait()
        last_copy(n).start()

    def stage_out(n):
        last_copy(n).wait()
        if n != len(PIECES) - 2:
            out_copy(PIECES[n][0]).start()

    vec_steps = [(pc, h), (px, h), (py, h)] + [(m, h) for m in more] + [(b, hp), (b, hq)]

    def vec_copy(i):
        return make(117 + i, vec, vec_in.at[i], *vec_steps[i])

    def stage_vec(i):
        vec_copy(i).wait()
        vec[...] += vec_in[i]
        if i + 1 < len(vec_steps):
            vec_copy(i + 1).start()

    stages = {
        "c": stage_core, "a": stage_a, "b": stage_b, "z": stage_z, "y": stage_y, "x": stage_x, "o": stage_out,
        "v": stage_vec,
    }

    def run(*items):
        for kind, k in items:
            stages[kind](k)

    def reduce_chunk(k, half):
        for z in range(4):
            grad = dot_tn(wide_a[z, :, 384 * half : 384 * half + 384], four[1])
            stage[k, z] = grad.astype(BF)

    def weight_grad(k, start, product):
        for half in range(2):
            grad = product(slice(384 * half, 384 * half + 384)).astype(BF)
            for z in range(2):
                stage[k, 2 * half + z, start : start + SLOT, :] = grad[SLOT * z : SLOT * z + SLOT, :]

    def to_keys(source, target):
        @pl.loop(0, 32)
        def _(i):
            rows = pl.ds(pl.multiple_of(i * 16, 16), 16)
            parts = [source[t, rows, :].astype(F32) for t in range(3)]
            for kb in range(4):
                total = parts[0] * masks[0, kb : kb + 1, :]
                for t in (1, 2):
                    total += parts[t] * masks[t, kb : kb + 1, :]
                target[kb, rows, :] = total.astype(BF)

    def fetch(i, slot):
        g, t = i // 3, i % 3
        tile = (pl.ds(pl.multiple_of(t * TILE, TILE), TILE), pl.ds(pl.multiple_of(g * 256, 256), 256))
        pairs = (
            (p_h.at[i], p_v), (ks_h.at[i], ks_v), (vs_h.at[i], vs_v), (q_h.at[g, tile[0]], q_v), (inv_h.at[tile], i_v),
        )
        return [pltpu.make_async_copy(src, dst.at[slot], flow.at[n, slot]) for n, (src, dst) in enumerate(pairs)]

    loads[0].wait()
    loads[1].wait()
    for c in get_weights(0) + loads[2:4] + get_weights(1) + loads[4:] + fetch(0, 0):
        c.start()
    vec[...] = sums_in[...]
    reduce_chunk(0, 0)
    pl.semaphore_wait(barrier, len(targets))
    core_copy(0).start()
    reduce_chunk(1, 1)
    core_copy(1).start()
    run(("c", 0),)
    loads[2].wait()
    loads[3].wait()

    between = {0: (("c", 1),), 2: (("a", 0),)}
    for j in range(4):
        for c in get_weights(j):
            c.wait()
        for t in range(3):
            rows = slice(TILE * t, TILE * t + TILE)
            back = dot_nt(four[1, rows, :], pool[j % 2]) * wide_b[j, rows, :].astype(F32)
            back = back.astype(BF)
            wide_b[j, rows, :] = back
            vec[6 + j : 7 + j, :] += column_sum(back.astype(F32))
            before = four[1, rows, :].astype(F32) if j == 0 else own[rows, :]
            own[rows, :] = before + dot_nt(back, pool[2 + j % 2])
        if j < 2:
            for c in get_weights(j + 2):
                c.start()
        for half in range(2):
            grad = dot_tn(four[0, :, 384 * half : 384 * half + 384], wide_b[j])
            stage[2 + half, j] = grad.astype(BF)
        run(*between.get(j, ()))
    core_copy(2).start()
    core_copy(3).start()

    for n in (4, 5, 6):
        loads[n].wait()
    for t in range(3):
        rows = slice(TILE * t, TILE * t + TILE)
        normed_delta = own[rows, :]
        scaled = four[3, rows, :].astype(F32)
        vec[1:2, :] += column_sum(normed_delta * scaled)
        vec[2:3, :] += column_sum(normed_delta)
        mixed_delta = norm_back(normed_delta * g1[...].reshape(1, D), scaled, inverse_one[rows, 0:1])
        own[rows, :] = mixed_delta
        mixer_delta = mixed_delta.astype(BF)
        four[3, rows, :] = mixer_delta
        vec[0:1, :] += column_sum(mixer_delta.astype(F32))
        four[0, rows, :] = dot_nt(mixer_delta, pool[4]).astype(BF)
    run(("a", 1), ("c", 2))

    left = left_lanes(TILE)
    plan = {0: (("c", 3),), 1: (("b", 0),), 3: (("b", 1),), 6: (("a", 2), ("z", 0)), 8: (("a", 3), ("z", 1))}

    @pl.loop(0, 9)
    def _(i):
        slot = i % 2
        g, t = i // 3, i % 3
        lanes = pl.multiple_of(g * 256, 256)

        @pl.when(i < 8)
        def _():
            for c in fetch(i + 1, 1 - slot):
                c.start()

        for c in fetch(i, slot):
            c.wait()
        for pair in range(2):
            at = slice(128 * pair, 128 * pair + 128)
            q = q_v[slot, :, at]
            tile = (0, pl.ds(pl.multiple_of(t * TILE, TILE), TILE), pl.ds(pl.multiple_of(lanes + 128 * pair, 128), 128))
            delta = (four[tile].astype(F32) * i_v[slot, :, at]).astype(BF)
            keys = ks_v[slot, :, at]
            values = vs_v[slot, :, at]
            prod = delta.astype(F32) * four[(2,) + tile[1:]].astype(F32)
            dq, dk, dv = [], [], []
            for side in range(2):
                mask = left if side == 0 else jnp.logical_not(left)
                inner = jnp.sum(jnp.where(mask, prod, 0.0), axis=-1, keepdims=True)
                delta_side = jnp.where(mask, delta, jnp.zeros_like(delta))
                probs = p_v[slot, 2 * pair + side]
                dp = dot_nt(delta_side, values)
                ds = (probs.astype(F32) * (dp - inner)).astype(BF)
                dv.append(dot_tn(probs, delta_side))
                dk.append(dot_tn(ds, jnp.where(mask, q, jnp.zeros_like(q))))
                dq.append(dot_nn(ds, keys))
            where = pl.ds(pl.multiple_of(lanes + 128 * pair, 128), 128)
            wide_a[t, 0:BLOCK, where] = ((dk[0] + dk[1]) * SCALE).astype(BF)
            wide_b[t, 0:BLOCK, where] = (dv[0] + dv[1]).astype(BF)
            wide_a[3, pl.ds(pl.multiple_of(t * TILE, TILE), TILE), where] = (
                jnp.where(left, dq[0], dq[1]) * SCALE
            ).astype(BF)
        for n, items in plan.items():

            @pl.when(i == n)
            def _():
                run(*items)

    to_keys(wide_b, pool)
    get_x = [local(16 + kb, xw_h.at[pl.ds(BLOCK * kb, BLOCK)], wide_b.at[kb, pl.ds(0, BLOCK)]) for kb in range(4)]
    own_at = own_offset(h)
    own_x = [
        local(
            32 + c,
            xw_h.at[pl.ds(pl.multiple_of(own_at + TILE * c, TILE), TILE)],
            wide_b.at[c, pl.ds(BLOCK, TILE)],
        )
        for c in range(3)
    ]
    for c in get_x + own_x:
        c.start()
    run(("b", 2), ("y", 0))
    weight_grad(0, 0, lambda at: dot_tn(four[2, :, at], four[3]))
    to_keys(wide_a, four)
    get_w = [
        local(20 + 4 * m + s, wt_h.at[s, m], wide_a.at[m, pl.ds(SLOT * s, SLOT)]) for m in range(3) for s in range(4)
    ]
    for c in get_w:
        c.start()
    for c in get_x:
        c.wait()

    def x_rows():
        return wide_b[:, 0:BLOCK, :].reshape(WINDOW, D)

    weight_grad(0, SLOT, lambda at: dot_tn(pool[0:4, 0:BLOCK, at].reshape(WINDOW, 384), x_rows()))
    core_copy(4).start()
    vec[10:11, :] = column_sum(wide_a[3].astype(F32))
    vec[11:12, :] = (
        column_sum(pool[0, 0:BLOCK, :].astype(F32))
        + column_sum(pool[1, 0:BLOCK, :].astype(F32))
        + column_sum(pool[2, 0:BLOCK, :].astype(F32))
        + column_sum(pool[3, 0:BLOCK, :].astype(F32))
    )
    vec_copy(0).start()
    run(("b", 3),)
    for c in get_w:
        c.wait()
    pair_at = own_offset(hp)
    mid_at = pl.multiple_of(1536 * (h % 2), 256)

    def row_part(start):
        kb, rows = start // BLOCK, pl.ds(pl.multiple_of(start % BLOCK, TILE), TILE)
        return dot_nn(four[kb, rows, :], wide_a[1]) + dot_nn(pool[kb, rows, :], wide_a[2])

    spare = pl.ds(BLOCK, TILE)

    def pair_copy(c):
        return make(112 + c, pool.at[c, spare], dx_pair.at[pl.ds(TILE * c, TILE)], b, hp)

    def mid_copy(c):
        return make(115 + c, pool.at[3 + c, spare], dx_mid.at[pl.ds(TILE * c, TILE)], b, hm)

    def pair_part(c):
        pool[c, BLOCK:, :] = row_part(pair_at + TILE * c).astype(BF)

    def mid_part(c):
        @pl.when(middle)
        def _():
            pool[3 + c, BLOCK:, :] = row_part(mid_at + TILE * c).astype(BF)

    def mid_start(c):
        @pl.when(middle)
        def _():
            mid_copy(c).start()

    def own_part(c):
        rows = slice(TILE * c, TILE * c + TILE)
        own[rows, :] += row_part(own_at + TILE * c) + dot_nn(wide_a[3, rows, :], wide_a[0])

    pair_part(0)
    pair_copy(0).start()
    mid_part(0)
    mid_start(0)
    run(("c", 4),)
    pair_part(1)
    pair_copy(1).start()
    mid_part(1)
    mid_start(1)
    weight_grad(1, 0, lambda at: dot_tn(four[:, 0:BLOCK, at].reshape(WINDOW, 384), x_rows()))
    for c in own_x:
        c.wait()
    weight_grad(1, SLOT, lambda at: dot_tn(wide_a[3, :, at], wide_b[0:3, BLOCK:, :].reshape(ROWS, D)))
    core_copy(5).start()
    core_copy(6).start()
    run(("x", 0), ("y", 1), ("v", 0))
    pair_part(2)
    run(("c", 5), ("c", 6), ("a", 4), ("v", 1), ("x", 1))
    own_part(0)
    run(("a", 5), ("a", 6), ("v", 2), ("z", 2))
    own_part(1)
    run(("v", 3), ("z", 3), ("y", 2))
    own_part(2)
    run(("b", 4), ("v", 4), ("o", 0), ("b", 5), ("b", 6))
    pair_copy(2).start()
    run(
        ("y", 3), ("x", 2), ("o", 1), ("z", 4), ("x", 3), ("o", 2), ("y", 4), ("z", 5), ("o", 3), ("x", 4), ("z", 6),
        ("y", 5), ("o", 4), ("y", 6), ("x", 5), ("x", 6), ("o", 5),
    )
    for i in range(5, len(vec_steps)):
        run(("v", i))
    sums_o[...] = vec[...]
    for c in range(3):
        pair_copy(c).wait()
        rows = slice(TILE * c, TILE * c + TILE)
        own[rows, :] += dx_pair[rows, :].astype(F32)

    @pl.when(middle)
    def _():
        for c in range(2):
            mid_copy(c).wait()
            rows = pl.ds(pl.multiple_of(256 * (h % 2) + TILE * c, TILE), TILE)
            own[rows, :] += dx_mid[TILE * c : TILE * c + TILE, :].astype(F32)

    tg_o[...] = own[...].astype(BF)
    run(("o", 6),)
    for k in range(CHUNKS):
        out_copy(k).wait()


def finish(nb, *args):
    hb = pl.BlockSpec(memory_space=pl.ANY)
    vm = pl.BlockSpec(memory_space=pltpu.VMEM)
    extra = max(0, nb.bit_length() - 4)
    count = 122 + extra * (2 * len(PIECES) + 1)
    return pl.pallas_call(
        functools.partial(finish_kernel, nb),
        out_shape=(
            jax.ShapeDtypeStruct((CHUNKS, 384, D), BF),
            jax.ShapeDtypeStruct((ROWS, D), BF),
            jax.ShapeDtypeStruct((16, D), F32),
            jax.ShapeDtypeStruct((len(PIECES), extra, 4, 48, D) if extra else (1, 1, 1, 16, 128), BF),
        ),
        in_specs=[hb] * 16 + [vm] * 4,
        out_specs=(hb, vm, vm, hb),
        scratch_shapes=[
            pltpu.VMEM((4, 4, 384, D), BF),
            pltpu.VMEM((CHUNKS, 4, 192, D), BF),
            pltpu.VMEM((CHUNKS, 4, 96, D), BF),
            pltpu.VMEM((CHUNKS, 4, 48, D), BF),
            pltpu.VMEM((CHUNKS, 3, 48, D), BF),
            pltpu.VMEM((CHUNKS, 384, D), BF),
            pltpu.VMEM((ROWS, D), BF),
            pltpu.VMEM((BLOCK, D), BF),
            pltpu.VMEM((16, D), F32),
            pltpu.VMEM((5 + extra, 16, D), F32),
            pltpu.VMEM((4, ROWS, D), BF),
            pltpu.VMEM((4, ROWS, D), BF),
            pltpu.VMEM((4, ROWS, D), BF),
            pltpu.VMEM((5, ROWS, D), BF),
            pltpu.VMEM((ROWS, D), F32),
            pltpu.VMEM((2, 4, TILE, BLOCK), BF),
            pltpu.VMEM((2, BLOCK, 256), BF),
            pltpu.VMEM((2, BLOCK, 256), BF),
            pltpu.VMEM((2, TILE, 256), BF),
            pltpu.VMEM((2, TILE, 256), F32),
            pltpu.SemaphoreType.DMA((35,)),
            pltpu.SemaphoreType.DMA((5, 2)),
            pltpu.SemaphoreType.DMA((count,)),
            pltpu.SemaphoreType.DMA((count,)),
        ],
        compiler_params=pltpu.CompilerParams(
            collective_id=1, has_side_effects=True, vmem_limit_bytes=63 * 2**20
        ),
        name="finish",
    )(*args)


def unpack_kernel(
    res, sums, reduce_h, expand_h, mixer_h, value_h, key_h, query_h, qbias_o, vbias_o, hidden_o, *rest
):
    vec_o, (low, full, sems) = rest[:6], rest[6:]
    h = lax.axis_index("head")
    gets = [pltpu.make_async_copy(res.at[k], low.at[k], sems.at[k]) for k in range(CHUNKS)]
    for c in gets:
        c.start()
    for n, ref in enumerate(vec_o):
        ref[...] = sums[n : n + 1, :].reshape(D)
    for j in range(4):
        hidden_o[D * j : D * j + D] = sums[6 + j : 7 + j, :].reshape(D)
    for n, ref in ((10, qbias_o), (11, vbias_o)):
        mine = sums[n : n + 1, 0:SLOT]
        for z in range(1, 4):
            mine = jnp.where(h == z, sums[n : n + 1, SLOT * z : SLOT * z + SLOT], mine)
        ref[...] = mine.reshape(SLOT)
    upper, lower = pl.ds(0, SLOT), pl.ds(SLOT, SLOT)
    targets = (
        (reduce_h.at[pl.ds(0, 384)],),
        (reduce_h.at[pl.ds(384, 384)],),
        (expand_h.at[pl.ds(0, 384)],),
        (expand_h.at[pl.ds(384, 384)],),
        (mixer_h, value_h),
        (key_h, query_h),
    )
    puts = []
    for k in range(CHUNKS):
        gets[k].wait()

        @pl.loop(0, 12)
        def _(i):
            rows = pl.ds(pl.multiple_of(i * 32, 32), 32)
            full[k, rows, :] = low[k, rows, :].astype(F32)

        views = (full.at[k],) if k < 4 else (full.at[k, upper], full.at[k, lower])
        for view, target in zip(views, targets[k]):
            c = pltpu.make_async_copy(view, target, sems.at[CHUNKS + len(puts)])
            c.start()
            puts.append(c)
    for c in puts:
        c.wait()


def unpack(res, sums):
    vm = pl.BlockSpec(memory_space=pltpu.VMEM)
    hb = pl.BlockSpec(memory_space=pl.ANY)
    square = jax.ShapeDtypeStruct((D, D), F32)
    strip = jax.ShapeDtypeStruct((SLOT, D), F32)
    short = jax.ShapeDtypeStruct((SLOT,), F32)
    row = jax.ShapeDtypeStruct((D,), F32)
    return pl.pallas_call(
        unpack_kernel,
        out_shape=(square, square, strip, strip, strip, strip, short, short, jax.ShapeDtypeStruct((FF,), F32)) + (row,) * 6,
        in_specs=[hb, vm],
        out_specs=(hb,) * 6 + (vm,) * 9,
        scratch_shapes=[
            pltpu.VMEM((CHUNKS, 384, D), BF),
            pltpu.VMEM((CHUNKS, 384, D), F32),
            pltpu.SemaphoreType.DMA((14,)),
        ],
        compiler_params=pltpu.CompilerParams(vmem_limit_bytes=VMEM_LIMIT),
        name="unpack",
    )(res, sums)


def layer(
    nb, tokens, query_weight, key_weight, value_weight, query_bias, value_bias, mixer_weight, mixer_bias,
    first_gain, first_shift, expand_weight, expand_bias, reduce_weight, reduce_bias, second_gain,
    second_shift, cotangent, group_kinds, pair_orders, triple_orders,
):
    (
        xw, wt, _, _, _, _, probs, keys, values, q, att, low, rdel, scaled, layer_output, inv, inverse, act, slope,
        masks, sums,
    ) = begin(
        tokens,
        query_weight.T,
        key_weight.T,
        value_weight.T,
        query_bias.reshape(1, -1),
        value_bias.reshape(1, -1),
        pair_orders.transpose(0, 2, 1),
        triple_orders.transpose(1, 0, 2),
        group_kinds,
        cotangent,
        mixer_weight,
        expand_weight,
        reduce_weight,
        mixer_bias,
        first_gain,
        first_shift,
        reduce_bias,
        second_gain,
        second_shift,
        expand_bias,
    )
    res, tokens_grad, sums, _ = finish(
        nb, act, slope, low, rdel, att, scaled, probs, keys, values, q, inv, xw, wt, mixer_weight, expand_weight,
        reduce_weight, inverse, first_gain, masks, sums,
    )
    out = unpack(res, sums)
    reduce_grad, expand_grad, mixer_grad, value_grad, key_grad, query_grad, query_sum, value_sum, hidden_sum = out[:9]
    mixer_sum, gain_one, shift_one, reduce_sum, gain_two, shift_two = out[9:]
    return (
        layer_output,
        tokens_grad,
        query_grad.T,
        key_grad.T,
        value_grad.T,
        query_sum,
        value_sum,
        mixer_grad,
        mixer_sum,
        gain_one,
        shift_one,
        expand_grad,
        hidden_sum,
        reduce_grad,
        reduce_sum,
        gain_two,
        shift_two,
    )


def solution(mesh):
    rows = P(("batch", "head"), None)
    return jax.shard_map(
        functools.partial(layer, mesh.shape["batch"]),
        mesh=mesh,
        in_specs=(
            rows,
            P(None, "head"),
            P(None, "head"),
            P(None, "head"),
            P("head"),
            P("head"),
            P(),
            P(),
            P(),
            P(),
            P(),
            P(),
            P(),
            P(),
            P(),
            P(),
            rows,
            P("batch"),
            P("batch", "head", None),
            P("batch", "head", None),
        ),
        out_specs=(
            rows,
            rows,
            P(None, "head"),
            P(None, "head"),
            P(None, "head"),
            P("head"),
            P("head"),
            P("head", None),
            P(),
            P(),
            P(),
            P(None, "head"),
            P(),
            P("head", None),
            P(),
            P(),
            P(),
        ),
        check_vma=False,
    )
```

```python
import functools
import math

import jax
import jax.numpy as jnp
from jax import lax
from jax.experimental import pallas as pl
from jax.experimental.pallas import tpu as pltpu
from jax.sharding import PartitionSpec as P

MESH = pl.DeviceIdType.MESH
BF = jnp.bfloat16
F32 = jnp.float32
VMEM_LIMIT = 60 * 2**20

D = 768
HEAD_SIZE = 64
BLOCK = 512
ROWS = 768
TILE = 256
WINDOW = 2048
SLOT = 192
FF = 3072
EPSILON = 1e-05
SCALE = 1.0 / math.sqrt(HEAD_SIZE)
EXP2_SCALE = SCALE * math.log2(math.e)
CHUNKS = 6
PIECES = ((0, 0, 384), (1, 0, 384), (2, 0, 384), (3, 0, 384), (4, 0, 384), (5, 0, 256), (5, 256, 128))


def dot_nn(a, b):
    return lax.dot_general(a, b, (((1,), (0,)), ((), ())), preferred_element_type=F32)


def dot_nt(a, b):
    return lax.dot_general(a, b, (((1,), (1,)), ((), ())), preferred_element_type=F32)


def dot_tn(a, b):
    return lax.dot_general(a, b, (((0,), (0,)), ((), ())), preferred_element_type=F32)


def remote(src, dst, send, recv, b, h):
    return pltpu.make_async_remote_copy(
        src_ref=src, dst_ref=dst, send_sem=send, recv_sem=recv, device_id=(b, h), device_id_type=MESH
    )


def flip(b, step):
    return b + step - 2 * step * ((b // step) % 2)


def own_offset(h):
    return pl.multiple_of(768 * h - 1024 * (h // 2), 256)


def key_index(kinds, pairs, triples, h, tile, head):
    block = (3 * h + tile) // 2
    slot, local = head // 3, head % 3
    pair_pick = 2 * (block // 2) + pairs[slot, block // 2, block % 2, local]
    triple_pick = 3 * (block // 3) + triples[slot, local, block // 3, block % 3]
    chosen = jnp.where(kinds[0] == 0, pair_pick, triple_pick)
    return chosen - 2 * (h // 2)


def left_lanes(rows):
    return lax.broadcasted_iota(jnp.int32, (rows, 128), 1) < 64


def normal_parts(v):
    bell = jnp.exp2(v * v * (-0.5 * math.log2(math.e)))
    t = 1.0 / (1.0 + (0.3275911 / math.sqrt(2.0)) * jnp.abs(v))
    poly = 0.5 * 1.061405429
    poly = poly * t + 0.5 * -1.453152027
    poly = poly * t + 0.5 * 1.421413741
    poly = poly * t + 0.5 * -0.284496736
    poly = poly * t + 0.5 * 0.254829592
    tail = poly * t * bell
    phi_sum = jnp.where(v >= 0, 1.0 - tail, tail)
    return phi_sum, bell * (1.0 / math.sqrt(2.0 * math.pi))


def norm_parts(values):
    center = values - jnp.mean(values, axis=-1, keepdims=True)
    inverse = lax.rsqrt(jnp.mean(center * center, axis=-1, keepdims=True) + EPSILON)
    return center * inverse, inverse


def norm_back(inner, scaled, inverse):
    inner_mean = jnp.mean(inner, axis=-1, keepdims=True)
    cross_mean = jnp.mean(inner * scaled, axis=-1, keepdims=True)
    return inverse * (inner - inner_mean - scaled * cross_mean)


def column_sum(values):
    return jnp.sum(values, axis=0, keepdims=True)


def begin_kernel(
    tok, wq, wk, wv, qb, vb, pairs, triples, kinds, cot_h, mw_h, ew_h, rw_h, mb, g1, s1, rb, g2, s2, eb,
    xw_h, wt_h, qbs, vbs, pairs_all, triples_all, p_h, ks_h, vs_h, q_h, att_h, low_h, rdel_h, scaled_h, out_h,
    inv_h, inverse_h, act_h, slope_h, masks_o, sums_o,
    x_v, w_v, qb_v, vb_v, pairs_s, triples_s, kv, q_v, p_v, ks_v, vs_v, att, inv, cot, mw, ew, rw, act,
    low, rdel, scaled_v, out_v, inverse_v, loc, flow, send, recv,
):
    b = lax.axis_index("batch")
    h = lax.axis_index("head")
    core = b % 2
    pc, px, py = flip(b, 1), flip(b, 2), flip(b, 4)
    hp = flip(h, 1)
    hm = 3 - h
    middle = jnp.logical_or(h == 1, h == 2)
    others = [(h + d) % 4 for d in (1, 2, 3)]
    barrier = pltpu.get_barrier_semaphore()
    for target in [(pc, h), (px, h), (py, h)] + [(b, o) for o in others]:
        pl.semaphore_signal(barrier, inc=1, device_id=target, device_id_type=MESH)

    def local(i, src, dst):
        return pltpu.make_async_copy(src, dst, loc.at[i])

    own = own_offset(h)
    rest = pl.multiple_of(1536 * (1 - h // 2), 256)
    small = ((qb, qbs), (vb, vbs), (pairs, pairs_all), (triples, triples_all))
    weights = (wq, wk, wv)
    kept = [local(0, tok, x_v.at[pl.ds(own, ROWS)])]
    kept += [local(1 + m, src, w_v.at[h, m]) for m, src in enumerate(weights)]
    kept += [local(4 + m, src, dst.at[h]) for m, (src, dst) in enumerate(small)]
    for c in kept:
        c.start()
    fill = local(8, tok.at[pl.ds(0, BLOCK)], x_v.at[pl.ds(rest, BLOCK)])

    @pl.when(jnp.logical_not(middle))
    def _():
        fill.start()

    pl.semaphore_wait(barrier, 6)

    def piece(who):
        return pl.ds(pl.multiple_of(((who // 2) % 4) * 48, 16), 48)

    lanes = pl.ds(pl.multiple_of(core * 384, 128), 384)
    sem = iter(range(128))

    def make(src, dst, who, where):
        i = next(sem)
        return remote(src, dst, send.at[i], recv.at[i], who, where)

    mine = piece(b)
    near = (1, 3, 2)
    over_z = {}
    for d in near:
        for m, src in enumerate(weights):
            c = make(src.at[mine, lanes], w_v.at[h, m, mine, lanes], b, others[d - 1])
            c.start()
            over_z[d, m] = c
    tables = []
    for src, dst in small:
        for d in near:
            c = make(src, dst.at[h], b, others[d - 1])
            c.start()
            tables.append(c)
    pair = [
        make(
            tok.at[pl.ds(TILE * c, TILE)], x_v.at[pl.ds(pl.multiple_of(own + TILE * c, TILE), TILE)], b, hp
        )
        for c in range(3)
    ]
    cross = make(
        tok.at[pl.ds(pl.multiple_of(256 * (h % 2), 256), BLOCK)],
        x_v.at[pl.ds(pl.multiple_of(1536 * ((h + 1) % 2), 256), BLOCK)],
        b,
        hm,
    )
    loads = [
        local(9 + i, src, dst)
        for i, (src, dst) in enumerate(((mw_h, mw), (ew_h, ew), (rw_h, rw), (cot_h, cot)))
    ]
    for c in loads:
        c.start()
    sums_o[...] = jnp.zeros_like(sums_o)

    def forward(d, m, rows, who):
        slot = (h + 4 - d) % 4
        ref = w_v.at[slot, m, rows, lanes]
        c = make(ref, ref, who, h)
        c.start()
        return c

    units = [(d, m) for d in near for m in range(3)]
    first = {}
    for i, (d, m) in enumerate(units):
        over_z[d, m].wait()
        first[d, m] = forward(d, m, mine, px if i % 2 == 0 else py)
        if i == 5:
            for c in pair:
                c.start()

            @pl.when(middle)
            def _():
                cross.start()

    second = {}
    for i, (d, m) in enumerate(units):
        first[d, m].wait()
        came, go = (px, py) if i % 2 == 0 else (py, px)
        second[d, m] = [forward(d, m, mine, go), forward(d, m, piece(came), go)]
    third = {}
    for d, m in units:
        for c in second[d, m]:
            c.wait()
        third[d, m] = forward(d, m, slice(None), pc)
    for c in tables:
        c.wait()
    for c in kept:
        c.wait()
    tables = [
        local(13 + i, src, dst)
        for i, (src, dst) in enumerate(((qbs, qb_v), (vbs, vb_v), (pairs_all, pairs_s), (triples_all, triples_s)))
    ]
    for c in tables:
        c.start()
    for c in third.values():
        c.wait()
    for c in tables:
        c.wait()

    save_w = local(17, w_v, wt_h)
    save_w.start()
    q_bias = jnp.concatenate([qb_v[s] for s in range(4)], axis=1)
    v_bias = jnp.concatenate([vb_v[s] for s in range(4)], axis=1)

    def keys_values(start, count):
        for c in range(count // TILE):
            rows = pl.ds(pl.multiple_of(start + c * TILE, TILE), TILE)
            x = x_v[rows, :]
            kv[rows, :] = dot_nt(x, w_v[:, 1].reshape(D, D)).astype(BF)
            more = pl.ds(pl.multiple_of(WINDOW + start + c * TILE, TILE), TILE)
            kv[more, :] = (dot_nt(x, w_v[:, 2].reshape(D, D)) + v_bias).astype(BF)

    for c in range(3):
        x = x_v[pl.ds(pl.multiple_of(own + c * TILE, TILE), TILE), :]
        q = (dot_nt(x, w_v[:, 0].reshape(D, D)) + q_bias).astype(BF)
        for s in range(3):
            q_v[s, TILE * c : TILE * c + TILE, :] = q[:, 256 * s : 256 * s + 256]
    save_q = local(18, q_v, q_h)
    save_q.start()
    keys_values(own, ROWS)

    @pl.when(middle)
    def _():
        cross.wait()

    @pl.when(jnp.logical_not(middle))
    def _():
        fill.wait()

    keys_values(rest, BLOCK)
    for c in range(3):
        pair[c].wait()
        keys_values(own_offset(hp) + TILE * c, TILE)
    save_x = local(19, x_v, xw_h)
    save_x.start()

    left = left_lanes(TILE)
    left_keys = left_lanes(BLOCK)
    lane_head = lax.broadcasted_iota(jnp.int32, (8, 256), 1) // 64
    key_block = lax.broadcasted_iota(jnp.int32, (8, 256), 0)

    def stream(i, slot):
        parts = ((p_v, p_h), (ks_v, ks_h), (vs_v, vs_h))
        return [pltpu.make_async_copy(src.at[slot], dst.at[i], flow.at[n, slot]) for n, (src, dst) in enumerate(parts)]

    @pl.loop(0, 9)
    def _(i):
        slot = i % 2
        g, t = i // 3, i % 3
        rows = pl.ds(pl.multiple_of(t * TILE, TILE), TILE)

        @pl.when(i >= 2)
        def _():
            for c in stream(i - 2, slot):
                c.wait()

        mask_rows = jnp.zeros((8, 256), F32)
        heads = []
        for two in range(2):
            at = slice(128 * two, 128 * two + 128)
            wide = pl.ds(pl.multiple_of(g * 256 + 128 * two, 128), 128)
            q = q_v[g, rows, at]
            for side in range(2):
                chosen = key_index(kinds, pairs_s, triples_s, h, t, 4 * g + 2 * two + side)
                here = jnp.logical_and(lane_head == 2 * two + side, key_block == chosen)
                mask_rows = jnp.where(here, 1.0, mask_rows)

            def pick(first):
                total = None
                for kb in range(4):
                    part = kv[first + BLOCK * kb : first + BLOCK * kb + BLOCK, wide] * mask_rows[kb : kb + 1, at].astype(BF)
                    total = part if total is None else total + part
                return total

            keys, values = pick(0), pick(WINDOW)
            ks_v[slot, :, at] = keys
            vs_v[slot, :, at] = values
            for side in range(2):
                mask = left if side == 0 else jnp.logical_not(left)
                mask_keys = left_keys if side == 0 else jnp.logical_not(left_keys)
                scores = dot_nt(jnp.where(mask, q, jnp.zeros_like(q)), keys)
                heads.append((scores, jnp.where(mask_keys, values, jnp.ones_like(values))))
        raised = []
        for n, (scores, _) in enumerate(heads):
            top = jnp.max(scores, axis=-1, keepdims=True)
            raised.append(jnp.exp2((scores - top) * EXP2_SCALE).astype(BF))
            p_v[slot, n] = raised[n]
        found = [dot_nn(raised[n], heads[n][1]) for n in range(4)]
        for two in range(2):
            wide = pl.ds(pl.multiple_of(g * 256 + 128 * two, 128), 128)
            result = jnp.where(left, found[2 * two], found[2 * two + 1])
            total = jnp.where(left, found[2 * two + 1], found[2 * two])
            inverse = 1.0 / pltpu.roll(total, 64, 1)
            att[rows, wide] = (result * inverse).astype(BF)
            inv[rows, wide] = inverse
        masks_o[t, :, pl.ds(pl.multiple_of(g * 256, 256), 256)] = mask_rows
        for c in stream(i, slot):
            c.start()

    for i in (7, 8):
        for c in stream(i, i % 2):
            c.wait()
    save_att = local(20, att, att_h)
    save_att.start()
    save_inv = local(31, inv, inv_h)
    save_inv.start()
    for c in loads:
        c.wait()

    def row(ref):
        return ref[...].reshape(1, -1)

    def slope(j, t):
        return pl.ds(pl.multiple_of(768 * j + t * TILE, TILE), TILE)

    def tile_saves(t):
        at = pl.ds(pl.multiple_of(t * TILE, TILE), TILE)
        parts = [(low, low_h), (rdel, rdel_h), (scaled_v, scaled_h), (out_v, out_h), (inverse_v, inverse_h)]
        parts = [(src.at[at], dst.at[at]) for src, dst in parts]
        parts.append((act.at[:, at], act_h.at[:, at]))
        parts += [(kv.at[slope(j, t)], slope_h.at[j, at]) for j in range(4)]
        return [local(21 + n, src, dst) for n, (src, dst) in enumerate(parts)]

    @pl.loop(0, 3)
    def _(t):
        at = pl.ds(pl.multiple_of(t * TILE, TILE), TILE)
        x = x_v[pl.ds(pl.multiple_of(own + t * TILE, TILE), TILE), :]
        mixed = dot_nn(att[at, :], mw[...]) + row(mb) + x.astype(F32)
        scaled_one, inverse_one = norm_parts(mixed)
        normed = scaled_one * row(g1) + row(s1)
        normed_low = normed.astype(BF)
        low[at, :] = normed_low
        scaled_v[at, :] = scaled_one.astype(BF)
        inverse_v[at, :] = jnp.broadcast_to(inverse_one, (TILE, 128))
        branch = row(rb) + normed
        for j in range(4):
            cols = slice(768 * j, 768 * j + 768)
            hidden = dot_nn(normed_low, ew[:, cols]) + row(eb)[:, cols]
            phi_sum, bell = normal_parts(hidden)
            active = (hidden * phi_sum).astype(BF)
            act[j, at, :] = active
            kv[slope(j, t), :] = (phi_sum + hidden * bell).astype(BF)
            branch += dot_nn(active, rw[cols, :])
        scaled_two, inverse_two = norm_parts(branch)
        out_v[at, :] = (scaled_two * row(g2) + row(s2)).astype(BF)
        upstream = cot[at, :].astype(F32)
        sums_o[4:5, :] += column_sum(upstream * scaled_two)
        sums_o[5:6, :] += column_sum(upstream)
        branch_delta = norm_back(upstream * row(g2), scaled_two, inverse_two)
        reduce_delta = branch_delta.astype(BF)
        rdel[at, :] = reduce_delta
        sums_o[3:4, :] += column_sum(reduce_delta.astype(F32))

        @pl.when(t > 0)
        def _():
            for c in tile_saves(t - 1):
                c.wait()

        for c in tile_saves(t):
            c.start()

    for c in tile_saves(2):
        c.wait()
    for c in (save_w, save_q, save_x, save_att, save_inv):
        c.wait()


def begin(*args):
    hb = pl.BlockSpec(memory_space=pl.ANY)
    vm = pl.BlockSpec(memory_space=pltpu.VMEM)
    sm = pl.BlockSpec(memory_space=pltpu.SMEM)
    qb, pairs, triples = args[4], args[6], args[7]
    rows = jax.ShapeDtypeStruct((ROWS, D), BF)
    rows_wide = jax.ShapeDtypeStruct((ROWS, D), F32)
    wide = jax.ShapeDtypeStruct((4, ROWS, D), BF)
    picked = jax.ShapeDtypeStruct((9, BLOCK, 256), BF)
    return pl.pallas_call(
        begin_kernel,
        out_shape=(
            jax.ShapeDtypeStruct((WINDOW, D), BF),
            jax.ShapeDtypeStruct((4, 3, SLOT, D), BF),
            jax.ShapeDtypeStruct((4,) + qb.shape, F32),
            jax.ShapeDtypeStruct((4,) + qb.shape, F32),
            jax.ShapeDtypeStruct((4,) + pairs.shape, jnp.int32),
            jax.ShapeDtypeStruct((4,) + triples.shape, jnp.int32),
            jax.ShapeDtypeStruct((9, 4, TILE, BLOCK), BF),
            picked,
            picked,
            jax.ShapeDtypeStruct((3, ROWS, 256), BF),
            rows,
            rows,
            rows,
            rows,
            rows,
            rows_wide,
            jax.ShapeDtypeStruct((ROWS, 128), F32),
            wide,
            wide,
            jax.ShapeDtypeStruct((3, 8, D), F32),
            jax.ShapeDtypeStruct((16, D), F32),
        ),
        in_specs=[hb] * 8 + [sm] + [hb] * 4 + [vm] * 7,
        out_specs=(hb,) * 19 + (vm, vm),
        scratch_shapes=[
            pltpu.VMEM((WINDOW, D), BF),
            pltpu.VMEM((4, 3, SLOT, D), BF),
            pltpu.VMEM((4,) + qb.shape, F32),
            pltpu.VMEM((4,) + qb.shape, F32),
            pltpu.SMEM((4,) + pairs.shape, jnp.int32),
            pltpu.SMEM((4,) + triples.shape, jnp.int32),
            pltpu.VMEM((2 * WINDOW, D), BF),
            pltpu.VMEM((3, ROWS, 256), BF),
            pltpu.VMEM((2, 4, TILE, BLOCK), BF),
            pltpu.VMEM((2, BLOCK, 256), BF),
            pltpu.VMEM((2, BLOCK, 256), BF),
            pltpu.VMEM((ROWS, D), BF),
            pltpu.VMEM((ROWS, D), F32),
            pltpu.VMEM((ROWS, D), BF),
            pltpu.VMEM((D, D), BF),
            pltpu.VMEM((D, FF), BF),
            pltpu.VMEM((FF, D), BF),
            pltpu.VMEM((4, ROWS, D), BF),
            pltpu.VMEM((ROWS, D), BF),
            pltpu.VMEM((ROWS, D), BF),
            pltpu.VMEM((ROWS, D), BF),
            pltpu.VMEM((ROWS, D), BF),
            pltpu.VMEM((ROWS, 128), F32),
            pltpu.SemaphoreType.DMA((32,)),
            pltpu.SemaphoreType.DMA((3, 2)),
            pltpu.SemaphoreType.DMA((61,)),
            pltpu.SemaphoreType.DMA((61,)),
        ],
        compiler_params=pltpu.CompilerParams(
            collective_id=0, has_side_effects=True, vmem_limit_bytes=63 * 2**20
        ),
        name="begin",
    )(*args)


def finish_kernel(
    nb, act_h, slope_h, low_h, rdel_h, att_h, scaled_h, p_h, ks_h, vs_h, q_h, inv_h, xw_h, wt_h, mw_h, ew_h, rw_h,
    inverse_one, g1, masks, sums_in,
    res_h, tg_o, sums_o, from_more,
    stage, from_core, from_a, from_b, from_z, res, dx_pair, dx_mid, vec, vec_in,
    wide_a, wide_b, four, pool, own, p_v, ks_v, vs_v, q_v, i_v, loc, flow, send, recv,
):
    b = lax.axis_index("batch")
    h = lax.axis_index("head")
    core, xb, yb = b % 2, (b // 2) % 2, (b // 4) % 2
    pc, px, py = flip(b, 1), flip(b, 2), flip(b, 4)
    hp, hm, hq = flip(h, 1), 3 - h, flip(h, 2)
    middle = jnp.logical_or(h == 1, h == 2)
    others = [(h + d) % 4 for d in (1, 2, 3)]
    more = []
    step = 8
    while step < nb:
        more.append(flip(b, step))
        step *= 2
    barrier = pltpu.get_barrier_semaphore()
    targets = [(pc, h), (px, h), (py, h)] + [(m, h) for m in more] + [(b, o) for o in others]
    for target in targets:
        pl.semaphore_signal(barrier, inc=1, device_id=target, device_id_type=MESH)

    def local(i, src, dst):
        return pltpu.make_async_copy(src, dst, loc.at[i])

    loads = [
        local(0, act_h, wide_a),
        local(1, rdel_h, four.at[1]),
        local(2, low_h, four.at[0]),
        local(3, slope_h, wide_b),
        local(4, att_h, four.at[2]),
        local(5, scaled_h, four.at[3]),
        local(6, mw_h, pool.at[4]),
    ]
    for c in loads[:2]:
        c.start()

    def get_weights(j):
        cols = pl.ds(768 * j, 768)
        return [
            local(16 + j, rw_h.at[cols], pool.at[j % 2]),
            local(20 + j, ew_h.at[:, cols], pool.at[2 + j % 2]),
        ]

    def make(i, src, dst, who, where):
        return remote(src, dst, send.at[i], recv.at[i], who, where)

    bits = ((xb, px, yb, py), (yb, py, xb, px))
    columns = (pl.ds(0, 384), pl.ds(384, 384))

    def rows_of(start, count):
        return pl.ds(pl.multiple_of(start, 16), count)

    def size(n, level):
        return (PIECES[n][2] // 8, PIECES[n][2] // 4, PIECES[n][2] // 2)[level]

    def place_start(n, part, level):
        start = PIECES[n][1] + core * size(n, 2)
        if level < 2:
            start = start + bits[part][0] * size(n, 1)
        if level < 1:
            start = start + bits[part][2] * size(n, 0)
        return start

    def place(n, part, level):
        return rows_of(place_start(n, part, level), size(n, level))

    def landing(n, level):
        return slice(PIECES[n][1] * size(n, level) // PIECES[n][2], (PIECES[n][1] + PIECES[n][2]) * size(n, level) // PIECES[n][2])

    def land(ref, n, level, cols):
        rows = landing(n, level)
        return ref.at[PIECES[n][0], :, pl.ds(rows.start, rows.stop - rows.start), cols]

    def core_copy(n):
        k, first, _ = PIECES[n]
        src = stage.at[k % 4, :, rows_of(first + (1 - core) * size(n, 2), size(n, 2))]
        return make(n, src, land(from_core, n, 2, slice(None)), pc, h)

    def a_copy(n, part):
        k, first, _ = PIECES[n]
        a_bit, who = bits[part][:2]
        rows = rows_of(first + core * size(n, 2) + (1 - a_bit) * size(n, 1), size(n, 1))
        return make(7 + 2 * n + part, stage.at[k % 4, :, rows, columns[part]], land(from_a, n, 1, columns[part]), who, h)

    def b_copy(n, part):
        k = PIECES[n][0]
        _, _, b_bit, who = bits[part]
        rows = rows_of(place_start(n, part, 1) + (1 - b_bit) * size(n, 0), size(n, 0))
        return make(21 + 2 * n + part, stage.at[k % 4, :, rows, columns[part]], land(from_b, n, 0, columns[part]), who, h)

    def z_copy(n, part, d):
        o = others[d - 1]
        k = PIECES[n][0]
        rows = landing(n, 0)
        dst = from_z.at[k, d - 1, pl.ds(rows.start, rows.stop - rows.start), columns[part]]
        return make(35 + 6 * n + 3 * part + d - 1, stage.at[k % 4, o, place(n, part, 0), columns[part]], dst, b, o)

    def gather_copy(n, part, level):
        ref = res.at[PIECES[n][0], place(n, part, level), columns[part]]
        return make(77 + 14 * level + 2 * n + part, ref, ref, bits[part][3 if level == 0 else 1], h)

    def last_copy(n):
        ref = res.at[PIECES[n][0], place(n, 0, 2)]
        return make(105 + n, ref, ref, pc, h)

    def more_copy(n, part, i):
        src = stage.at[PIECES[n][0] % 4, :, place(n, part, 0), columns[part]]
        dst = from_more.at[n, i, :, pl.ds(0, size(n, 0)), columns[part]]
        return make(122 + len(more) * (2 * n + part + 1) + i, src, dst, more[i], h)

    def out_copy(k):
        return local(8 + k, res.at[k], res_h.at[k])

    def add(n, part, level, other):
        k, block = PIECES[n][0] % 4, size(n, 0)
        start, first = place_start(n, part, level), landing(n, level).start
        cols = slice(0, D) if level == 2 else slice(384 * part, 384 * part + 384)

        @pl.loop(0, size(n, level) // block * 4)
        def _(i):
            z, at = i % 4, i // 4 * block
            mine = rows_of(start + at, block)
            stage[k, z, mine, cols] = stage[k, z, mine, cols] + other[PIECES[n][0], z, rows_of(first + at, block), cols]

    def stage_core(n):
        core_copy(n).wait()
        add(n, 0, 2, from_core)
        for part in range(2):
            a_copy(n, part).start()

    def stage_a(n):
        for part in range(2):
            a_copy(n, part).wait()
            add(n, part, 1, from_a)
            b_copy(n, part).start()

    def stage_b(n):
        for part in range(2):
            b_copy(n, part).wait()
            add(n, part, 0, from_b)
            for i in range(len(more)):
                more_copy(n, part, i).start()
                more_copy(n, part, i).wait()
                get = local(7, from_more.at[n, i, :, pl.ds(0, size(n, 0))], land(from_b, n, 0, slice(None)))
                get.start()
                get.wait()
                add(n, part, 0, from_b)
            for d in (2, 1, 3):
                z_copy(n, part, d).start()

    def stage_z(n):
        k, rows = PIECES[n][0], landing(n, 0)
        for part in range(2):
            cols = slice(384 * part, 384 * part + 384)
            total = stage[k % 4, h, place(n, part, 0), cols].astype(F32)
            for d in (1, 2, 3):
                z_copy(n, part, d).wait()
                total += from_z[k, d - 1, rows, cols].astype(F32)
            res[k, place(n, part, 0), cols] = total.astype(BF)
            gather_copy(n, part, 0).start()

    def stage_y(n):
        for part in range(2):
            gather_copy(n, part, 0).wait()
            gather_copy(n, part, 1).start()

    def stage_x(n):
        for part in range(2):
            gather_copy(n, part, 1).wait()
        last_copy(n).start()

    def stage_out(n):
        last_copy(n).wait()
        if n != len(PIECES) - 2:
            out_copy(PIECES[n][0]).start()

    vec_steps = [(pc, h), (px, h), (py, h)] + [(m, h) for m in more] + [(b, hp), (b, hq)]

    def vec_copy(i):
        return make(117 + i, vec, vec_in.at[i], *vec_steps[i])

    def stage_vec(i):
        vec_copy(i).wait()
        vec[...] += vec_in[i]
        if i + 1 < len(vec_steps):
            vec_copy(i + 1).start()

    stages = {
        "c": stage_core, "a": stage_a, "b": stage_b, "z": stage_z, "y": stage_y, "x": stage_x, "o": stage_out,
        "v": stage_vec,
    }

    def run(*items):
        for kind, k in items:
            stages[kind](k)

    def reduce_chunk(k, half):
        for z in range(4):
            grad = dot_tn(wide_a[z, :, 384 * half : 384 * half + 384], four[1])
            stage[k, z] = grad.astype(BF)

    def weight_grad(k, start, product):
        for half in range(2):
            grad = product(slice(384 * half, 384 * half + 384)).astype(BF)
            for z in range(2):
                stage[k, 2 * half + z, start : start + SLOT, :] = grad[SLOT * z : SLOT * z + SLOT, :]

    def to_keys(source, target):
        @pl.loop(0, 32)
        def _(i):
            rows = pl.ds(pl.multiple_of(i * 16, 16), 16)
            parts = [source[t, rows, :].astype(F32) for t in range(3)]
            for kb in range(4):
                total = parts[0] * masks[0, kb : kb + 1, :]
                for t in (1, 2):
                    total += parts[t] * masks[t, kb : kb + 1, :]
                target[kb, rows, :] = total.astype(BF)

    def fetch(i, slot):
        g, t = i // 3, i % 3
        tile = (pl.ds(pl.multiple_of(t * TILE, TILE), TILE), pl.ds(pl.multiple_of(g * 256, 256), 256))
        pairs = (
            (p_h.at[i], p_v), (ks_h.at[i], ks_v), (vs_h.at[i], vs_v), (q_h.at[g, tile[0]], q_v), (inv_h.at[tile], i_v),
        )
        return [pltpu.make_async_copy(src, dst.at[slot], flow.at[n, slot]) for n, (src, dst) in enumerate(pairs)]

    loads[0].wait()
    loads[1].wait()
    for c in get_weights(0) + loads[2:4] + get_weights(1) + loads[4:] + fetch(0, 0):
        c.start()
    vec[...] = sums_in[...]
    reduce_chunk(0, 0)
    pl.semaphore_wait(barrier, len(targets))
    core_copy(0).start()
    reduce_chunk(1, 1)
    core_copy(1).start()
    run(("c", 0),)
    loads[2].wait()
    loads[3].wait()

    between = {0: (("c", 1),), 2: (("a", 0),)}
    for j in range(4):
        for c in get_weights(j):
            c.wait()
        for t in range(3):
            rows = slice(TILE * t, TILE * t + TILE)
            back = dot_nt(four[1, rows, :], pool[j % 2]) * wide_b[j, rows, :].astype(F32)
            back = back.astype(BF)
            wide_b[j, rows, :] = back
            vec[6 + j : 7 + j, :] += column_sum(back.astype(F32))
            before = four[1, rows, :].astype(F32) if j == 0 else own[rows, :]
            own[rows, :] = before + dot_nt(back, pool[2 + j % 2])
        if j < 2:
            for c in get_weights(j + 2):
                c.start()
        for half in range(2):
            grad = dot_tn(four[0, :, 384 * half : 384 * half + 384], wide_b[j])
            stage[2 + half, j] = grad.astype(BF)
        run(*between.get(j, ()))
    core_copy(2).start()
    core_copy(3).start()

    for n in (4, 5, 6):
        loads[n].wait()
    for t in range(3):
        rows = slice(TILE * t, TILE * t + TILE)
        normed_delta = own[rows, :]
        scaled = four[3, rows, :].astype(F32)
        vec[1:2, :] += column_sum(normed_delta * scaled)
        vec[2:3, :] += column_sum(normed_delta)
        mixed_delta = norm_back(normed_delta * g1[...].reshape(1, D), scaled, inverse_one[rows, 0:1])
        own[rows, :] = mixed_delta
        mixer_delta = mixed_delta.astype(BF)
        four[3, rows, :] = mixer_delta
        vec[0:1, :] += column_sum(mixer_delta.astype(F32))
        four[0, rows, :] = dot_nt(mixer_delta, pool[4]).astype(BF)
    run(("a", 1), ("c", 2))

    left = left_lanes(TILE)
    plan = {0: (("c", 3),), 1: (("b", 0),), 3: (("b", 1),), 6: (("a", 2), ("z", 0)), 8: (("a", 3), ("z", 1))}

    @pl.loop(0, 9)
    def _(i):
        slot = i % 2
        g, t = i // 3, i % 3
        lanes = pl.multiple_of(g * 256, 256)

        @pl.when(i < 8)
        def _():
            for c in fetch(i + 1, 1 - slot):
                c.start()

        for c in fetch(i, slot):
            c.wait()
        heads = []
        for pair in range(2):
            at = slice(128 * pair, 128 * pair + 128)
            q = q_v[slot, :, at]
            tile = (0, pl.ds(pl.multiple_of(t * TILE, TILE), TILE), pl.ds(pl.multiple_of(lanes + 128 * pair, 128), 128))
            delta = (four[tile].astype(F32) * i_v[slot, :, at]).astype(BF)
            prod = delta.astype(F32) * four[(2,) + tile[1:]].astype(F32)
            for side in range(2):
                mask = left if side == 0 else jnp.logical_not(left)
                inner = jnp.sum(jnp.where(mask, prod, 0.0), axis=-1, keepdims=True)
                delta_side = jnp.where(mask, delta, jnp.zeros_like(delta))
                q_side = jnp.where(mask, q, jnp.zeros_like(q))
                heads.append((inner, delta_side, q_side, dot_nt(delta_side, vs_v[slot, :, at])))
        dv = [dot_tn(p_v[slot, n], heads[n][1]) for n in range(4)]
        ds = [(p_v[slot, n].astype(F32) * (heads[n][3] - heads[n][0])).astype(BF) for n in range(4)]
        for pair in range(2):
            at = slice(128 * pair, 128 * pair + 128)
            two = (2 * pair, 2 * pair + 1)
            dk = [dot_tn(ds[n], heads[n][2]) for n in two]
            dq = [dot_nn(ds[n], ks_v[slot, :, at]) for n in two]
            where = pl.ds(pl.multiple_of(lanes + 128 * pair, 128), 128)
            wide_a[t, 0:BLOCK, where] = ((dk[0] + dk[1]) * SCALE).astype(BF)
            wide_b[t, 0:BLOCK, where] = (dv[2 * pair] + dv[2 * pair + 1]).astype(BF)
            wide_a[3, pl.ds(pl.multiple_of(t * TILE, TILE), TILE), where] = (
                jnp.where(left, dq[0], dq[1]) * SCALE
            ).astype(BF)
        for n, items in plan.items():

            @pl.when(i == n)
            def _():
                run(*items)

    to_keys(wide_b, pool)
    get_x = [local(16 + kb, xw_h.at[pl.ds(BLOCK * kb, BLOCK)], wide_b.at[kb, pl.ds(0, BLOCK)]) for kb in range(4)]
    own_at = own_offset(h)
    own_x = [
        local(
            32 + c,
            xw_h.at[pl.ds(pl.multiple_of(own_at + TILE * c, TILE), TILE)],
            wide_b.at[c, pl.ds(BLOCK, TILE)],
        )
        for c in range(3)
    ]
    for c in get_x + own_x:
        c.start()
    run(("b", 2), ("y", 0))
    weight_grad(0, 0, lambda at: dot_tn(four[2, :, at], four[3]))
    to_keys(wide_a, four)
    get_w = [
        local(20 + 4 * m + s, wt_h.at[s, m], wide_a.at[m, pl.ds(SLOT * s, SLOT)]) for m in range(3) for s in range(4)
    ]
    for c in get_w:
        c.start()
    for c in get_x:
        c.wait()

    def x_rows():
        return wide_b[:, 0:BLOCK, :].reshape(WINDOW, D)

    weight_grad(0, SLOT, lambda at: dot_tn(pool[0:4, 0:BLOCK, at].reshape(WINDOW, 384), x_rows()))
    core_copy(4).start()
    vec[10:11, :] = column_sum(wide_a[3].astype(F32))
    vec[11:12, :] = (
        column_sum(pool[0, 0:BLOCK, :].astype(F32))
        + column_sum(pool[1, 0:BLOCK, :].astype(F32))
        + column_sum(pool[2, 0:BLOCK, :].astype(F32))
        + column_sum(pool[3, 0:BLOCK, :].astype(F32))
    )
    vec_copy(0).start()
    run(("b", 3),)
    for c in get_w:
        c.wait()
    pair_at = own_offset(hp)
    mid_at = pl.multiple_of(1536 * (h % 2), 256)

    def row_part(start):
        kb, rows = start // BLOCK, pl.ds(pl.multiple_of(start % BLOCK, TILE), TILE)
        return dot_nn(four[kb, rows, :], wide_a[1]) + dot_nn(pool[kb, rows, :], wide_a[2])

    spare = pl.ds(BLOCK, TILE)

    def pair_copy(c):
        return make(112 + c, pool.at[c, spare], dx_pair.at[pl.ds(TILE * c, TILE)], b, hp)

    def mid_copy(c):
        return make(115 + c, pool.at[3 + c, spare], dx_mid.at[pl.ds(TILE * c, TILE)], b, hm)

    def pair_part(c):
        pool[c, BLOCK:, :] = row_part(pair_at + TILE * c).astype(BF)

    def mid_part(c):
        @pl.when(middle)
        def _():
            pool[3 + c, BLOCK:, :] = row_part(mid_at + TILE * c).astype(BF)

    def mid_start(c):
        @pl.when(middle)
        def _():
            mid_copy(c).start()

    def own_part(c):
        rows = slice(TILE * c, TILE * c + TILE)
        own[rows, :] += row_part(own_at + TILE * c) + dot_nn(wide_a[3, rows, :], wide_a[0])

    pair_part(0)
    pair_copy(0).start()
    mid_part(0)
    mid_start(0)
    run(("c", 4),)
    pair_part(1)
    pair_copy(1).start()
    mid_part(1)
    mid_start(1)
    weight_grad(1, 0, lambda at: dot_tn(four[:, 0:BLOCK, at].reshape(WINDOW, 384), x_rows()))
    for c in own_x:
        c.wait()
    weight_grad(1, SLOT, lambda at: dot_tn(wide_a[3, :, at], wide_b[0:3, BLOCK:, :].reshape(ROWS, D)))
    core_copy(5).start()
    core_copy(6).start()
    run(("x", 0), ("y", 1), ("v", 0))
    pair_part(2)
    run(("c", 5), ("c", 6), ("a", 4), ("v", 1), ("x", 1))
    own_part(0)
    run(("a", 5), ("a", 6), ("v", 2), ("z", 2))
    own_part(1)
    run(("v", 3), ("z", 3), ("y", 2))
    own_part(2)
    run(("b", 4), ("v", 4), ("o", 0), ("b", 5), ("b", 6))
    pair_copy(2).start()
    run(
        ("y", 3), ("x", 2), ("o", 1), ("z", 4), ("x", 3), ("o", 2), ("y", 4), ("z", 5), ("o", 3), ("x", 4), ("z", 6),
        ("y", 5), ("o", 4), ("y", 6), ("x", 5), ("x", 6), ("o", 5),
    )
    for i in range(5, len(vec_steps)):
        run(("v", i))
    sums_o[...] = vec[...]
    for c in range(3):
        pair_copy(c).wait()
        rows = slice(TILE * c, TILE * c + TILE)
        own[rows, :] += dx_pair[rows, :].astype(F32)

    @pl.when(middle)
    def _():
        for c in range(2):
            mid_copy(c).wait()
            rows = pl.ds(pl.multiple_of(256 * (h % 2) + TILE * c, TILE), TILE)
            own[rows, :] += dx_mid[TILE * c : TILE * c + TILE, :].astype(F32)

    tg_o[...] = own[...].astype(BF)
    run(("o", 6),)
    for k in range(CHUNKS):
        out_copy(k).wait()


def finish(nb, *args):
    hb = pl.BlockSpec(memory_space=pl.ANY)
    vm = pl.BlockSpec(memory_space=pltpu.VMEM)
    extra = max(0, nb.bit_length() - 4)
    count = 122 + extra * (2 * len(PIECES) + 1)
    return pl.pallas_call(
        functools.partial(finish_kernel, nb),
        out_shape=(
            jax.ShapeDtypeStruct((CHUNKS, 384, D), BF),
            jax.ShapeDtypeStruct((ROWS, D), BF),
            jax.ShapeDtypeStruct((16, D), F32),
            jax.ShapeDtypeStruct((len(PIECES), extra, 4, 48, D) if extra else (1, 1, 1, 16, 128), BF),
        ),
        in_specs=[hb] * 16 + [vm] * 4,
        out_specs=(hb, vm, vm, hb),
        scratch_shapes=[
            pltpu.VMEM((4, 4, 384, D), BF),
            pltpu.VMEM((CHUNKS, 4, 192, D), BF),
            pltpu.VMEM((CHUNKS, 4, 96, D), BF),
            pltpu.VMEM((CHUNKS, 4, 48, D), BF),
            pltpu.VMEM((CHUNKS, 3, 48, D), BF),
            pltpu.VMEM((CHUNKS, 384, D), BF),
            pltpu.VMEM((ROWS, D), BF),
            pltpu.VMEM((BLOCK, D), BF),
            pltpu.VMEM((16, D), F32),
            pltpu.VMEM((5 + extra, 16, D), F32),
            pltpu.VMEM((4, ROWS, D), BF),
            pltpu.VMEM((4, ROWS, D), BF),
            pltpu.VMEM((4, ROWS, D), BF),
            pltpu.VMEM((5, ROWS, D), BF),
            pltpu.VMEM((ROWS, D), F32),
            pltpu.VMEM((2, 4, TILE, BLOCK), BF),
            pltpu.VMEM((2, BLOCK, 256), BF),
            pltpu.VMEM((2, BLOCK, 256), BF),
            pltpu.VMEM((2, TILE, 256), BF),
            pltpu.VMEM((2, TILE, 256), F32),
            pltpu.SemaphoreType.DMA((35,)),
            pltpu.SemaphoreType.DMA((5, 2)),
            pltpu.SemaphoreType.DMA((count,)),
            pltpu.SemaphoreType.DMA((count,)),
        ],
        compiler_params=pltpu.CompilerParams(
            collective_id=1, has_side_effects=True, vmem_limit_bytes=63 * 2**20
        ),
        name="finish",
    )(*args)


def unpack_kernel(
    res, sums, reduce_h, expand_h, mixer_h, value_h, key_h, query_h, qbias_o, vbias_o, hidden_o, *rest
):
    vec_o, (low, full, sems) = rest[:6], rest[6:]
    h = lax.axis_index("head")
    gets = [pltpu.make_async_copy(res.at[k], low.at[k], sems.at[k]) for k in range(CHUNKS)]
    for c in gets:
        c.start()
    for n, ref in enumerate(vec_o):
        ref[...] = sums[n : n + 1, :].reshape(D)
    for j in range(4):
        hidden_o[D * j : D * j + D] = sums[6 + j : 7 + j, :].reshape(D)
    for n, ref in ((10, qbias_o), (11, vbias_o)):
        mine = sums[n : n + 1, 0:SLOT]
        for z in range(1, 4):
            mine = jnp.where(h == z, sums[n : n + 1, SLOT * z : SLOT * z + SLOT], mine)
        ref[...] = mine.reshape(SLOT)
    upper, lower = pl.ds(0, SLOT), pl.ds(SLOT, SLOT)
    targets = (
        (reduce_h.at[pl.ds(0, 384)],),
        (reduce_h.at[pl.ds(384, 384)],),
        (expand_h.at[pl.ds(0, 384)],),
        (expand_h.at[pl.ds(384, 384)],),
        (mixer_h, value_h),
        (key_h, query_h),
    )
    puts = []
    for k in range(CHUNKS):
        gets[k].wait()

        @pl.loop(0, 12)
        def _(i):
            rows = pl.ds(pl.multiple_of(i * 32, 32), 32)
            full[k, rows, :] = low[k, rows, :].astype(F32)

        views = (full.at[k],) if k < 4 else (full.at[k, upper], full.at[k, lower])
        for view, target in zip(views, targets[k]):
            c = pltpu.make_async_copy(view, target, sems.at[CHUNKS + len(puts)])
            c.start()
            puts.append(c)
    for c in puts:
        c.wait()


def unpack(res, sums):
    vm = pl.BlockSpec(memory_space=pltpu.VMEM)
    hb = pl.BlockSpec(memory_space=pl.ANY)
    square = jax.ShapeDtypeStruct((D, D), F32)
    strip = jax.ShapeDtypeStruct((SLOT, D), F32)
    short = jax.ShapeDtypeStruct((SLOT,), F32)
    row = jax.ShapeDtypeStruct((D,), F32)
    return pl.pallas_call(
        unpack_kernel,
        out_shape=(square, square, strip, strip, strip, strip, short, short, jax.ShapeDtypeStruct((FF,), F32)) + (row,) * 6,
        in_specs=[hb, vm],
        out_specs=(hb,) * 6 + (vm,) * 9,
        scratch_shapes=[
            pltpu.VMEM((CHUNKS, 384, D), BF),
            pltpu.VMEM((CHUNKS, 384, D), F32),
            pltpu.SemaphoreType.DMA((14,)),
        ],
        compiler_params=pltpu.CompilerParams(vmem_limit_bytes=VMEM_LIMIT),
        name="unpack",
    )(res, sums)


def layer(
    nb, tokens, query_weight, key_weight, value_weight, query_bias, value_bias, mixer_weight, mixer_bias,
    first_gain, first_shift, expand_weight, expand_bias, reduce_weight, reduce_bias, second_gain,
    second_shift, cotangent, group_kinds, pair_orders, triple_orders,
):
    (
        xw, wt, _, _, _, _, probs, keys, values, q, att, low, rdel, scaled, layer_output, inv, inverse, act, slope,
        masks, sums,
    ) = begin(
        tokens,
        query_weight.T,
        key_weight.T,
        value_weight.T,
        query_bias.reshape(1, -1),
        value_bias.reshape(1, -1),
        pair_orders.transpose(0, 2, 1),
        triple_orders.transpose(1, 0, 2),
        group_kinds,
        cotangent,
        mixer_weight,
        expand_weight,
        reduce_weight,
        mixer_bias,
        first_gain,
        first_shift,
        reduce_bias,
        second_gain,
        second_shift,
        expand_bias,
    )
    res, tokens_grad, sums, _ = finish(
        nb, act, slope, low, rdel, att, scaled, probs, keys, values, q, inv, xw, wt, mixer_weight, expand_weight,
        reduce_weight, inverse, first_gain, masks, sums,
    )
    out = unpack(res, sums)
    reduce_grad, expand_grad, mixer_grad, value_grad, key_grad, query_grad, query_sum, value_sum, hidden_sum = out[:9]
    mixer_sum, gain_one, shift_one, reduce_sum, gain_two, shift_two = out[9:]
    return (
        layer_output,
        tokens_grad,
        query_grad.T,
        key_grad.T,
        value_grad.T,
        query_sum,
        value_sum,
        mixer_grad,
        mixer_sum,
        gain_one,
        shift_one,
        expand_grad,
        hidden_sum,
        reduce_grad,
        reduce_sum,
        gain_two,
        shift_two,
    )


def solution(mesh):
    rows = P(("batch", "head"), None)
    return jax.shard_map(
        functools.partial(layer, mesh.shape["batch"]),
        mesh=mesh,
        in_specs=(
            rows,
            P(None, "head"),
            P(None, "head"),
            P(None, "head"),
            P("head"),
            P("head"),
            P(),
            P(),
            P(),
            P(),
            P(),
            P(),
            P(),
            P(),
            P(),
            P(),
            rows,
            P("batch"),
            P("batch", "head", None),
            P("batch", "head", None),
        ),
        out_specs=(
            rows,
            rows,
            P(None, "head"),
            P(None, "head"),
            P(None, "head"),
            P("head"),
            P("head"),
            P("head", None),
            P(),
            P(),
            P(),
            P(None, "head"),
            P(),
            P("head", None),
            P(),
            P(),
            P(),
        ),
        check_vma=False,
    )
```

```python
import functools
import math

import jax
import jax.numpy as jnp
from jax import lax
from jax.experimental import pallas as pl
from jax.experimental.pallas import tpu as pltpu
from jax.sharding import PartitionSpec as P

MESH = pl.DeviceIdType.MESH
BF = jnp.bfloat16
F32 = jnp.float32
VMEM_LIMIT = 60 * 2**20

D = 768
HEAD_SIZE = 64
BLOCK = 512
ROWS = 768
TILE = 256
WINDOW = 2048
SLOT = 192
FF = 3072
EPSILON = 1e-05
SCALE = 1.0 / math.sqrt(HEAD_SIZE)
EXP2_SCALE = SCALE * math.log2(math.e)
CHUNKS = 6
PIECES = ((0, 0, 384), (1, 0, 384), (2, 0, 384), (3, 0, 384), (4, 0, 384), (5, 0, 256), (5, 256, 128))


BEFORE = (
    ("R", 0), ("core", 0), ("R", 1), ("J", 0), ("core", 1), ("c", 0), ("J", 1), ("c", 1), ("J", 2), ("J", 3),
    ("core", 2), ("a", 0), ("LN", 0), ("c", 2), ("core", 3), ("a", 1),
)
DURING = {
    1: (
        ("b", 0),
    ),
    4: (
        ("a", 2),
    ),
    5: (
        ("z", 0), ("b", 1), ("c", 3),
    ),
    7: (
        ("b", 2),
    ),
}
AFTER = (
    ("M", 0), ("kv", 0), ("kk", 0), ("pp", 0), ("P", 0), ("a", 3), ("V", 0), ("core", 4), ("z", 1), ("y", 0),
    ("mm", 0), ("Q", 0), ("pp", 1), ("P", 1), ("c", 4), ("Mx", 0), ("b", 3), ("K", 0), ("core", 5), ("c", 5),
    ("x", 0), ("a", 4), ("sums", 0), ("ow", 0), ("z", 2), ("core", 6), ("v0", 0), ("mm", 1), ("ow", 1), ("ow", 2),
    ("a", 5), ("c", 6), ("b", 4), ("z", 3), ("y", 1), ("y", 2), ("b", 5), ("pp", 2), ("a", 6), ("o", 0), ("z", 4),
    ("b", 6), ("v", 0), ("y", 4), ("Mx", 1), ("P", 2), ("z", 5), ("y", 3), ("z", 6), ("x", 2), ("y", 5), ("dp", 0),
    ("v", 1), ("x", 1), ("o", 2), ("x", 4), ("y", 6), ("x", 3), ("v", 2), ("v", 3), ("x", 6), ("x", 5), ("dp", 1),
    ("v", 4), ("o", 6), ("o", 5), ("o", 1), ("o", 3), ("o", 4), ("dp", 2), ("dm", 0), ("dm", 1), ("fin", 0),
    ("end", 0),
)


def dot_nn(a, b):
    return lax.dot_general(a, b, (((1,), (0,)), ((), ())), preferred_element_type=F32)


def dot_nt(a, b):
    return lax.dot_general(a, b, (((1,), (1,)), ((), ())), preferred_element_type=F32)


def dot_tn(a, b):
    return lax.dot_general(a, b, (((0,), (0,)), ((), ())), preferred_element_type=F32)


def remote(src, dst, send, recv, b, h):
    return pltpu.make_async_remote_copy(
        src_ref=src, dst_ref=dst, send_sem=send, recv_sem=recv, device_id=(b, h), device_id_type=MESH
    )


def flip(b, step):
    return b + step - 2 * step * ((b // step) % 2)


def own_offset(h):
    return pl.multiple_of(768 * h - 1024 * (h // 2), 256)


def key_index(kinds, pairs, triples, h, tile, head):
    block = (3 * h + tile) // 2
    slot, local = head // 3, head % 3
    pair_pick = 2 * (block // 2) + pairs[slot, block // 2, block % 2, local]
    triple_pick = 3 * (block // 3) + triples[slot, local, block // 3, block % 3]
    chosen = jnp.where(kinds[0] == 0, pair_pick, triple_pick)
    return chosen - 2 * (h // 2)


def left_lanes(rows):
    return lax.broadcasted_iota(jnp.int32, (rows, 128), 1) < 64


def normal_parts(v):
    bell = jnp.exp2(v * v * (-0.5 * math.log2(math.e)))
    t = 1.0 / (1.0 + (0.3275911 / math.sqrt(2.0)) * jnp.abs(v))
    poly = 0.5 * 1.061405429
    poly = poly * t + 0.5 * -1.453152027
    poly = poly * t + 0.5 * 1.421413741
    poly = poly * t + 0.5 * -0.284496736
    poly = poly * t + 0.5 * 0.254829592
    tail = poly * t * bell
    phi_sum = jnp.where(v >= 0, 1.0 - tail, tail)
    return phi_sum, bell * (1.0 / math.sqrt(2.0 * math.pi))


def norm_parts(values):
    center = values - jnp.mean(values, axis=-1, keepdims=True)
    inverse = lax.rsqrt(jnp.mean(center * center, axis=-1, keepdims=True) + EPSILON)
    return center * inverse, inverse


def norm_back(inner, scaled, inverse):
    inner_mean = jnp.mean(inner, axis=-1, keepdims=True)
    cross_mean = jnp.mean(inner * scaled, axis=-1, keepdims=True)
    return inverse * (inner - inner_mean - scaled * cross_mean)


def column_sum(values):
    return jnp.sum(values, axis=0, keepdims=True)


def begin_kernel(
    tok, wq, wk, wv, qb, vb, pairs, triples, kinds, cot_h, mw_h, ew_h, rw_h, mb, g1, s1, rb, g2, s2, eb,
    xw_h, wt_h, qbs, vbs, pairs_all, triples_all, p_h, ks_h, vs_h, q_h, att_h, low_h, rdel_h, scaled_h, out_h,
    inv_h, inverse_h, act_h, slope_h, masks_o, sums_o,
    x_v, w_v, qb_v, vb_v, pairs_s, triples_s, kv, q_v, p_v, ks_v, vs_v, att, inv, cot, mw, ew, rw, act,
    low, rdel, scaled_v, out_v, inverse_v, loc, flow, send, recv,
):
    b = lax.axis_index("batch")
    h = lax.axis_index("head")
    core = b % 2
    pc, px, py = flip(b, 1), flip(b, 2), flip(b, 4)
    hp = flip(h, 1)
    hm = 3 - h
    middle = jnp.logical_or(h == 1, h == 2)
    others = [(h + d) % 4 for d in (1, 2, 3)]
    barrier = pltpu.get_barrier_semaphore()
    for target in [(pc, h), (px, h), (py, h)] + [(b, o) for o in others]:
        pl.semaphore_signal(barrier, inc=1, device_id=target, device_id_type=MESH)

    def local(i, src, dst):
        return pltpu.make_async_copy(src, dst, loc.at[i])

    own = own_offset(h)
    rest = pl.multiple_of(1536 * (1 - h // 2), 256)
    small = ((qb, qbs), (vb, vbs), (pairs, pairs_all), (triples, triples_all))
    weights = (wq, wk, wv)
    kept = [local(0, tok, x_v.at[pl.ds(own, ROWS)])]
    kept += [local(1 + m, src, w_v.at[h, m]) for m, src in enumerate(weights)]
    kept += [local(4 + m, src, dst.at[h]) for m, (src, dst) in enumerate(small)]
    for c in kept:
        c.start()
    fill = local(8, tok.at[pl.ds(0, BLOCK)], x_v.at[pl.ds(rest, BLOCK)])

    @pl.when(jnp.logical_not(middle))
    def _():
        fill.start()

    pl.semaphore_wait(barrier, 6)

    def piece(who):
        return pl.ds(pl.multiple_of(((who // 2) % 4) * 48, 16), 48)

    lanes = pl.ds(pl.multiple_of(core * 384, 128), 384)
    sem = iter(range(128))

    def make(src, dst, who, where):
        i = next(sem)
        return remote(src, dst, send.at[i], recv.at[i], who, where)

    mine = piece(b)
    near = (1, 3, 2)
    over_z = {}
    for d in near:
        for m, src in enumerate(weights):
            c = make(src.at[mine, lanes], w_v.at[h, m, mine, lanes], b, others[d - 1])
            c.start()
            over_z[d, m] = c
    tables = []
    for src, dst in small:
        for d in near:
            c = make(src, dst.at[h], b, others[d - 1])
            c.start()
            tables.append(c)
    pair = [
        make(
            tok.at[pl.ds(TILE * c, TILE)], x_v.at[pl.ds(pl.multiple_of(own + TILE * c, TILE), TILE)], b, hp
        )
        for c in range(3)
    ]
    cross = make(
        tok.at[pl.ds(pl.multiple_of(256 * (h % 2), 256), BLOCK)],
        x_v.at[pl.ds(pl.multiple_of(1536 * ((h + 1) % 2), 256), BLOCK)],
        b,
        hm,
    )
    loads = [
        local(9 + i, src, dst)
        for i, (src, dst) in enumerate(((mw_h, mw), (ew_h, ew), (rw_h, rw), (cot_h, cot)))
    ]
    for c in loads:
        c.start()
    sums_o[...] = jnp.zeros_like(sums_o)

    def forward(d, m, rows, who):
        slot = (h + 4 - d) % 4
        ref = w_v.at[slot, m, rows, lanes]
        c = make(ref, ref, who, h)
        c.start()
        return c

    units = [(d, m) for d in near for m in range(3)]
    first = {}
    for i, (d, m) in enumerate(units):
        over_z[d, m].wait()
        first[d, m] = forward(d, m, mine, px if i % 2 == 0 else py)
        if i == 5:
            for c in pair:
                c.start()

            @pl.when(middle)
            def _():
                cross.start()

    second = {}
    for i, (d, m) in enumerate(units):
        first[d, m].wait()
        came, go = (px, py) if i % 2 == 0 else (py, px)
        second[d, m] = [forward(d, m, mine, go), forward(d, m, piece(came), go)]
    third = {}
    for d, m in units:
        for c in second[d, m]:
            c.wait()
        third[d, m] = forward(d, m, slice(None), pc)
    for c in tables:
        c.wait()
    for c in kept:
        c.wait()
    tables = [
        local(13 + i, src, dst)
        for i, (src, dst) in enumerate(((qbs, qb_v), (vbs, vb_v), (pairs_all, pairs_s), (triples_all, triples_s)))
    ]
    for c in tables:
        c.start()
    for c in third.values():
        c.wait()
    for c in tables:
        c.wait()

    save_w = local(17, w_v, wt_h)
    save_w.start()
    q_bias = jnp.concatenate([qb_v[s] for s in range(4)], axis=1)
    v_bias = jnp.concatenate([vb_v[s] for s in range(4)], axis=1)

    def keys_values(start, count):
        for c in range(count // TILE):
            rows = pl.ds(pl.multiple_of(start + c * TILE, TILE), TILE)
            x = x_v[rows, :]
            kv[rows, :] = dot_nt(x, w_v[:, 1].reshape(D, D)).astype(BF)
            more = pl.ds(pl.multiple_of(WINDOW + start + c * TILE, TILE), TILE)
            kv[more, :] = (dot_nt(x, w_v[:, 2].reshape(D, D)) + v_bias).astype(BF)

    for c in range(3):
        x = x_v[pl.ds(pl.multiple_of(own + c * TILE, TILE), TILE), :]
        q = (dot_nt(x, w_v[:, 0].reshape(D, D)) + q_bias).astype(BF)
        for s in range(3):
            q_v[s, TILE * c : TILE * c + TILE, :] = q[:, 256 * s : 256 * s + 256]
    save_q = local(18, q_v, q_h)
    save_q.start()
    keys_values(own, ROWS)

    @pl.when(middle)
    def _():
        cross.wait()

    @pl.when(jnp.logical_not(middle))
    def _():
        fill.wait()

    keys_values(rest, BLOCK)
    for c in range(3):
        pair[c].wait()
        keys_values(own_offset(hp) + TILE * c, TILE)
    save_x = local(19, x_v, xw_h)
    save_x.start()

    left = left_lanes(TILE)
    left_keys = left_lanes(BLOCK)
    lane_head = lax.broadcasted_iota(jnp.int32, (8, 256), 1) // 64
    key_block = lax.broadcasted_iota(jnp.int32, (8, 256), 0)

    def stream(i, slot):
        parts = ((p_v, p_h), (ks_v, ks_h), (vs_v, vs_h))
        return [pltpu.make_async_copy(src.at[slot], dst.at[i], flow.at[n, slot]) for n, (src, dst) in enumerate(parts)]

    @pl.loop(0, 9)
    def _(i):
        slot = i % 2
        g, t = i // 3, i % 3
        rows = pl.ds(pl.multiple_of(t * TILE, TILE), TILE)

        @pl.when(i >= 2)
        def _():
            for c in stream(i - 2, slot):
                c.wait()

        mask_rows = jnp.zeros((8, 256), F32)
        heads = []
        for two in range(2):
            at = slice(128 * two, 128 * two + 128)
            wide = pl.ds(pl.multiple_of(g * 256 + 128 * two, 128), 128)
            q = q_v[g, rows, at]
            for side in range(2):
                chosen = key_index(kinds, pairs_s, triples_s, h, t, 4 * g + 2 * two + side)
                here = jnp.logical_and(lane_head == 2 * two + side, key_block == chosen)
                mask_rows = jnp.where(here, 1.0, mask_rows)

            def pick(first):
                total = None
                for kb in range(4):
                    part = kv[first + BLOCK * kb : first + BLOCK * kb + BLOCK, wide] * mask_rows[kb : kb + 1, at].astype(BF)
                    total = part if total is None else total + part
                return total

            keys, values = pick(0), pick(WINDOW)
            ks_v[slot, :, at] = keys
            vs_v[slot, :, at] = values
            for side in range(2):
                mask = left if side == 0 else jnp.logical_not(left)
                mask_keys = left_keys if side == 0 else jnp.logical_not(left_keys)
                scores = dot_nt(jnp.where(mask, q, jnp.zeros_like(q)), keys)
                heads.append((scores, jnp.where(mask_keys, values, jnp.ones_like(values))))
        raised = []
        for n, (scores, _) in enumerate(heads):
            top = jnp.max(scores, axis=-1, keepdims=True)
            raised.append(jnp.exp2((scores - top) * EXP2_SCALE).astype(BF))
            p_v[slot, n] = raised[n]
        found = [dot_nn(raised[n], heads[n][1]) for n in range(4)]
        for two in range(2):
            wide = pl.ds(pl.multiple_of(g * 256 + 128 * two, 128), 128)
            result = jnp.where(left, found[2 * two], found[2 * two + 1])
            total = jnp.where(left, found[2 * two + 1], found[2 * two])
            inverse = 1.0 / pltpu.roll(total, 64, 1)
            att[rows, wide] = (result * inverse).astype(BF)
            inv[rows, wide] = inverse
        masks_o[t, :, pl.ds(pl.multiple_of(g * 256, 256), 256)] = mask_rows
        for c in stream(i, slot):
            c.start()

    for i in (7, 8):
        for c in stream(i, i % 2):
            c.wait()
    save_att = local(20, att, att_h)
    save_att.start()
    save_inv = local(31, inv, inv_h)
    save_inv.start()
    for c in loads:
        c.wait()

    def row(ref):
        return ref[...].reshape(1, -1)

    def slope(j, t):
        return pl.ds(pl.multiple_of(768 * j + t * TILE, TILE), TILE)

    def tile_saves(t):
        at = pl.ds(pl.multiple_of(t * TILE, TILE), TILE)
        parts = [(low, low_h), (rdel, rdel_h), (scaled_v, scaled_h), (out_v, out_h), (inverse_v, inverse_h)]
        parts = [(src.at[at], dst.at[at]) for src, dst in parts]
        parts.append((act.at[:, at], act_h.at[:, at]))
        parts += [(kv.at[slope(j, t)], slope_h.at[j, at]) for j in range(4)]
        return [local(21 + n, src, dst) for n, (src, dst) in enumerate(parts)]

    @pl.loop(0, 3)
    def _(t):
        at = pl.ds(pl.multiple_of(t * TILE, TILE), TILE)
        x = x_v[pl.ds(pl.multiple_of(own + t * TILE, TILE), TILE), :]
        mixed = dot_nn(att[at, :], mw[...]) + row(mb) + x.astype(F32)
        scaled_one, inverse_one = norm_parts(mixed)
        normed = scaled_one * row(g1) + row(s1)
        normed_low = normed.astype(BF)
        low[at, :] = normed_low
        scaled_v[at, :] = scaled_one.astype(BF)
        inverse_v[at, :] = jnp.broadcast_to(inverse_one, (TILE, 128))
        branch = row(rb) + normed
        for j in range(4):
            cols = slice(768 * j, 768 * j + 768)
            hidden = dot_nn(normed_low, ew[:, cols]) + row(eb)[:, cols]
            phi_sum, bell = normal_parts(hidden)
            active = (hidden * phi_sum).astype(BF)
            act[j, at, :] = active
            kv[slope(j, t), :] = (phi_sum + hidden * bell).astype(BF)
            branch += dot_nn(active, rw[cols, :])
        scaled_two, inverse_two = norm_parts(branch)
        out_v[at, :] = (scaled_two * row(g2) + row(s2)).astype(BF)
        upstream = cot[at, :].astype(F32)
        sums_o[4:5, :] += column_sum(upstream * scaled_two)
        sums_o[5:6, :] += column_sum(upstream)
        branch_delta = norm_back(upstream * row(g2), scaled_two, inverse_two)
        reduce_delta = branch_delta.astype(BF)
        rdel[at, :] = reduce_delta
        sums_o[3:4, :] += column_sum(reduce_delta.astype(F32))

        @pl.when(t > 0)
        def _():
            for c in tile_saves(t - 1):
                c.wait()

        for c in tile_saves(t):
            c.start()

    for c in tile_saves(2):
        c.wait()
    for c in (save_w, save_q, save_x, save_att, save_inv):
        c.wait()


def begin(*args):
    hb = pl.BlockSpec(memory_space=pl.ANY)
    vm = pl.BlockSpec(memory_space=pltpu.VMEM)
    sm = pl.BlockSpec(memory_space=pltpu.SMEM)
    qb, pairs, triples = args[4], args[6], args[7]
    rows = jax.ShapeDtypeStruct((ROWS, D), BF)
    rows_wide = jax.ShapeDtypeStruct((ROWS, D), F32)
    wide = jax.ShapeDtypeStruct((4, ROWS, D), BF)
    picked = jax.ShapeDtypeStruct((9, BLOCK, 256), BF)
    return pl.pallas_call(
        begin_kernel,
        out_shape=(
            jax.ShapeDtypeStruct((WINDOW, D), BF),
            jax.ShapeDtypeStruct((4, 3, SLOT, D), BF),
            jax.ShapeDtypeStruct((4,) + qb.shape, F32),
            jax.ShapeDtypeStruct((4,) + qb.shape, F32),
            jax.ShapeDtypeStruct((4,) + pairs.shape, jnp.int32),
            jax.ShapeDtypeStruct((4,) + triples.shape, jnp.int32),
            jax.ShapeDtypeStruct((9, 4, TILE, BLOCK), BF),
            picked,
            picked,
            jax.ShapeDtypeStruct((3, ROWS, 256), BF),
            rows,
            rows,
            rows,
            rows,
            rows,
            rows_wide,
            jax.ShapeDtypeStruct((ROWS, 128), F32),
            wide,
            wide,
            jax.ShapeDtypeStruct((3, 8, D), F32),
            jax.ShapeDtypeStruct((16, D), F32),
        ),
        in_specs=[hb] * 8 + [sm] + [hb] * 4 + [vm] * 7,
        out_specs=(hb,) * 19 + (vm, vm),
        scratch_shapes=[
            pltpu.VMEM((WINDOW, D), BF),
            pltpu.VMEM((4, 3, SLOT, D), BF),
            pltpu.VMEM((4,) + qb.shape, F32),
            pltpu.VMEM((4,) + qb.shape, F32),
            pltpu.SMEM((4,) + pairs.shape, jnp.int32),
            pltpu.SMEM((4,) + triples.shape, jnp.int32),
            pltpu.VMEM((2 * WINDOW, D), BF),
            pltpu.VMEM((3, ROWS, 256), BF),
            pltpu.VMEM((2, 4, TILE, BLOCK), BF),
            pltpu.VMEM((2, BLOCK, 256), BF),
            pltpu.VMEM((2, BLOCK, 256), BF),
            pltpu.VMEM((ROWS, D), BF),
            pltpu.VMEM((ROWS, D), F32),
            pltpu.VMEM((ROWS, D), BF),
            pltpu.VMEM((D, D), BF),
            pltpu.VMEM((D, FF), BF),
            pltpu.VMEM((FF, D), BF),
            pltpu.VMEM((4, ROWS, D), BF),
            pltpu.VMEM((ROWS, D), BF),
            pltpu.VMEM((ROWS, D), BF),
            pltpu.VMEM((ROWS, D), BF),
            pltpu.VMEM((ROWS, D), BF),
            pltpu.VMEM((ROWS, 128), F32),
            pltpu.SemaphoreType.DMA((32,)),
            pltpu.SemaphoreType.DMA((3, 2)),
            pltpu.SemaphoreType.DMA((61,)),
            pltpu.SemaphoreType.DMA((61,)),
        ],
        compiler_params=pltpu.CompilerParams(
            collective_id=0, has_side_effects=True, vmem_limit_bytes=63 * 2**20
        ),
        name="begin",
    )(*args)


def finish_kernel(
    nb, act_h, slope_h, low_h, rdel_h, att_h, scaled_h, p_h, ks_h, vs_h, q_h, inv_h, xw_h, wt_h, mw_h, ew_h, rw_h,
    inverse_one, g1, masks, sums_in,
    res_h, tg_o, sums_o, from_more,
    stage, from_core, from_a, from_b, from_z, res, dx_pair, dx_mid, vec, vec_in,
    wide_a, wide_b, four, pool, own, p_v, ks_v, vs_v, q_v, i_v, loc, flow, send, recv,
):
    b = lax.axis_index("batch")
    h = lax.axis_index("head")
    core, xb, yb = b % 2, (b // 2) % 2, (b // 4) % 2
    pc, px, py = flip(b, 1), flip(b, 2), flip(b, 4)
    hp, hm, hq = flip(h, 1), 3 - h, flip(h, 2)
    middle = jnp.logical_or(h == 1, h == 2)
    others = [(h + d) % 4 for d in (1, 2, 3)]
    more = []
    step = 8
    while step < nb:
        more.append(flip(b, step))
        step *= 2
    barrier = pltpu.get_barrier_semaphore()
    targets = [(pc, h), (px, h), (py, h)] + [(m, h) for m in more] + [(b, o) for o in others]
    for target in targets:
        pl.semaphore_signal(barrier, inc=1, device_id=target, device_id_type=MESH)

    def local(i, src, dst):
        return pltpu.make_async_copy(src, dst, loc.at[i])

    loads = [
        local(0, act_h.at[:, :, pl.ds(0, 384)], wide_a.at[:, :, pl.ds(0, 384)]),
        local(1, rdel_h, four.at[1]),
        local(2, low_h, four.at[0]),
        local(3, slope_h, wide_b),
        local(4, att_h, four.at[2]),
        local(5, scaled_h, four.at[3]),
        local(6, mw_h, pool.at[4]),
        local(7, act_h.at[:, :, pl.ds(384, 384)], wide_a.at[:, :, pl.ds(384, 384)]),
    ]
    for c in loads[:2]:
        c.start()

    def get_weights(j):
        cols = pl.ds(768 * j, 768)
        return [
            local(16 + j, rw_h.at[cols], pool.at[j % 2]),
            local(20 + j, ew_h.at[:, cols], pool.at[2 + j % 2]),
        ]

    def make(i, src, dst, who, where):
        return remote(src, dst, send.at[i], recv.at[i], who, where)

    bits = ((xb, px, yb, py), (yb, py, xb, px))
    columns = (pl.ds(0, 384), pl.ds(384, 384))

    def rows_of(start, count):
        return pl.ds(pl.multiple_of(start, 16), count)

    def size(n, level):
        return (PIECES[n][2] // 8, PIECES[n][2] // 4, PIECES[n][2] // 2)[level]

    def place_start(n, part, level):
        start = PIECES[n][1] + core * size(n, 2)
        if level < 2:
            start = start + bits[part][0] * size(n, 1)
        if level < 1:
            start = start + bits[part][2] * size(n, 0)
        return start

    def place(n, part, level):
        return rows_of(place_start(n, part, level), size(n, level))

    def landing(n, level):
        return slice(PIECES[n][1] * size(n, level) // PIECES[n][2], (PIECES[n][1] + PIECES[n][2]) * size(n, level) // PIECES[n][2])

    def land(ref, n, level, cols):
        rows = landing(n, level)
        return ref.at[PIECES[n][0], :, pl.ds(rows.start, rows.stop - rows.start), cols]

    def core_copy(n):
        k, first, _ = PIECES[n]
        src = stage.at[k % 4, :, rows_of(first + (1 - core) * size(n, 2), size(n, 2))]
        return make(n, src, land(from_core, n, 2, slice(None)), pc, h)

    def a_copy(n, part):
        k, first, _ = PIECES[n]
        a_bit, who = bits[part][:2]
        rows = rows_of(first + core * size(n, 2) + (1 - a_bit) * size(n, 1), size(n, 1))
        return make(7 + 2 * n + part, stage.at[k % 4, :, rows, columns[part]], land(from_a, n, 1, columns[part]), who, h)

    def b_copy(n, part):
        k = PIECES[n][0]
        _, _, b_bit, who = bits[part]
        rows = rows_of(place_start(n, part, 1) + (1 - b_bit) * size(n, 0), size(n, 0))
        return make(21 + 2 * n + part, stage.at[k % 4, :, rows, columns[part]], land(from_b, n, 0, columns[part]), who, h)

    def z_copy(n, part, d):
        o = others[d - 1]
        k = PIECES[n][0]
        rows = landing(n, 0)
        dst = from_z.at[k, d - 1, pl.ds(rows.start, rows.stop - rows.start), columns[part]]
        return make(35 + 6 * n + 3 * part + d - 1, stage.at[k % 4, o, place(n, part, 0), columns[part]], dst, b, o)

    def gather_copy(n, part, level):
        ref = res.at[PIECES[n][0], place(n, part, level), columns[part]]
        return make(77 + 14 * level + 2 * n + part, ref, ref, bits[part][3 if level == 0 else 1], h)

    def last_copy(n):
        ref = res.at[PIECES[n][0], place(n, 0, 2)]
        return make(105 + n, ref, ref, pc, h)

    def more_copy(n, part, i):
        src = stage.at[PIECES[n][0] % 4, :, place(n, part, 0), columns[part]]
        dst = from_more.at[n, i, :, pl.ds(0, size(n, 0)), columns[part]]
        return make(122 + len(more) * (2 * n + part + 1) + i, src, dst, more[i], h)

    def out_copy(k):
        return local(8 + k, res.at[k], res_h.at[k])

    def add(n, part, level, other):
        k, block = PIECES[n][0] % 4, size(n, 0)
        start, first = place_start(n, part, level), landing(n, level).start
        cols = slice(0, D) if level == 2 else slice(384 * part, 384 * part + 384)

        @pl.loop(0, size(n, level) // block * 4)
        def _(i):
            z, at = i % 4, i // 4 * block
            mine = rows_of(start + at, block)
            stage[k, z, mine, cols] = stage[k, z, mine, cols] + other[PIECES[n][0], z, rows_of(first + at, block), cols]

    def stage_core(n):
        core_copy(n).wait()
        add(n, 0, 2, from_core)
        for part in range(2):
            a_copy(n, part).start()

    def stage_a(n):
        for part in range(2):
            a_copy(n, part).wait()
            add(n, part, 1, from_a)
            b_copy(n, part).start()

    def stage_b(n):
        for part in range(2):
            b_copy(n, part).wait()
            add(n, part, 0, from_b)
            for i in range(len(more)):
                more_copy(n, part, i).start()
                more_copy(n, part, i).wait()
                get = local(35, from_more.at[n, i, :, pl.ds(0, size(n, 0))], land(from_b, n, 0, slice(None)))
                get.start()
                get.wait()
                add(n, part, 0, from_b)
            for d in (2, 1, 3):
                z_copy(n, part, d).start()

    def stage_z(n):
        k, rows = PIECES[n][0], landing(n, 0)
        for part in range(2):
            cols = slice(384 * part, 384 * part + 384)
            total = stage[k % 4, h, place(n, part, 0), cols].astype(F32)
            for d in (1, 2, 3):
                z_copy(n, part, d).wait()
                total += from_z[k, d - 1, rows, cols].astype(F32)
            res[k, place(n, part, 0), cols] = total.astype(BF)
            gather_copy(n, part, 0).start()

    def stage_y(n):
        for part in range(2):
            gather_copy(n, part, 0).wait()
            gather_copy(n, part, 1).start()

    def stage_x(n):
        for part in range(2):
            gather_copy(n, part, 1).wait()
        last_copy(n).start()

    landed = []

    def stage_out(n):
        last_copy(n).wait()
        landed.append(n)
        k = PIECES[n][0]
        if all(m in landed for m in range(len(PIECES)) if PIECES[m][0] == k):
            out_copy(k).start()

    vec_steps = [(pc, h), (px, h), (py, h)] + [(m, h) for m in more] + [(b, hp), (b, hq)]

    def vec_copy(i):
        return make(117 + i, vec, vec_in.at[i], *vec_steps[i])

    def stage_vec(i):
        vec_copy(i).wait()
        vec[...] += vec_in[i]
        if i + 1 < len(vec_steps):
            vec_copy(i + 1).start()

    stages = {
        "c": stage_core, "a": stage_a, "b": stage_b, "z": stage_z, "y": stage_y, "x": stage_x, "o": stage_out,
        "v": stage_vec,
    }

    def run(*items):
        for kind, k in items:
            stages[kind](k)

    def reduce_chunk(k, half):
        for z in range(4):
            grad = dot_tn(wide_a[z, :, 384 * half : 384 * half + 384], four[1])
            stage[k, z] = grad.astype(BF)

    def weight_grad(k, start, product):
        for half in range(2):
            grad = product(slice(384 * half, 384 * half + 384)).astype(BF)
            for z in range(2):
                stage[k, 2 * half + z, start : start + SLOT, :] = grad[SLOT * z : SLOT * z + SLOT, :]

    def to_keys(source, target):
        @pl.loop(0, 32)
        def _(i):
            rows = pl.ds(pl.multiple_of(i * 16, 16), 16)
            parts = [source[t, rows, :].astype(F32) for t in range(3)]
            for kb in range(4):
                total = parts[0] * masks[0, kb : kb + 1, :]
                for t in (1, 2):
                    total += parts[t] * masks[t, kb : kb + 1, :]
                target[kb, rows, :] = total.astype(BF)

    def fetch(i, slot):
        g, t = i // 3, i % 3
        tile = (pl.ds(pl.multiple_of(t * TILE, TILE), TILE), pl.ds(pl.multiple_of(g * 256, 256), 256))
        pairs = (
            (p_h.at[i], p_v), (ks_h.at[i], ks_v), (vs_h.at[i], vs_v), (q_h.at[g, tile[0]], q_v), (inv_h.at[tile], i_v),
        )
        return [pltpu.make_async_copy(src, dst.at[slot], flow.at[n, slot]) for n, (src, dst) in enumerate(pairs)]

    ready = []

    def need(name, copies):
        if name not in ready:
            ready.append(name)
            for c in copies:
                c.wait()

    def reduce_part(half):
        if half == 1:
            loads[7].wait()
        reduce_chunk(half, half)
        if half == 0:
            pl.semaphore_wait(barrier, len(targets))

    def expand_part(j):
        need("low", loads[2:4])
        for c in get_weights(j):
            c.wait()
        for t in range(3):
            rows = slice(TILE * t, TILE * t + TILE)
            back = dot_nt(four[1, rows, :], pool[j % 2]) * wide_b[j, rows, :].astype(F32)
            back = back.astype(BF)
            wide_b[j, rows, :] = back
            vec[6 + j : 7 + j, :] += column_sum(back.astype(F32))
            before = four[1, rows, :].astype(F32) if j == 0 else own[rows, :]
            own[rows, :] = before + dot_nt(back, pool[2 + j % 2])
        if j < 2:
            for c in get_weights(j + 2):
                c.start()
        for half in range(2):
            grad = dot_tn(four[0, :, 384 * half : 384 * half + 384], wide_b[j])
            stage[2 + half, j] = grad.astype(BF)

    def norm_part(_):
        need("mixer", loads[4:7])
        for t in range(3):
            rows = slice(TILE * t, TILE * t + TILE)
            normed_delta = own[rows, :]
            scaled = four[3, rows, :].astype(F32)
            vec[1:2, :] += column_sum(normed_delta * scaled)
            vec[2:3, :] += column_sum(normed_delta)
            mixed_delta = norm_back(normed_delta * g1[...].reshape(1, D), scaled, inverse_one[rows, 0:1])
            own[rows, :] = mixed_delta
            mixer_delta = mixed_delta.astype(BF)
            four[3, rows, :] = mixer_delta
            vec[0:1, :] += column_sum(mixer_delta.astype(F32))
            four[0, rows, :] = dot_nt(mixer_delta, pool[4]).astype(BF)

    own_at = own_offset(h)
    pair_at = own_offset(hp)
    mid_at = pl.multiple_of(1536 * (h % 2), 256)
    get_x = [local(16 + kb, xw_h.at[pl.ds(BLOCK * kb, BLOCK)], wide_b.at[kb, pl.ds(0, BLOCK)]) for kb in range(4)]
    own_x = [
        local(
            32 + c,
            xw_h.at[pl.ds(pl.multiple_of(own_at + TILE * c, TILE), TILE)],
            wide_b.at[c, pl.ds(BLOCK, TILE)],
        )
        for c in range(3)
    ]
    get_w = [
        local(20 + 4 * m + s, wt_h.at[s, m], wide_a.at[m, pl.ds(SLOT * s, SLOT)]) for m in range(3) for s in range(4)
    ]

    def value_keys(_):
        to_keys(wide_b, pool)
        for c in get_x + own_x:
            c.start()

    def key_keys(_):
        to_keys(wide_a, four)
        for c in get_w:
            c.start()

    def x_rows():
        need("rows", get_x)
        return wide_b[:, 0:BLOCK, :].reshape(WINDOW, D)

    def mixer_grad(_):
        weight_grad(0, 0, lambda at: dot_tn(four[2, :, at], four[3]))

    def value_grad(_):
        weight_grad(0, SLOT, lambda at: dot_tn(pool[0:4, 0:BLOCK, at].reshape(WINDOW, 384), x_rows()))

    def key_grad(_):
        weight_grad(1, 0, lambda at: dot_tn(four[:, 0:BLOCK, at].reshape(WINDOW, 384), x_rows()))

    def query_grad(_):
        need("own rows", own_x)
        weight_grad(1, SLOT, lambda at: dot_tn(wide_a[3, :, at], wide_b[0:3, BLOCK:, :].reshape(ROWS, D)))

    def bias_sums(_):
        vec[10:11, :] = column_sum(wide_a[3].astype(F32))
        total = column_sum(pool[0, 0:BLOCK, :].astype(F32))
        for kb in range(1, 4):
            total += column_sum(pool[kb, 0:BLOCK, :].astype(F32))
        vec[11:12, :] = total

    def row_part(start):
        need("weights", get_w)
        kb, rows = start // BLOCK, pl.ds(pl.multiple_of(start % BLOCK, TILE), TILE)
        return dot_nn(four[kb, rows, :], wide_a[1]) + dot_nn(pool[kb, rows, :], wide_a[2])

    spare = pl.ds(BLOCK, TILE)

    def pair_copy(c):
        return make(112 + c, pool.at[c, spare], dx_pair.at[pl.ds(TILE * c, TILE)], b, hp)

    def mid_copy(c):
        return make(115 + c, pool.at[3 + c, spare], dx_mid.at[pl.ds(TILE * c, TILE)], b, hm)

    def pair_part(c):
        pool[c, BLOCK:, :] = row_part(pair_at + TILE * c).astype(BF)

    def mid_part(c):
        need("weights", get_w)

        @pl.when(middle)
        def _():
            pool[3 + c, BLOCK:, :] = row_part(mid_at + TILE * c).astype(BF)

    def mid_start(c):
        @pl.when(middle)
        def _():
            mid_copy(c).start()

    def own_part(c):
        rows = slice(TILE * c, TILE * c + TILE)
        own[rows, :] += row_part(own_at + TILE * c) + dot_nn(wide_a[3, rows, :], wide_a[0])

    def pair_add(c):
        pair_copy(c).wait()
        rows = slice(TILE * c, TILE * c + TILE)
        own[rows, :] += dx_pair[rows, :].astype(F32)

    def mid_add(c):
        @pl.when(middle)
        def _():
            mid_copy(c).wait()
            rows = pl.ds(pl.multiple_of(256 * (h % 2) + TILE * c, TILE), TILE)
            own[rows, :] += dx_mid[TILE * c : TILE * c + TILE, :].astype(F32)

    def final_part(_):
        for i in range(5, len(vec_steps)):
            stage_vec(i)
        sums_o[...] = vec[...]
        tg_o[...] = own[...].astype(BF)

    def drain(_):
        for k in range(CHUNKS):
            out_copy(k).wait()

    stages.update(
        {
            "R": reduce_part, "J": expand_part, "LN": norm_part, "kv": value_keys, "kk": key_keys, "M": mixer_grad,
            "V": value_grad, "K": key_grad, "Q": query_grad, "sums": bias_sums, "pp": pair_part, "mm": mid_part,
            "ow": own_part, "dp": pair_add, "dm": mid_add, "fin": final_part, "end": drain,
            "core": lambda n: core_copy(n).start(), "P": lambda c: pair_copy(c).start(), "Mx": mid_start,
            "v0": lambda _: vec_copy(0).start(),
        }
    )

    loads[0].wait()
    loads[1].wait()
    for c in loads[7:] + get_weights(0) + loads[2:4] + get_weights(1) + loads[4:7] + fetch(0, 0):
        c.start()
    vec[...] = sums_in[...]
    run(*BEFORE)

    left = left_lanes(TILE)
    @pl.loop(0, 9)
    def _(i):
        slot = i % 2
        g, t = i // 3, i % 3
        lanes = pl.multiple_of(g * 256, 256)

        @pl.when(i < 8)
        def _():
            for c in fetch(i + 1, 1 - slot):
                c.start()

        for c in fetch(i, slot):
            c.wait()
        heads = []
        for pair in range(2):
            at = slice(128 * pair, 128 * pair + 128)
            q = q_v[slot, :, at]
            tile = (0, pl.ds(pl.multiple_of(t * TILE, TILE), TILE), pl.ds(pl.multiple_of(lanes + 128 * pair, 128), 128))
            delta = (four[tile].astype(F32) * i_v[slot, :, at]).astype(BF)
            prod = delta.astype(F32) * four[(2,) + tile[1:]].astype(F32)
            for side in range(2):
                mask = left if side == 0 else jnp.logical_not(left)
                inner = jnp.sum(jnp.where(mask, prod, 0.0), axis=-1, keepdims=True)
                delta_side = jnp.where(mask, delta, jnp.zeros_like(delta))
                q_side = jnp.where(mask, q, jnp.zeros_like(q))
                heads.append((inner, delta_side, q_side, dot_nt(delta_side, vs_v[slot, :, at])))
        dv = [dot_tn(p_v[slot, n], heads[n][1]) for n in range(4)]
        ds = [(p_v[slot, n].astype(F32) * (heads[n][3] - heads[n][0])).astype(BF) for n in range(4)]
        for pair in range(2):
            at = slice(128 * pair, 128 * pair + 128)
            two = (2 * pair, 2 * pair + 1)
            dk = [dot_tn(ds[n], heads[n][2]) for n in two]
            dq = [dot_nn(ds[n], ks_v[slot, :, at]) for n in two]
            where = pl.ds(pl.multiple_of(lanes + 128 * pair, 128), 128)
            wide_a[t, 0:BLOCK, where] = ((dk[0] + dk[1]) * SCALE).astype(BF)
            wide_b[t, 0:BLOCK, where] = (dv[2 * pair] + dv[2 * pair + 1]).astype(BF)
            wide_a[3, pl.ds(pl.multiple_of(t * TILE, TILE), TILE), where] = (
                jnp.where(left, dq[0], dq[1]) * SCALE
            ).astype(BF)
        for n, items in DURING.items():

            @pl.when(i == n)
            def _():
                run(*items)

    run(*AFTER)


def finish(nb, *args):
    hb = pl.BlockSpec(memory_space=pl.ANY)
    vm = pl.BlockSpec(memory_space=pltpu.VMEM)
    extra = max(0, nb.bit_length() - 4)
    count = 122 + extra * (2 * len(PIECES) + 1)
    return pl.pallas_call(
        functools.partial(finish_kernel, nb),
        out_shape=(
            jax.ShapeDtypeStruct((CHUNKS, 384, D), BF),
            jax.ShapeDtypeStruct((ROWS, D), BF),
            jax.ShapeDtypeStruct((16, D), F32),
            jax.ShapeDtypeStruct((len(PIECES), extra, 4, 48, D) if extra else (1, 1, 1, 16, 128), BF),
        ),
        in_specs=[hb] * 16 + [vm] * 4,
        out_specs=(hb, vm, vm, hb),
        scratch_shapes=[
            pltpu.VMEM((4, 4, 384, D), BF),
            pltpu.VMEM((CHUNKS, 4, 192, D), BF),
            pltpu.VMEM((CHUNKS, 4, 96, D), BF),
            pltpu.VMEM((CHUNKS, 4, 48, D), BF),
            pltpu.VMEM((CHUNKS, 3, 48, D), BF),
            pltpu.VMEM((CHUNKS, 384, D), BF),
            pltpu.VMEM((ROWS, D), BF),
            pltpu.VMEM((BLOCK, D), BF),
            pltpu.VMEM((16, D), F32),
            pltpu.VMEM((5 + extra, 16, D), F32),
            pltpu.VMEM((4, ROWS, D), BF),
            pltpu.VMEM((4, ROWS, D), BF),
            pltpu.VMEM((4, ROWS, D), BF),
            pltpu.VMEM((5, ROWS, D), BF),
            pltpu.VMEM((ROWS, D), F32),
            pltpu.VMEM((2, 4, TILE, BLOCK), BF),
            pltpu.VMEM((2, BLOCK, 256), BF),
            pltpu.VMEM((2, BLOCK, 256), BF),
            pltpu.VMEM((2, TILE, 256), BF),
            pltpu.VMEM((2, TILE, 256), F32),
            pltpu.SemaphoreType.DMA((36,)),
            pltpu.SemaphoreType.DMA((5, 2)),
            pltpu.SemaphoreType.DMA((count,)),
            pltpu.SemaphoreType.DMA((count,)),
        ],
        compiler_params=pltpu.CompilerParams(
            collective_id=1, has_side_effects=True, vmem_limit_bytes=63 * 2**20
        ),
        name="finish",
    )(*args)


def unpack_kernel(
    res, sums, reduce_h, expand_h, mixer_h, value_h, key_h, query_h, qbias_o, vbias_o, hidden_o, *rest
):
    vec_o, (low, full, sems) = rest[:6], rest[6:]
    h = lax.axis_index("head")
    gets = [pltpu.make_async_copy(res.at[k], low.at[k], sems.at[k]) for k in range(CHUNKS)]
    for c in gets:
        c.start()
    for n, ref in enumerate(vec_o):
        ref[...] = sums[n : n + 1, :].reshape(D)
    for j in range(4):
        hidden_o[D * j : D * j + D] = sums[6 + j : 7 + j, :].reshape(D)
    for n, ref in ((10, qbias_o), (11, vbias_o)):
        mine = sums[n : n + 1, 0:SLOT]
        for z in range(1, 4):
            mine = jnp.where(h == z, sums[n : n + 1, SLOT * z : SLOT * z + SLOT], mine)
        ref[...] = mine.reshape(SLOT)
    upper, lower = pl.ds(0, SLOT), pl.ds(SLOT, SLOT)
    targets = (
        (reduce_h.at[pl.ds(0, 384)],),
        (reduce_h.at[pl.ds(384, 384)],),
        (expand_h.at[pl.ds(0, 384)],),
        (expand_h.at[pl.ds(384, 384)],),
        (mixer_h, value_h),
        (key_h, query_h),
    )
    puts = []
    for k in range(CHUNKS):
        gets[k].wait()

        @pl.loop(0, 12, unroll=4)
        def _(i):
            rows = pl.ds(pl.multiple_of(i * 32, 32), 32)
            full[k, rows, :] = low[k, rows, :].astype(F32)

        views = (full.at[k],) if k < 4 else (full.at[k, upper], full.at[k, lower])
        for view, target in zip(views, targets[k]):
            c = pltpu.make_async_copy(view, target, sems.at[CHUNKS + len(puts)])
            c.start()
            puts.append(c)
    for c in puts:
        c.wait()


def unpack(res, sums):
    vm = pl.BlockSpec(memory_space=pltpu.VMEM)
    hb = pl.BlockSpec(memory_space=pl.ANY)
    square = jax.ShapeDtypeStruct((D, D), F32)
    strip = jax.ShapeDtypeStruct((SLOT, D), F32)
    short = jax.ShapeDtypeStruct((SLOT,), F32)
    row = jax.ShapeDtypeStruct((D,), F32)
    return pl.pallas_call(
        unpack_kernel,
        out_shape=(square, square, strip, strip, strip, strip, short, short, jax.ShapeDtypeStruct((FF,), F32)) + (row,) * 6,
        in_specs=[hb, vm],
        out_specs=(hb,) * 6 + (vm,) * 9,
        scratch_shapes=[
            pltpu.VMEM((CHUNKS, 384, D), BF),
            pltpu.VMEM((CHUNKS, 384, D), F32),
            pltpu.SemaphoreType.DMA((14,)),
        ],
        compiler_params=pltpu.CompilerParams(vmem_limit_bytes=VMEM_LIMIT),
        name="unpack",
    )(res, sums)


def layer(
    nb, tokens, query_weight, key_weight, value_weight, query_bias, value_bias, mixer_weight, mixer_bias,
    first_gain, first_shift, expand_weight, expand_bias, reduce_weight, reduce_bias, second_gain,
    second_shift, cotangent, group_kinds, pair_orders, triple_orders,
):
    (
        xw, wt, _, _, _, _, probs, keys, values, q, att, low, rdel, scaled, layer_output, inv, inverse, act, slope,
        masks, sums,
    ) = begin(
        tokens,
        query_weight.T,
        key_weight.T,
        value_weight.T,
        query_bias.reshape(1, -1),
        value_bias.reshape(1, -1),
        pair_orders.transpose(0, 2, 1),
        triple_orders.transpose(1, 0, 2),
        group_kinds,
        cotangent,
        mixer_weight,
        expand_weight,
        reduce_weight,
        mixer_bias,
        first_gain,
        first_shift,
        reduce_bias,
        second_gain,
        second_shift,
        expand_bias,
    )
    res, tokens_grad, sums, _ = finish(
        nb, act, slope, low, rdel, att, scaled, probs, keys, values, q, inv, xw, wt, mixer_weight, expand_weight,
        reduce_weight, inverse, first_gain, masks, sums,
    )
    out = unpack(res, sums)
    reduce_grad, expand_grad, mixer_grad, value_grad, key_grad, query_grad, query_sum, value_sum, hidden_sum = out[:9]
    mixer_sum, gain_one, shift_one, reduce_sum, gain_two, shift_two = out[9:]
    return (
        layer_output,
        tokens_grad,
        query_grad.T,
        key_grad.T,
        value_grad.T,
        query_sum,
        value_sum,
        mixer_grad,
        mixer_sum,
        gain_one,
        shift_one,
        expand_grad,
        hidden_sum,
        reduce_grad,
        reduce_sum,
        gain_two,
        shift_two,
    )


def solution(mesh):
    rows = P(("batch", "head"), None)
    return jax.shard_map(
        functools.partial(layer, mesh.shape["batch"]),
        mesh=mesh,
        in_specs=(
            rows,
            P(None, "head"),
            P(None, "head"),
            P(None, "head"),
            P("head"),
            P("head"),
            P(),
            P(),
            P(),
            P(),
            P(),
            P(),
            P(),
            P(),
            P(),
            P(),
            rows,
            P("batch"),
            P("batch", "head", None),
            P("batch", "head", None),
        ),
        out_specs=(
            rows,
            rows,
            P(None, "head"),
            P(None, "head"),
            P(None, "head"),
            P("head"),
            P("head"),
            P("head", None),
            P(),
            P(),
            P(),
            P(None, "head"),
            P(),
            P("head", None),
            P(),
            P(),
            P(),
        ),
        check_vma=False,
    )
```
